32 devices in a mesh: dp: 4 (over y, x), fsdp: 8 (over z, core).
Axes of the slice: x: 2, y: 2, z: 4, core: 2. Of those that a mesh axis runs over, the one named last changes fastest.
Arguments:
- tokens: bfloat16 [8, 1280, 1536], P('fsdp', 'dp'), may hold values from -6 to 6
- cotangent: bfloat16 [8, 1280, 1536], P('fsdp', 'dp'), may hold values from -12 to 12
- lengths: int32 [8], P('fsdp'), may hold values from 320 to 1280, as said below
- qkv_weight: float32 [1536, 2048], P('dp', 'fsdp'), may hold values from -0.109375 to 0.109375
- qkv_first: float32 [1536, 2048], P('dp', 'fsdp'), may hold values from -0.001953125 to 0.001953125
- qkv_second: float32 [1536, 2048], P('dp', 'fsdp'), may hold values from 1.0684257e-08 to 1.7094811e-07
- out_weight: float32 [1536, 1536], P('dp', 'fsdp'), may hold values from -0.66340347 to 0.66340347
- out_first: float32 [1536, 1536], P('dp', 'fsdp'), may hold values from -0.001953125 to 0.001953125
- out_second: float32 [1536, 1536], P('dp', 'fsdp'), may hold values from 1.0684257e-08 to 1.7094811e-07
- mlp_in_weight: float32 [1536, 17920], P('dp', 'fsdp'), may hold values from -0.15625 to 0.15625
- mlp_in_first: float32 [1536, 17920], P('dp', 'fsdp'), may hold values from -0.001953125 to 0.001953125
- mlp_in_second: float32 [1536, 17920], P('dp', 'fsdp'), may hold values from 1.0684257e-08 to 1.7094811e-07
- down_weight: float32 [8960, 1536], P('dp', 'fsdp'), may hold values from -0.091910525 to 0.091910525
- down_first: float32 [8960, 1536], P('dp', 'fsdp'), may hold values from -0.001953125 to 0.001953125
- down_second: float32 [8960, 1536], P('dp', 'fsdp'), may hold values from 1.0684257e-08 to 1.7094811e-07
- small_params: float32 [8, 640], P('dp', 'fsdp'), may hold values from -2 to 3.5, as said below
- small_first: float32 [8, 640], P('dp', 'fsdp'), may hold values from -0.001953125 to 0.001953125
- small_second: float32 [8, 640], P('dp', 'fsdp'), may hold values from 1.0684257e-08 to 1.7094811e-07
Outputs:
- mixed: bfloat16 [8, 1280, 1536], P('fsdp', 'dp')
- input_grad: bfloat16 [8, 1280, 1536], P('fsdp', 'dp')
- grad_norm: float32 [], replicated
- qkv_new: float32 [1536, 2048], P('dp', 'fsdp')
- qkv_first_new: float32 [1536, 2048], P('dp', 'fsdp')
- qkv_second_new: float32 [1536, 2048], P('dp', 'fsdp')
- qkv_copy: bfloat16 [1536, 2048], P('dp', 'fsdp')
- out_new: float32 [1536, 1536], P('dp', 'fsdp')
- out_first_new: float32 [1536, 1536], P('dp', 'fsdp')
- out_second_new: float32 [1536, 1536], P('dp', 'fsdp')
- out_copy: bfloat16 [1536, 1536], P('dp', 'fsdp')
- mlp_in_new: float32 [1536, 17920], P('dp', 'fsdp')
- mlp_in_first_new: float32 [1536, 17920], P('dp', 'fsdp')
- mlp_in_second_new: float32 [1536, 17920], P('dp', 'fsdp')
- mlp_in_copy: bfloat16 [1536, 17920], P('dp', 'fsdp')
- down_new: float32 [8960, 1536], P('dp', 'fsdp')
- down_first_new: float32 [8960, 1536], P('dp', 'fsdp')
- down_second_new: float32 [8960, 1536], P('dp', 'fsdp')
- down_copy: bfloat16 [8960, 1536], P('dp', 'fsdp')
- small_new: float32 [8, 640], P('dp', 'fsdp')
- small_first_new: float32 [8, 640], P('dp', 'fsdp')
- small_second_new: float32 [8, 640], P('dp', 'fsdp')
- small_copy: bfloat16 [8, 640], P('dp', 'fsdp')
The draws below stay inside these ranges and needn't reach their ends.
Inputs may be any that keep to these rules, and one draw needn't show every extreme that they name: `lengths`: each row's valid tokens come first; in every draw at least one row is valid over all 1280 tokens. `small_params`: the two gains are positive, the bias has both signs.
All inputs are finite; a program needn't handle non-finite values.
Results may differ from the reference program's by a relative error of at most 0.035.
Values may be sent and summed in bfloat16 or wider, within the bound.
No kernel may reach another device: no remote copies, remote signals or barrier semaphores. Data moves between devices by JAX's collectives and lax.ppermute only.
A program may use at most 512 MiB of HBM per device.

```python
import math
import jax
import jax.numpy as jnp
from jax import lax

D = 1536
HEADS = 12
KV_HEADS = 2
HEAD = 128
FF = 8960
STEP = 5
SEQ = 1280
SEQS = 8
GROUP = 6
QKV = 2048
SMALL = 5120
PARAMS = 46797824


def rising(count, growth):
    places = jnp.arange(count, dtype=jnp.float32)
    return jnp.exp(jnp.log(growth) * (places / (count - 1) - 0.5))


def rough_normal(key, shape, bound):
    return jnp.clip(jax.random.normal(key, shape, jnp.float32), -bound, bound)


def group_small(gain_attn, gain_mlp, biases):
    count = KV_HEADS * HEAD
    pieces = [gain_attn.reshape(count, GROUP), gain_mlp.reshape(count, GROUP), biases[:D].reshape(count, GROUP), biases[D:D + count][:, None], biases[D + count:][:, None]]
    return jnp.concatenate(pieces, axis=1).reshape(8, SMALL // 8)


def draw_small_params(key, part):
    key = jax.random.fold_in(key, 11)
    gain_key, bias_key = jax.random.split(key)
    growth = 3.0
    biases = 0.5 * rough_normal(bias_key, (QKV,), 4.0)
    gains = rising(D, growth)[None, :] * jax.random.uniform(gain_key, (2, D), jnp.float32, 0.6, 1.4)
    return group_small(gains[0], gains[1], biases)


def draw_out_weight(key, part):
    key = jax.random.fold_in(key, 12)
    growth = 3.0
    noise = rough_normal(key, (D, D), 5.0)
    return noise * rising(D, growth)[:, None] * (3.0 / D ** 0.5)


def draw_down_weight(key, part):
    key = jax.random.fold_in(key, 13)
    growth = 3.0
    noise = rough_normal(key, (FF, D), 5.0)
    return noise * rising(FF, growth)[:, None] * (1.0 / FF ** 0.5)


def draw_cotangent(key, part):
    key = jax.random.fold_in(key, 14)
    growth = 3.0
    noise = rough_normal(key, (SEQS, SEQ, D), 5.0)
    return (noise * rising(D, growth)[None, None, :]).astype(jnp.bfloat16)


def draw_lengths(key, part):
    key = jax.random.fold_in(key, 15)
    length_key, chosen_key = jax.random.split(key)
    drawn = jax.random.randint(length_key, (SEQS,), SEQ // 4, SEQ + 1)
    chosen = jax.random.randint(chosen_key, (), 0, SEQS)
    return jnp.where(jnp.arange(SEQS) == chosen, SEQ, drawn).astype(jnp.int32)


def block_levels(own_key, shape, cuts, smallest, largest):
    def one(dim, shards_of):
        draws = jax.random.uniform(jax.random.fold_in(jax.random.fold_in(own_key, 6), dim), (shards_of,), jnp.float32, smallest / len(cuts), largest / len(cuts))
        return jnp.repeat(jnp.exp(draws), shape[dim] // shards_of).reshape((-1,) + (1,) * (len(shape) - dim - 1))

    loudness = one(*cuts[0])
    for cut in cuts[1:]:
        loudness = loudness * one(*cut)
    return loudness


def centred(stream_key, extent, width, reach, cuts=(), kind=jnp.bfloat16):
    result = width * jax.random.normal(stream_key, extent, jnp.float32)
    if cuts:
        result = result * block_levels(stream_key, extent, cuts, -0.22, 0.18)
    return jnp.clip(result, -reach, reach).astype(kind)


def setup_inputs(seed: int = 0) -> dict:
    keys = jax.random.split(jax.random.key(seed), 19)
    return {
        "tokens": centred(keys[0], (SEQS, SEQ, D), 1.0, 6.0, ((0, 8), (1, 4))),
        "cotangent": draw_cotangent(jax.random.fold_in(keys[18], 71), 0),
        "lengths": draw_lengths(jax.random.fold_in(keys[18], 71), 0),
        "qkv_weight": centred(keys[3], (D, QKV), (2 * D) ** -0.5, 0.109375, ((0, 4), (1, 8)), jnp.float32),
        "qkv_first": centred(keys[4], (D, QKV), ((1.0 * PARAMS) ** -0.5), 0.001953125, ((0, 4), (1, 8)), jnp.float32),
        "qkv_second": jnp.clip(jnp.exp(math.log(1.7094811255446984e-07) - 2.7725887 * jax.random.uniform(keys[5], (D, QKV), jnp.float32) ** block_levels(keys[5], (D, QKV), ((0, 4), (1, 8)), -0.2, 0.2)), 1.0684257034654365e-08, 1.7094811255446984e-07),
        "out_weight": draw_out_weight(jax.random.fold_in(keys[18], 71), 0),
        "out_first": centred(keys[7], (D, D), ((1.0 * PARAMS) ** -0.5), 0.001953125, ((0, 4), (1, 8)), jnp.float32),
        "out_second": jnp.clip(jnp.exp(math.log(1.7094811255446984e-07) - 2.7725887 * jax.random.uniform(keys[8], (D, D), jnp.float32) ** block_levels(keys[8], (D, D), ((0, 4), (1, 8)), -0.2, 0.2)), 1.0684257034654365e-08, 1.7094811255446984e-07),
        "mlp_in_weight": centred(keys[9], (D, 2 * FF), D ** -0.5, 0.15625, ((0, 4), (1, 8)), jnp.float32),
        "mlp_in_first": centred(keys[10], (D, 2 * FF), ((1.0 * PARAMS) ** -0.5), 0.001953125, ((0, 4), (1, 8)), jnp.float32),
        "mlp_in_second": jnp.clip(jnp.exp(math.log(1.7094811255446984e-07) - 2.7725887 * jax.random.uniform(keys[11], (D, 2 * FF), jnp.float32) ** block_levels(keys[11], (D, 2 * FF), ((0, 4), (1, 8)), -0.2, 0.2)), 1.0684257034654365e-08, 1.7094811255446984e-07),
        "down_weight": draw_down_weight(jax.random.fold_in(keys[18], 71), 0),
        "down_first": centred(keys[13], (FF, D), ((1.0 * PARAMS) ** -0.5), 0.001953125, ((0, 4), (1, 8)), jnp.float32),
        "down_second": jnp.clip(jnp.exp(math.log(1.7094811255446984e-07) - 2.7725887 * jax.random.uniform(keys[14], (FF, D), jnp.float32) ** block_levels(keys[14], (FF, D), ((0, 4), (1, 8)), -0.2, 0.2)), 1.0684257034654365e-08, 1.7094811255446984e-07),
        "small_params": draw_small_params(jax.random.fold_in(keys[18], 71), 0),
        "small_first": centred(keys[16], (8, SMALL // 8), ((1.0 * PARAMS) ** -0.5), 0.001953125, ((0, 4), (1, 8)), jnp.float32),
        "small_second": jnp.clip(jnp.exp(math.log(1.7094811255446984e-07) - 2.7725887 * jax.random.uniform(keys[17], (8, SMALL // 8), jnp.float32) ** block_levels(keys[17], (8, SMALL // 8), ((0, 4), (1, 8)), -0.2, 0.2)), 1.0684257034654365e-08, 1.7094811255446984e-07),
    }


NORM_EPS = 1e-06
ROPE_BASE = 1000000.0
BETA_FIRST = 0.5
BETA_SECOND = 0.5
ADAM_EPS = 1e-08
MATRIX_RATE = 0.03
SMALL_RATE = 0.3
MATRIX_DECAY = 0.1
CLIP_NORM = 1.0
MASKED = -1e+30
HIGHEST = lax.Precision.HIGHEST

@jax.custom_vjp
def low(v):
    return lax.optimization_barrier(v.astype(jnp.bfloat16)).astype(jnp.float32)

@jax.custom_vjp
def low_back(v):
    return v

def low_keep(v):
    return (low(v), None)

def low_pass(kept, grad):
    return (grad,)

def back_keep(v):
    return (v, None)

def back_low(kept, grad):
    return (low(grad),)
low.defvjp(low_keep, low_pass)
low_back.defvjp(back_keep, back_low)

def unpack_small(small_vec):
    grouped = small_vec.reshape(KV_HEADS * HEAD, 3 * GROUP + 2)
    gain_attn = grouped[:, :GROUP].reshape(-1)
    gain_mlp = grouped[:, GROUP:2 * GROUP].reshape(-1)
    biases = jnp.concatenate([grouped[:, 2 * GROUP:3 * GROUP].reshape(-1), grouped[:, 3 * GROUP], grouped[:, 3 * GROUP + 1]])
    return (gain_attn, gain_mlp, biases)

def rotate_half(values):
    half_width = HEAD // 2
    return jnp.concatenate([-values[..., half_width:], values[..., :half_width]], axis=-1)

def rope_tables(positions):
    pair_index = jnp.arange(HEAD // 2, dtype=jnp.float32)
    inverse = jnp.power(jnp.float32(ROPE_BASE), -2.0 * pair_index / HEAD)
    angles = positions[:, None] * inverse[None, :]
    angles = jnp.concatenate([angles, angles], axis=-1)
    return (jnp.cos(angles), jnp.sin(angles))

def rms_scale(values):
    return lax.rsqrt(lax.optimization_barrier(jnp.mean(values * values, axis=-1, keepdims=True)) + NORM_EPS)

def layer_group(params, inputs, group_lengths):
    qkv_mat, out_mat, in_mat, down_mat, small_vec = params
    group_size = inputs.shape[0]
    kv_width = KV_HEADS * HEAD
    gain_attn, gain_mlp, biases = unpack_small(small_vec)
    normed = low(inputs * rms_scale(inputs) * gain_attn)
    projected = low_back(jnp.einsum('gtd,de->gte', normed, qkv_mat, precision=HIGHEST)) + biases
    queries = projected[..., :D].reshape(group_size, SEQ, HEADS, HEAD)
    key_rows = projected[..., D:D + kv_width].reshape(group_size, SEQ, KV_HEADS, HEAD)
    values = low(projected[..., D + kv_width:].reshape(group_size, SEQ, KV_HEADS, HEAD))
    places = jnp.arange(SEQ, dtype=jnp.int32)
    cosine, sine_table = rope_tables(places.astype(jnp.float32))
    cosine = cosine[:, None, :]
    sine_table = sine_table[:, None, :]
    queries = low(queries * cosine + rotate_half(queries) * sine_table)
    queries = queries.reshape(group_size, SEQ, KV_HEADS, GROUP, HEAD)
    key_rows = low(key_rows * cosine + rotate_half(key_rows) * sine_table)
    scores = low_back(jnp.einsum('gtkhd,gskd->gkhts', queries, key_rows, precision=HIGHEST) * HEAD ** (-0.5))
    allowed = (places[None, :] <= places[:, None])[None] & (places[None, None, :] < group_lengths[:, None, None])
    scores = jnp.where(allowed[:, None, None], scores, MASKED)
    weights = low(jax.nn.softmax(scores, axis=-1))
    attended = jnp.einsum('gkhts,gskd->gtkhd', weights, values, precision=HIGHEST).reshape(group_size, SEQ, D)
    attended = low_back(low(attended))
    middle = inputs + low_back(jnp.einsum('gtd,de->gte', attended, out_mat, precision=HIGHEST))
    normed_again = low(middle * rms_scale(middle) * gain_mlp)
    gate_up = low_back(jnp.einsum('gtd,de->gte', normed_again, in_mat, precision=HIGHEST))
    hidden = low(jax.nn.silu(gate_up[..., :FF]) * gate_up[..., FF:])
    return middle + low_back(jnp.einsum('gtf,fd->gtd', hidden, down_mat, precision=HIGHEST))

def update(weight, first, second, gradient, clip_factor, rate, decay):
    step_grad = gradient * clip_factor
    first_new = BETA_FIRST * first + (1.0 - BETA_FIRST) * step_grad
    second_new = BETA_SECOND * second + (1.0 - BETA_SECOND) * step_grad * step_grad
    first_fix = 1.0 - BETA_FIRST ** STEP
    second_fix = 1.0 - BETA_SECOND ** STEP
    weight_new = weight - rate * (first_new / first_fix / (jnp.sqrt(second_new / second_fix) + ADAM_EPS) + decay * weight)
    return (weight_new, first_new, second_new, weight_new.astype(jnp.bfloat16))

def reference(tokens, cotangent, lengths, qkv_weight, qkv_first, qkv_second, out_weight, out_first, out_second, mlp_in_weight, mlp_in_first, mlp_in_second, down_weight, down_first, down_second, small_params, small_first, small_second):
    masters = (qkv_weight, out_weight, mlp_in_weight, down_weight, small_params.reshape(-1))
    copies = tuple((master.astype(jnp.bfloat16).astype(jnp.float32) for master in masters))
    group_size = math.gcd(SEQS, 4)
    batches = SEQS // group_size
    inputs = tokens.astype(jnp.float32).reshape(batches, group_size, SEQ, D)
    grouped_lengths = lengths.reshape(batches, group_size)

    def forward(params, block_inputs):

        def one_group(paired):
            return layer_group(params, paired[0], paired[1])
        return lax.map(jax.checkpoint(one_group), (block_inputs, grouped_lengths))
    outputs, pullback = jax.vjp(forward, copies, inputs)
    places = jnp.arange(SEQ, dtype=jnp.int32)
    valid = (places[None, :] < lengths[:, None]).astype(jnp.float32)
    cot_masked = (cotangent.astype(jnp.float32) * valid[:, :, None]).reshape(batches, group_size, SEQ, D)
    weight_grads, input_cot = pullback(cot_masked)
    small_grad = weight_grads[4].reshape(8, SMALL // 8)
    all_grads = (weight_grads[0], weight_grads[1], weight_grads[2], weight_grads[3], small_grad)
    squares = sum((jnp.sum(part_grad * part_grad) for part_grad in all_grads))
    grad_norm = jnp.sqrt(squares)
    clip_factor = CLIP_NORM / jnp.maximum(grad_norm, CLIP_NORM)
    qkv_out = update(qkv_weight, qkv_first, qkv_second, all_grads[0], clip_factor, MATRIX_RATE, MATRIX_DECAY)
    out_out = update(out_weight, out_first, out_second, all_grads[1], clip_factor, MATRIX_RATE, MATRIX_DECAY)
    mlp_out = update(mlp_in_weight, mlp_in_first, mlp_in_second, all_grads[2], clip_factor, MATRIX_RATE, MATRIX_DECAY)
    down_out = update(down_weight, down_first, down_second, all_grads[3], clip_factor, MATRIX_RATE, MATRIX_DECAY)
    small_out = update(small_params, small_first, small_second, all_grads[4], clip_factor, SMALL_RATE, 0.0)
    mixed = outputs.reshape(SEQS, SEQ, D).astype(jnp.bfloat16)
    input_grad = input_cot.reshape(SEQS, SEQ, D).astype(jnp.bfloat16)
    return (mixed, input_grad, grad_norm, qkv_out[0], qkv_out[1], qkv_out[2], qkv_out[3], out_out[0], out_out[1], out_out[2], out_out[3], mlp_out[0], mlp_out[1], mlp_out[2], mlp_out[3], down_out[0], down_out[1], down_out[2], down_out[3], small_out[0], small_out[1], small_out[2], small_out[3])
```

```python
import jax
import jax.numpy as jnp
from jax import lax
from jax.sharding import PartitionSpec as P

D = 1536
HEADS = 12
KV_HEADS = 2
HEAD = 128
FF = 8960
STEP = 5
GROUP = 6
SMALL = 5120
QKV = 2048
KV_WIDTH = KV_HEADS * HEAD


NORM_EPS = 1e-06
ROPE_BASE = 1000000.0
BETA_FIRST = 0.5
BETA_SECOND = 0.5
ADAM_EPS = 1e-08
MATRIX_RATE = 0.03
SMALL_RATE = 0.3
MATRIX_DECAY = 0.1
CLIP_NORM = 1.0
MASKED = -1e30
SCALE = HEAD ** (-0.5)
CHUNKS = (768, 768, 704)


def unpack_small(small_vec):
    grouped = small_vec.reshape(KV_HEADS * HEAD, 3 * GROUP + 2)
    gain_attn = grouped[:, :GROUP].reshape(-1)
    gain_mlp = grouped[:, GROUP : 2 * GROUP].reshape(-1)
    biases = jnp.concatenate(
        [
            grouped[:, 2 * GROUP : 3 * GROUP].reshape(-1),
            grouped[:, 3 * GROUP],
            grouped[:, 3 * GROUP + 1],
        ]
    )
    return (gain_attn, gain_mlp, biases)


def group_small(gain_attn, gain_mlp, biases):
    count = KV_HEADS * HEAD
    pieces = [
        gain_attn.reshape(count, GROUP),
        gain_mlp.reshape(count, GROUP),
        biases[:D].reshape(count, GROUP),
        biases[D : D + count][:, None],
        biases[D + count :][:, None],
    ]
    return jnp.concatenate(pieces, axis=1).reshape(8, SMALL // 8)


def rotate_half(values):
    half_width = HEAD // 2
    return jnp.concatenate([-values[..., half_width:], values[..., :half_width]], axis=-1)


def rope_tables(positions):
    pair_index = jnp.arange(HEAD // 2, dtype=jnp.float32)
    inverse = jnp.power(jnp.float32(ROPE_BASE), -2.0 * pair_index / HEAD)
    angles = positions[:, None] * inverse[None, :]
    angles = jnp.concatenate([angles, angles], axis=-1)
    return (jnp.cos(angles), jnp.sin(angles))


def rms_scale(values):
    return lax.rsqrt(jnp.mean(values * values, axis=-1, keepdims=True) + NORM_EPS)


def dot_nn(left, right):
    return jnp.dot(left, right, preferred_element_type=jnp.float32)


def dot_nt(left, right):
    return lax.dot_general(
        left, right, (((1,), (1,)), ((), ())), preferred_element_type=jnp.float32
    )


def dot_tn(left, right):
    return lax.dot_general(
        left, right, (((0,), (0,)), ((), ())), preferred_element_type=jnp.float32
    )


def update(weight, first, second, gradient, clip_factor, rate, decay):
    step_grad = gradient * clip_factor
    first_new = BETA_FIRST * first + (1.0 - BETA_FIRST) * step_grad
    second_new = BETA_SECOND * second + (1.0 - BETA_SECOND) * step_grad * step_grad
    first_fix = 1.0 - BETA_FIRST**STEP
    second_fix = 1.0 - BETA_SECOND**STEP
    weight_new = weight - rate * (
        first_new / first_fix / (jnp.sqrt(second_new / second_fix) + ADAM_EPS) + decay * weight
    )
    return (weight_new, first_new, second_new, weight_new.astype(jnp.bfloat16))


def dp_send(block, k):
    count = lax.axis_size("dp")
    return lax.ppermute(block, "dp", [(i, i ^ k) for i in range(count)])


def core_swap(block):
    count = lax.axis_size("fsdp")
    return lax.ppermute(block, "fsdp", [(i, i ^ 1) for i in range(count)])


def dp_gather(block):
    return [block] + [dp_send(block, k) for k in range(1, lax.axis_size("dp"))]


def dp_own(array, k):
    return lax.dynamic_index_in_dim(array, lax.axis_index("dp") ^ k, 0, keepdims=False)


def dp_exchange(array):
    count = lax.axis_size("dp")
    place = lax.axis_index("dp")
    got = jnp.stack([dp_own(array, 0)] + [dp_send(dp_own(array, k), k) for k in range(1, count)])
    return jnp.stack(
        [lax.dynamic_index_in_dim(got, place ^ a, 0, keepdims=False) for a in range(count)]
    )


def dp_columns(array, k, width):
    return lax.dynamic_slice_in_dim(array, (lax.axis_index("dp") ^ k) * width, width, 1)


def dp_order(blocks):
    place = lax.axis_index("dp")
    stacked = jnp.stack(blocks)
    return jnp.concatenate(
        [
            lax.dynamic_index_in_dim(stacked, place ^ a, 0, keepdims=False)
            for a in range(len(blocks))
        ],
        axis=1,
    )


def parity_groups():
    count = lax.axis_size("fsdp")
    return [[2 * i + c for i in range(count // 2)] for c in range(2)]


def is_even():
    return lax.rem(lax.axis_index("fsdp"), 2) == 0


def gather_matrix(shard):
    piece = shard.T
    along = lax.all_gather(
        piece, "fsdp", axis=0, tiled=True, axis_index_groups=parity_groups()
    )
    own = dp_gather(along)
    other = [core_swap(block) for block in own]
    return own, other


def interleave(own, other):
    slices = lax.axis_size("fsdp") // 2
    rows = own.shape[0]
    even = jnp.where(is_even(), own, other)
    odd = jnp.where(is_even(), other, own)
    both = jnp.stack([even.reshape(rows, slices, -1), odd.reshape(rows, slices, -1)], axis=2)
    return both.reshape(rows, -1)


def split_parity(array):
    slices = lax.axis_size("fsdp") // 2
    rows = array.shape[0]
    both = array.reshape(rows, slices, 2, -1)
    even = both[:, :, 0].reshape(rows, -1)
    odd = both[:, :, 1].reshape(rows, -1)
    return jnp.where(is_even(), even, odd), jnp.where(is_even(), odd, even)


def reduce_matrix(own_terms, other_terms):
    summed = [
        mine.astype(jnp.float32) + core_swap(theirs).astype(jnp.float32)
        for mine, theirs in zip(own_terms, other_terms)
    ]
    total = summed[0]
    for k in range(1, len(summed)):
        total = total + dp_send(summed[k].astype(jnp.bfloat16), k).astype(jnp.float32)
    shard = lax.psum_scatter(
        total.astype(jnp.bfloat16),
        "fsdp",
        scatter_dimension=0,
        tiled=True,
        axis_index_groups=parity_groups(),
    )
    return shard.T.astype(jnp.float32)


def bf16(array):
    return array.astype(jnp.bfloat16)


def mlp_in_pieces(shard):
    ranks = lax.axis_size("dp")
    rows, columns = shard.shape
    part = columns // ranks
    sent = shard.reshape(rows, ranks, part).transpose(1, 2, 0)
    got = dp_exchange(sent)
    return got.transpose(1, 0, 2).reshape(part, ranks * rows)


def mlp_in_back(grad):
    ranks = lax.axis_size("dp")
    part = grad.shape[0]
    rows = grad.shape[1] // ranks
    got = dp_exchange(grad.reshape(part, ranks, rows).transpose(1, 0, 2))
    return got.transpose(2, 0, 1).reshape(rows, ranks * part)


def down_pieces(shard, part):
    ranks = lax.axis_size("dp")
    units, columns = shard.shape
    slices = units // (ranks * part)
    sent = shard.reshape(slices, ranks, part, columns).transpose(1, 3, 0, 2)
    got = dp_exchange(sent)
    return got.transpose(1, 0, 2, 3).reshape(columns, ranks * slices, part)


def down_back(grad):
    ranks = lax.axis_size("dp")
    columns, all_slices, part = grad.shape
    slices = all_slices // ranks
    got = dp_exchange(grad.reshape(columns, ranks, slices, part).transpose(1, 0, 2, 3))
    return got.transpose(2, 0, 3, 1).reshape(slices * ranks * part, columns)


def sharded_pass(tokens, cotangent, lengths, half_qkv, half_out, half_in, half_down, half_small):
    ranks = lax.axis_size("dp")
    lines = lax.axis_size("fsdp")
    place = lax.axis_index("dp")
    local_rows = tokens.shape[1]
    block_rows = D // ranks

    qkv_own, qkv_other = gather_matrix(half_qkv)
    small_full = lax.all_gather(half_small, ("dp", "fsdp"), axis=0, tiled=False)
    small_rows, small_columns = half_small.shape
    small_vec = small_full.reshape(ranks, lines, small_rows, small_columns)
    small_vec = small_vec.transpose(0, 2, 1, 3).reshape(-1).astype(jnp.float32)
    gain_attn, gain_mlp, biases = unpack_small(small_vec)

    out_own, out_other = gather_matrix(half_out)
    part = half_in.shape[1] // ranks
    in_piece = mlp_in_pieces(half_in)
    down_piece = down_pieces(half_down, part)
    slices = lines // 2
    in_chunks = []
    down_chunks = []
    start = 0
    for size in CHUNKS:
        width = size // slices
        in_chunks.append(
            lax.all_gather(in_piece[start : start + width], "fsdp", axis=0, tiled=True)
        )
        down_chunks.append(
            lax.all_gather(
                down_piece[:, :, start : start + width].reshape(-1, size),
                "fsdp",
                axis=0,
                tiled=True,
            )
        )
        start += width

    inputs = tokens[0].astype(jnp.float32)
    row_length = lengths[0]
    local_places = jnp.arange(local_rows, dtype=jnp.int32)
    query_places = place * local_rows + local_places
    key_places = jnp.concatenate([(place ^ k) * local_rows + local_places for k in range(ranks)])
    valid = (query_places < row_length).astype(jnp.float32)
    out_cot = cotangent[0].astype(jnp.float32) * valid[:, None]
    out_cot_all = jnp.concatenate(dp_gather(bf16(out_cot)))

    cosine, sine_table = rope_tables(query_places.astype(jnp.float32))
    cosine = cosine[:, None, :]
    sine_table = sine_table[:, None, :]
    first_scale = rms_scale(inputs)
    first_normed = inputs * first_scale
    normed = bf16(first_normed * gain_attn)
    normed_blocks = [dp_columns(normed, k, block_rows) for k in range(ranks)]
    projected = interleave(
        sum(dot_nt(block, mat) for block, mat in zip(normed_blocks, qkv_own)),
        sum(dot_nt(block, mat) for block, mat in zip(normed_blocks, qkv_other)),
    )
    projected = projected + biases
    queries = projected[:, :D].reshape(local_rows, HEADS, HEAD)
    key_rows = projected[:, D : D + KV_WIDTH].reshape(local_rows, KV_HEADS, HEAD)
    queries = bf16(queries * cosine + rotate_half(queries) * sine_table)
    queries = queries.reshape(local_rows, KV_HEADS, GROUP, HEAD)
    key_rows = bf16(key_rows * cosine + rotate_half(key_rows) * sine_table)
    key_rows = key_rows.reshape(local_rows, KV_WIDTH)
    value_rows = bf16(projected[:, D + KV_WIDTH :])
    kv_all = jnp.concatenate(dp_gather(jnp.concatenate([key_rows, value_rows], axis=1)))
    all_keys = kv_all[:, :KV_WIDTH].reshape(-1, KV_HEADS, HEAD)
    all_values = kv_all[:, KV_WIDTH:].reshape(-1, KV_HEADS, HEAD)
    allowed = (key_places[None, :] <= query_places[:, None]) & (key_places[None, :] < row_length)

    def score_block():
        raw_scores = (
            jnp.einsum("tkhd,skd->khts", queries, all_keys, preferred_element_type=jnp.float32)
            * SCALE
        )
        return jnp.where(allowed[None, None], raw_scores, MASKED)

    scores = score_block()
    row_peak = jnp.max(scores, axis=-1, keepdims=True)
    exponent = jnp.exp(scores - row_peak)
    row_total = jnp.sum(exponent, axis=-1, keepdims=True)
    log_total = row_peak + jnp.log(row_total)
    probs_low = bf16(exponent / row_total)
    attended = jnp.einsum(
        "khts,skd->tkhd", probs_low, all_values, preferred_element_type=jnp.float32
    )
    attended = bf16(attended.reshape(local_rows, D))
    attended_blocks = [dp_columns(attended, k, block_rows) for k in range(ranks)]
    middle = inputs + interleave(
        sum(dot_nt(block, mat) for block, mat in zip(attended_blocks, out_own)),
        sum(dot_nt(block, mat) for block, mat in zip(attended_blocks, out_other)),
    )
    second_scale = rms_scale(middle)
    second_normed = middle * second_scale
    normed_again = bf16(second_normed * gain_mlp)

    normed_all = jnp.concatenate(dp_gather(normed_again))
    mixed_part = 0.0
    back_part = 0.0
    in_grads = []
    down_grads = []
    for size, in_mat, down_mat in zip(CHUNKS, in_chunks, down_chunks):
        gate_up = dot_nt(normed_all, in_mat)
        gate = gate_up[:, :size]
        up = gate_up[:, size:]
        sigmoid_gate = jax.nn.sigmoid(gate)
        activated = gate * sigmoid_gate
        hidden = bf16(activated * up)
        mixed_part = mixed_part + dot_nt(hidden, down_mat)
        hidden_cot = dot_nn(out_cot_all, down_mat)
        gate_cot = hidden_cot * up * sigmoid_gate * (1.0 + gate * (1.0 - sigmoid_gate))
        up_cot = hidden_cot * activated
        gate_up_cot = bf16(jnp.concatenate([gate_cot, up_cot], axis=1))
        back_part = back_part + dot_nn(gate_up_cot, in_mat)
        down_grads.append(
            lax.psum_scatter(
                bf16(dot_tn(out_cot_all, hidden)), "fsdp", scatter_dimension=0, tiled=True
            ).reshape(-1, slices, size // slices)
        )
        in_grads.append(
            lax.psum_scatter(
                bf16(dot_tn(gate_up_cot, normed_all)), "fsdp", scatter_dimension=0, tiled=True
            )
        )

    def token_reduce(partial):
        partial = partial.reshape(ranks, local_rows, D)
        total = partial[0]
        for k in range(1, ranks):
            total = total + dp_send(bf16(partial[k]), k).astype(jnp.float32)
        return total

    normed_again_cot = token_reduce(back_part)
    mixed = bf16(middle + token_reduce(mixed_part))
    in_grad = mlp_in_back(jnp.concatenate(in_grads)).astype(jnp.float32)
    down_grad = down_back(jnp.concatenate(down_grads, axis=2)).astype(jnp.float32)

    gain_mlp_grad = jnp.sum(normed_again_cot * second_normed, axis=0)
    scaled_second = normed_again_cot * gain_mlp
    middle_cot = out_cot + second_scale * (
        scaled_second
        - second_normed * jnp.mean(scaled_second * second_normed, axis=-1, keepdims=True)
    )
    middle_low = bf16(middle_cot)
    middle_own, middle_other = split_parity(middle_low)
    out_grad = reduce_matrix(
        [bf16(dot_tn(middle_own, block)) for block in attended_blocks],
        [bf16(dot_tn(middle_other, block)) for block in attended_blocks],
    )
    attended_cot = bf16(
        dp_order(
            [
                dot_nn(middle_own, mine) + dot_nn(middle_other, theirs)
                for mine, theirs in zip(out_own, out_other)
            ]
        )
    ).reshape(local_rows, KV_HEADS, GROUP, HEAD)
    scores = score_block()
    probs = jnp.exp(scores - log_total)
    probs_again = bf16(probs)
    probs_cot = jnp.einsum(
        "tkhd,skd->khts", attended_cot, all_values, preferred_element_type=jnp.float32
    )
    row_dot = jnp.sum(probs * probs_cot, axis=-1, keepdims=True)
    scores_cot = bf16(probs * (probs_cot - row_dot))
    query_cot = jnp.einsum(
        "khts,skd->tkhd", scores_cot, all_keys, preferred_element_type=jnp.float32
    )
    query_cot = query_cot.reshape(local_rows, HEADS, HEAD) * SCALE
    key_cot = jnp.einsum("khts,tkhd->skd", scores_cot, queries, preferred_element_type=jnp.float32)
    key_cot = key_cot.reshape(-1, KV_WIDTH) * SCALE
    value_cot = jnp.einsum(
        "khts,tkhd->skd", probs_again, attended_cot, preferred_element_type=jnp.float32
    )
    value_cot = value_cot.reshape(-1, KV_WIDTH)
    kv_cot = jnp.concatenate([key_cot, value_cot], axis=1).reshape(ranks, local_rows, -1)
    kv_total = kv_cot[0]
    for k in range(1, ranks):
        kv_total = kv_total + dp_send(bf16(kv_cot[k]), k).astype(jnp.float32)
    query_back = query_cot * cosine - rotate_half(query_cot * sine_table)
    key_local = kv_total[:, :KV_WIDTH].reshape(local_rows, KV_HEADS, HEAD)
    key_back = key_local * cosine - rotate_half(key_local * sine_table)
    projected_cot = jnp.concatenate(
        [
            query_back.reshape(local_rows, D),
            key_back.reshape(local_rows, KV_WIDTH),
            kv_total[:, KV_WIDTH:],
        ],
        axis=1,
    )
    bias_grad = jnp.sum(projected_cot, axis=0)
    projected_low = bf16(projected_cot)
    projected_own, projected_other = split_parity(projected_low)
    qkv_grad = reduce_matrix(
        [bf16(dot_tn(projected_own, block)) for block in normed_blocks],
        [bf16(dot_tn(projected_other, block)) for block in normed_blocks],
    )
    normed_cot = dp_order(
        [
            dot_nn(projected_own, mine) + dot_nn(projected_other, theirs)
            for mine, theirs in zip(qkv_own, qkv_other)
        ]
    )
    gain_attn_grad = jnp.sum(normed_cot * first_normed, axis=0)
    scaled_first = normed_cot * gain_attn
    input_cot = middle_cot + first_scale * (
        scaled_first - first_normed * jnp.mean(scaled_first * first_normed, axis=-1, keepdims=True)
    )
    small_term = group_small(gain_attn_grad, gain_mlp_grad, bias_grad)
    small_sum = lax.psum(small_term, ("dp", "fsdp"))
    small_grad = lax.dynamic_slice(
        small_sum,
        (place * small_rows, lax.axis_index("fsdp") * small_columns),
        (small_rows, small_columns),
    )
    return (mixed, input_cot, qkv_grad, out_grad, in_grad, down_grad, small_grad)


def per_device(
    tokens,
    cotangent,
    lengths,
    qkv_weight,
    qkv_first,
    qkv_second,
    out_weight,
    out_first,
    out_second,
    mlp_in_weight,
    mlp_in_first,
    mlp_in_second,
    down_weight,
    down_first,
    down_second,
    small_params,
    small_first,
    small_second,
):
    results = sharded_pass(
        tokens,
        cotangent,
        lengths,
        bf16(qkv_weight),
        bf16(out_weight),
        bf16(mlp_in_weight),
        bf16(down_weight),
        bf16(small_params),
    )
    mixed, input_cot, qkv_grad, out_grad, in_grad, down_grad, small_grad = results
    local_squares = sum(
        (jnp.sum(piece * piece) for piece in (qkv_grad, out_grad, in_grad, down_grad, small_grad))
    )
    total_squares = lax.psum(local_squares, ("dp", "fsdp"))
    grad_norm = jnp.sqrt(total_squares)
    clip_factor = CLIP_NORM / jnp.maximum(grad_norm, CLIP_NORM)
    outs = [mixed[None], bf16(input_cot)[None], grad_norm]
    for weight, first, second, gradient, rate, decay in (
        (qkv_weight, qkv_first, qkv_second, qkv_grad, MATRIX_RATE, MATRIX_DECAY),
        (out_weight, out_first, out_second, out_grad, MATRIX_RATE, MATRIX_DECAY),
        (mlp_in_weight, mlp_in_first, mlp_in_second, in_grad, MATRIX_RATE, MATRIX_DECAY),
        (down_weight, down_first, down_second, down_grad, MATRIX_RATE, MATRIX_DECAY),
        (small_params, small_first, small_second, small_grad, SMALL_RATE, 0.0),
    ):
        outs.extend(update(weight, first, second, gradient, clip_factor, rate, decay))
    return tuple(outs)


def solution(mesh):
    rows = P("fsdp", "dp", None)
    shard = P("dp", "fsdp")
    return jax.shard_map(
        per_device,
        mesh=mesh,
        in_specs=(rows, rows, P("fsdp")) + (shard,) * 15,
        out_specs=(rows, rows, P()) + (shard,) * 20,
        check_vma=False,
    )
```

```python
import functools
import math

import jax
import jax.numpy as jnp
from jax import lax
from jax.experimental import pallas as pl
from jax.experimental.pallas import tpu as pltpu
from jax.sharding import PartitionSpec as P

D = 1536
HEADS = 12
KV_HEADS = 2
HEAD = 128
FF = 8960
STEP = 5
GROUP = 6
SMALL = 5120
QKV = 2048
KV_WIDTH = KV_HEADS * HEAD


NORM_EPS = 1e-06
ROPE_BASE = 1000000.0
BETA_FIRST = 0.5
BETA_SECOND = 0.5
ADAM_EPS = 1e-08
MATRIX_RATE = 0.03
SMALL_RATE = 0.3
MATRIX_DECAY = 0.1
CLIP_NORM = 1.0
MASKED = -1e30
SCALE = HEAD ** (-0.5)
CHUNKS = (1024, 1216)
UNIT_TILE = 512
TOKEN_TILE = 640
GRAD_TILE = 512
TURN_TILE = 256
VMEM_LIMIT = 60 * 2**20


def unpack_small(small_vec):
    grouped = small_vec.reshape(KV_HEADS * HEAD, 3 * GROUP + 2)
    gain_attn = grouped[:, :GROUP].reshape(-1)
    gain_mlp = grouped[:, GROUP : 2 * GROUP].reshape(-1)
    biases = jnp.concatenate(
        [
            grouped[:, 2 * GROUP : 3 * GROUP].reshape(-1),
            grouped[:, 3 * GROUP],
            grouped[:, 3 * GROUP + 1],
        ]
    )
    return (gain_attn, gain_mlp, biases)


def group_small(gain_attn, gain_mlp, biases):
    count = KV_HEADS * HEAD
    pieces = [
        gain_attn.reshape(count, GROUP),
        gain_mlp.reshape(count, GROUP),
        biases[:D].reshape(count, GROUP),
        biases[D : D + count][:, None],
        biases[D + count :][:, None],
    ]
    return jnp.concatenate(pieces, axis=1).reshape(8, SMALL // 8)


def rope_tables(positions):
    pair_index = jnp.arange(HEAD // 2, dtype=jnp.float32)
    inverse = jnp.power(jnp.float32(ROPE_BASE), -2.0 * pair_index / HEAD)
    angles = positions[:, None] * inverse[None, :]
    angles = jnp.concatenate([angles, angles], axis=-1)
    return (jnp.cos(angles), jnp.sin(angles))


def bf16(array):
    return array.astype(jnp.bfloat16)


def dot_nn(left, right):
    return jnp.dot(left, right, preferred_element_type=jnp.float32)


def dot_nt(left, right):
    return lax.dot_general(
        left, right, (((1,), (1,)), ((), ())), preferred_element_type=jnp.float32
    )


def dot_tn(left, right):
    return lax.dot_general(
        left, right, (((0,), (0,)), ((), ())), preferred_element_type=jnp.float32
    )


def update(weight, first, second, gradient, clip_factor, rate, decay):
    step_grad = gradient * clip_factor
    first_new = BETA_FIRST * first + (1.0 - BETA_FIRST) * step_grad
    second_new = BETA_SECOND * second + (1.0 - BETA_SECOND) * step_grad * step_grad
    first_fix = 1.0 - BETA_FIRST**STEP
    second_fix = 1.0 - BETA_SECOND**STEP
    weight_new = weight - rate * (
        first_new / first_fix / (jnp.sqrt(second_new / second_fix) + ADAM_EPS) + decay * weight
    )
    return (weight_new, first_new, second_new, weight_new.astype(jnp.bfloat16))


def dp_send(block, k):
    count = lax.axis_size("dp")
    return lax.ppermute(block, "dp", [(i, i ^ k) for i in range(count)])


def core_swap(block):
    count = lax.axis_size("fsdp")
    return lax.ppermute(block, "fsdp", [(i, i ^ 1) for i in range(count)])


def dp_gather(block):
    return [block] + [dp_send(block, k) for k in range(1, lax.axis_size("dp"))]


def dp_own(array, k):
    return lax.dynamic_index_in_dim(array, lax.axis_index("dp") ^ k, 0, keepdims=False)


def dp_exchange(array):
    count = lax.axis_size("dp")
    place = lax.axis_index("dp")
    got = jnp.stack([dp_own(array, 0)] + [dp_send(dp_own(array, k), k) for k in range(1, count)])
    return jnp.stack(
        [lax.dynamic_index_in_dim(got, place ^ a, 0, keepdims=False) for a in range(count)]
    )


def line_send(block, r):
    count = lax.axis_size("fsdp")
    return lax.ppermute(block, "fsdp", [(i, i ^ (2 * r)) for i in range(count)])


def line_gather(block):
    count = lax.axis_size("fsdp") // 2
    place = lax.axis_index("fsdp") // 2
    got = jnp.stack([block] + [line_send(block, r) for r in range(1, count)])
    return jnp.stack(
        [lax.dynamic_index_in_dim(got, place ^ a, 0, keepdims=False) for a in range(count)]
    )


def sum_everywhere(term):
    term = term + core_swap(term)
    lines = [line_send(term, r) for r in range(1, lax.axis_size("fsdp") // 2)]
    term = term + sum(lines)
    return term + sum(dp_send(term, k) for k in range(1, lax.axis_size("dp")))


def is_even():
    return lax.rem(lax.axis_index("fsdp"), 2) == 0


def gather_line(piece):
    return line_gather(piece).reshape(-1, piece.shape[1])


def gather_rest(along):
    own = dp_gather(along)
    return own, [core_swap(block) for block in own]


def reduce_matrix(own_terms, other_terms):
    summed = [
        mine.astype(jnp.float32) + core_swap(theirs).astype(jnp.float32)
        for mine, theirs in zip(own_terms, other_terms)
    ]
    total = summed[0]
    for k in range(1, len(summed)):
        total = total + dp_send(summed[k].astype(jnp.bfloat16), k).astype(jnp.float32)
    count = lax.axis_size("fsdp") // 2
    place = lax.axis_index("fsdp") // 2
    parts = total.reshape(count, -1, total.shape[1])
    shard = lax.dynamic_index_in_dim(parts, place, 0, keepdims=False)
    for r in range(1, count):
        part = lax.dynamic_index_in_dim(parts, place ^ r, 0, keepdims=False)
        shard = shard + line_send(bf16(part), r).astype(jnp.float32)
    return shard.T


def exchange_weights(half_in, half_down):
    ranks = lax.axis_size("dp")
    rows, columns = half_in.shape
    part = columns // ranks
    width = half_down.shape[1]
    slices = half_down.shape[0] // (ranks * part)
    in_sent = half_in.reshape(rows, ranks, part).transpose(1, 2, 0)
    down_sent = half_down.reshape(slices, ranks, part, width).transpose(1, 2, 0, 3)
    sent = jnp.concatenate([in_sent, down_sent.reshape(ranks, part, slices * width)], axis=2)
    got = yield sent
    in_piece = got[:, :, :rows].transpose(1, 0, 2).reshape(part, ranks * rows)
    down_piece = got[:, :, rows:].reshape(ranks, part, slices, width).transpose(3, 0, 2, 1)
    yield in_piece, down_piece.reshape(width, ranks * slices, part)


def exchange_gradients(in_grad, down_grad, columns):
    ranks = lax.axis_size("dp")
    part = in_grad.shape[0]
    rows = in_grad.shape[1] // ranks
    slices = down_grad.shape[1] // ranks
    in_sent = in_grad.reshape(part, ranks, rows).transpose(1, 0, 2)
    down_sent = down_grad.reshape(columns, ranks, slices, part).transpose(1, 3, 2, 0)
    sent = jnp.concatenate([in_sent, down_sent.reshape(ranks, part, slices * columns)], axis=2)
    got = dp_exchange(sent)
    return got[:, :, :rows], got[:, :, rows:].reshape(ranks, part, slices, columns)


def column_slices(own, other, first, target, width, slices):
    for j in range(slices):
        mine = own(j)
        theirs = other(j)
        target[:, pl.ds(2 * j * width, width)] = jnp.where(first, mine, theirs)
        target[:, pl.ds((2 * j + 1) * width, width)] = jnp.where(first, theirs, mine)


def block_columns(ref, place, k, width):
    return ref[:, pl.ds(pl.multiple_of((place ^ k) * width, 128), width)]


def project_kernel(ranks, slices, *refs):
    info, tokens, gain, bias, cosine, sine = refs[:6]
    own = refs[6 : 6 + ranks]
    other = refs[6 + ranks : 6 + 2 * ranks]
    normed, queries, kv, proj = refs[6 + 2 * ranks :]
    place = info[0]
    first = info[1] == 0
    width = own[0].shape[1]
    step = own[0].shape[0] // slices
    part = QKV // (2 * slices)
    x = tokens[...].astype(jnp.float32)
    scale = lax.rsqrt(jnp.mean(x * x, axis=-1, keepdims=True) + NORM_EPS)
    normed[...] = bf16(x * scale * gain[...])

    def product(mats, j):
        return sum(
            dot_nt(block_columns(normed, place, k, width), mats[k][pl.ds(j * step, part), :])
            for k in range(ranks)
        )

    column_slices(
        lambda j: product(own, j), lambda j: product(other, j), first, proj, part, slices
    )
    for h in range(HEADS + KV_HEADS):
        cols = pl.ds(h * HEAD, HEAD)
        u = proj[:, cols] + bias[:, cols]
        turned = bf16(u * cosine[...] + pltpu.roll(u, HEAD // 2, 1) * sine[...])
        if h < HEADS:
            queries[:, cols] = turned
        else:
            kv[:, pl.ds((h - HEADS) * HEAD, HEAD)] = turned
    cols = pl.ds(D + KV_WIDTH, KV_WIDTH)
    kv[:, pl.ds(KV_WIDTH, KV_WIDTH)] = bf16(proj[:, cols] + bias[:, cols])


def score_bias(info, rows, ranks, target):
    place = info[0]
    length = info[2]
    query = place * rows + lax.broadcasted_iota(jnp.int32, (rows, rows), 1)
    for k in range(ranks):
        key = (place ^ k) * rows + lax.broadcasted_iota(jnp.int32, (rows, rows), 0)
        seen = (key <= query) & (key < length)
        target[pl.ds(k * rows, rows), :] = jnp.where(seen, 0.0, MASKED)


def attend_kernel(ranks, slices, *refs):
    info, tokens, gain, queries = refs[:4]
    kv = refs[4 : 4 + ranks]
    own = refs[4 + ranks : 4 + 2 * ranks]
    other = refs[4 + 2 * ranks : 4 + 3 * ranks]
    attended, totals, middle, normed_again, bias, keys, values, values_t = refs[4 + 3 * ranks :]
    place = info[0]
    first = info[1] == 0
    rows = tokens.shape[0]
    width = own[0].shape[1]
    part = own[0].shape[0] // slices
    score_bias(info, rows, ranks, bias)
    for k in range(ranks):
        keys[pl.ds(k * rows, rows), :] = kv[k][:, pl.ds(0, KV_WIDTH)]
        values[pl.ds(k * rows, rows), :] = kv[k][:, pl.ds(KV_WIDTH, KV_WIDTH)]
    values_t[...] = values[...].T

    @pl.loop(0, HEADS)
    def _(h):
        cols = pl.ds(pl.multiple_of(h * HEAD, HEAD), HEAD)
        kv_cols = pl.ds(pl.multiple_of((h // GROUP) * HEAD, HEAD), HEAD)
        scores = dot_nt(keys[:, kv_cols], queries[:, cols]) * SCALE + bias[...]
        peak = jnp.max(scores, axis=0, keepdims=True)
        exponent = jnp.exp(scores - peak)
        total = jnp.sum(exponent, axis=0, keepdims=True)
        totals[pl.ds(h, 1), :] = peak + jnp.log(total)
        probs = bf16(exponent * (1.0 / total))
        attended[:, cols] = bf16(dot_nn(values_t[kv_cols, :], probs).T)

    def product(mats, j):
        return sum(
            dot_nt(block_columns(attended, place, k, width), mats[k][pl.ds(j * part, part), :])
            for k in range(ranks)
        )

    column_slices(
        lambda j: product(own, j), lambda j: product(other, j), first, middle, part, slices
    )
    total = middle[...] + tokens[...].astype(jnp.float32)
    middle[...] = total
    scale = lax.rsqrt(jnp.mean(total * total, axis=-1, keepdims=True) + NORM_EPS)
    normed_again[...] = bf16(total * scale * gain[...])


def attend_back_kernel(ranks, slices, *refs):
    info, middle, cotangent, gain, queries, totals = refs[:6]
    got = refs[6 : 6 + ranks]
    kv = refs[6 + ranks : 6 + 2 * ranks]
    own = refs[6 + 2 * ranks : 6 + 3 * ranks]
    other = refs[6 + 3 * ranks : 6 + 4 * ranks]
    refs = refs[6 + 4 * ranks :]
    middle_cot, middle_low, gain_grad, query_cot = refs[:4]
    kv_cot = refs[4 : 4 + ranks]
    bias, keys, values, keys_t, attended_cot, key_sum, value_sum, low_own, low_other = refs[
        4 + ranks :
    ]
    place = info[0]
    first = info[1] == 0
    rows = middle.shape[0]
    width = own[0].shape[1]
    part = own[0].shape[0] // slices
    position = place * rows + lax.broadcasted_iota(jnp.int32, (rows, 1), 0)
    valid = jnp.where(position < info[2], 1.0, 0.0)
    cot = got[0][...].astype(jnp.float32)
    for k in range(1, ranks):
        cot = cot + got[k][...].astype(jnp.float32)
    v = middle[...]
    scale = lax.rsqrt(jnp.mean(v * v, axis=-1, keepdims=True) + NORM_EPS)
    n = v * scale
    gain_grad[...] = jnp.sum(cot * n, axis=0, keepdims=True)
    scaled = cot * gain[...]
    back = scale * (scaled - n * jnp.mean(scaled * n, axis=-1, keepdims=True))
    back = back + cotangent[...].astype(jnp.float32) * valid
    middle_cot[...] = back
    middle_low[...] = bf16(back)
    for j in range(slices):
        even = middle_low[:, pl.ds(2 * j * part, part)]
        odd = middle_low[:, pl.ds((2 * j + 1) * part, part)]
        low_own[:, pl.ds(j * part, part)] = jnp.where(first, even, odd)
        low_other[:, pl.ds(j * part, part)] = jnp.where(first, odd, even)
    for k in range(ranks):
        cols = pl.ds(pl.multiple_of((place ^ k) * width, 128), width)
        attended_cot[:, cols] = bf16(
            dot_nn(low_own[...], own[k][...]) + dot_nn(low_other[...], other[k][...])
        )
    score_bias(info, rows, ranks, bias)
    for k in range(ranks):
        keys[pl.ds(k * rows, rows), :] = kv[k][:, pl.ds(0, KV_WIDTH)]
        values[pl.ds(k * rows, rows), :] = kv[k][:, pl.ds(KV_WIDTH, KV_WIDTH)]
    keys_t[...] = keys[...].T
    key_sum[...] = jnp.zeros_like(key_sum)
    value_sum[...] = jnp.zeros_like(value_sum)

    @pl.loop(0, HEADS)
    def _(h):
        cols = pl.ds(pl.multiple_of(h * HEAD, HEAD), HEAD)
        kv_cols = pl.ds(pl.multiple_of((h // GROUP) * HEAD, HEAD), HEAD)
        query = queries[:, cols]
        out_cot = attended_cot[:, cols]
        scores = dot_nt(keys[:, kv_cols], query) * SCALE + bias[...]
        probs = jnp.exp(scores - totals[pl.ds(h, 1), :])
        probs_cot = dot_nt(values[:, kv_cols], out_cot)
        row_dot = jnp.sum(probs * probs_cot, axis=0, keepdims=True)
        scores_cot = bf16(probs * (probs_cot - row_dot))
        value_sum[:, kv_cols] += dot_nn(bf16(probs), out_cot)
        key_sum[:, kv_cols] += dot_nn(scores_cot, query)
        query_cot[:, cols] = dot_nn(keys_t[kv_cols, :], scores_cot).T * SCALE

    for k in range(ranks):
        at = pl.ds(k * rows, rows)
        kv_cot[k][:, pl.ds(0, KV_WIDTH)] = bf16(key_sum[at, :] * SCALE)
        kv_cot[k][:, pl.ds(KV_WIDTH, KV_WIDTH)] = bf16(value_sum[at, :])


def outer_kernel(ranks, slices, *refs):
    info, left, right = refs[:3]
    own = refs[3 : 3 + ranks]
    other = refs[3 + ranks : 3 + 2 * ranks]
    (turned,) = refs[3 + 2 * ranks :]
    place = info[0]
    parity = info[1]
    width = own[0].shape[1]
    part = own[0].shape[0] // slices
    turned[...] = right[...].T
    for k in range(ranks):
        block = block_columns(left, place, k, width)
        for j in range(slices):
            at = pl.ds(j * part, part)
            mine = pl.ds(pl.multiple_of((2 * j + parity) * part, 16), part)
            theirs = pl.ds(pl.multiple_of((2 * j + 1 - parity) * part, 16), part)
            own[k][at, :] = bf16(dot_nn(turned[mine, :], block))
            other[k][at, :] = bf16(dot_nn(turned[theirs, :], block))


def project_back_kernel(ranks, *refs):
    info, query_cot, cosine, sine = refs[:4]
    got = refs[4 : 4 + ranks]
    projected_low, bias_grad = refs[4 + ranks :]
    kv_cot = got[0][...].astype(jnp.float32)
    for k in range(1, ranks):
        kv_cot = kv_cot + got[k][...].astype(jnp.float32)
    for h in range(HEADS + 2 * KV_HEADS):
        cols = pl.ds(h * HEAD, HEAD)
        if h < HEADS:
            u = query_cot[:, cols]
        else:
            u = kv_cot[:, (h - HEADS) * HEAD : (h - HEADS + 1) * HEAD]
        if h < HEADS + KV_HEADS:
            u = u * cosine[...] + pltpu.roll(u * sine[...], HEAD // 2, 1)
        bias_grad[:, cols] = jnp.sum(u, axis=0, keepdims=True)
        projected_low[:, cols] = bf16(u)


def input_back_kernel(ranks, slices, *refs):
    info, projected_low, tokens, gain, middle_cot = refs[:5]
    own = refs[5 : 5 + ranks]
    other = refs[5 + ranks : 5 + 2 * ranks]
    input_grad, gain_grad, low_own, low_other, normed_cot = refs[5 + 2 * ranks :]
    place = info[0]
    first = info[1] == 0
    width = own[0].shape[1]
    step = own[0].shape[0] // slices
    part = QKV // (2 * slices)
    for j in range(slices):
        even = projected_low[:, pl.ds(2 * j * part, part)]
        odd = projected_low[:, pl.ds((2 * j + 1) * part, part)]
        low_own[:, pl.ds(j * part, part)] = jnp.where(first, even, odd)
        low_other[:, pl.ds(j * part, part)] = jnp.where(first, odd, even)
    for k in range(ranks):
        cols = pl.ds(pl.multiple_of((place ^ k) * width, 128), width)
        normed_cot[:, cols] = sum(
            dot_nn(low[:, pl.ds(j * part, part)], mats[k][pl.ds(j * step, part), :])
            for low, mats in ((low_own, own), (low_other, other))
            for j in range(slices)
        )
    x = tokens[...].astype(jnp.float32)
    scale = lax.rsqrt(jnp.mean(x * x, axis=-1, keepdims=True) + NORM_EPS)
    n = x * scale
    cot = normed_cot[...]
    gain_grad[...] = jnp.sum(cot * n, axis=0, keepdims=True)
    scaled = cot * gain[...]
    back = scale * (scaled - n * jnp.mean(scaled * n, axis=-1, keepdims=True))
    input_grad[...] = bf16(middle_cot[...] + back)


def call(kernel, args, outs, scratch, flops):
    vmem = pl.BlockSpec(memory_space=pltpu.VMEM)
    moved = sum(math.prod(a.shape) * a.dtype.itemsize for a in args)
    moved += sum(math.prod(a.shape) * a.dtype.itemsize for a in outs)
    return pl.pallas_call(
        kernel,
        out_shape=tuple(outs),
        in_specs=[pl.BlockSpec(memory_space=pltpu.SMEM)] + [vmem] * (len(args) - 1),
        out_specs=(vmem,) * len(outs),
        scratch_shapes=scratch,
        compiler_params=pltpu.CompilerParams(vmem_limit_bytes=VMEM_LIMIT),
        cost_estimate=pl.CostEstimate(flops=flops, bytes_accessed=moved, transcendentals=0),
    )(*args)


def f32_like(*shape):
    return jax.ShapeDtypeStruct(shape, jnp.float32)


def bf16_like(*shape):
    return jax.ShapeDtypeStruct(shape, jnp.bfloat16)


def fetch(source, target, sem):
    copy = pltpu.make_async_copy(source, target, sem)
    copy.start()
    return copy


def unit_blocks(units):
    return [(s, min(UNIT_TILE, units - s)) for s in range(0, units, UNIT_TILE)]


def transpose_tokens(source, target, tokens):
    @pl.loop(0, tokens // TURN_TILE)
    def _(t):
        at = pl.multiple_of(t * TURN_TILE, TURN_TILE)
        target[:, pl.ds(at, TURN_TILE)] = source[pl.ds(at, TURN_TILE), :].T


def load_chunk(units, ranks, refs, na, oc, w, d, sem, back=None, mixed=None):
    rows = refs["na"][0].shape[0]
    slot = 0
    first = []
    later = []

    def begin(source, target, into):
        nonlocal slot
        into.append(fetch(source, target, sem.at[slot]))
        slot += 1

    for k in range(ranks):
        begin(refs["na"][k], na.at[pl.ds(k * rows, rows)], first)
    for b, (s, n) in enumerate(unit_blocks(units)):
        for half in range(2):
            at = pl.ds(half * units + s, n)
            begin(refs["w"].at[at], w.at[at], later if b else first)
        if b == 0:
            for k in range(ranks):
                begin(refs["oc"][k], oc.at[pl.ds(k * rows, rows)], first)
            begin(refs["d"], d, first)
            if back is not None:
                begin(refs["back"], back, first)
                begin(refs["mixed"], mixed, first)
    for copy in first:
        copy.wait()
    return later


def unit_block(units, s, n, tokens, na, oc, w, d, back, mixed, gt, ut, ht, at_row, add, final):
    wg = w.at[pl.ds(s, n)]
    wu = w.at[pl.ds(units + s, n)]
    db = d.at[:, pl.ds(s, n)]

    @pl.loop(0, tokens // TOKEN_TILE)
    def _(t):
        at = pl.ds(pl.multiple_of(t * TOKEN_TILE, TOKEN_TILE), TOKEN_TILE)
        gate = dot_nt(na[at, :], wg[...])
        up = dot_nt(na[at, :], wu[...])
        hidden_cot = dot_nn(oc[at, :], db[...])
        sigmoid = 1.0 / (1.0 + jnp.exp(-gate))
        activated = gate * sigmoid
        hidden = bf16(activated * up)
        gate_cot = bf16(hidden_cot * up * sigmoid * (1.0 + gate * (1.0 - sigmoid)))
        up_cot = bf16(hidden_cot * activated)
        ht[pl.ds(at_row, n), at] = hidden.T
        gt[pl.ds(at_row, n), at] = gate_cot.T
        ut[pl.ds(at_row, n), at] = up_cot.T
        back_term = dot_nn(gate_cot, wg[...]) + dot_nn(up_cot, wu[...])
        mixed_term = dot_nt(hidden, db[...])
        if add:
            back_term = back_term + back[at, :]
            mixed_term = mixed_term + mixed[at, :]
        if final:
            na[at, :] = bf16(back_term)
            oc[at, :] = bf16(mixed_term)
        else:
            back[at, :] = back_term
            mixed[at, :] = mixed_term


def gradient_block(units, s, n, na, oc_t, gt, ut, ht, at_row, dw, dd):
    at = pl.ds(at_row, n)

    @pl.loop(0, D // GRAD_TILE)
    def _(j):
        cols = pl.ds(pl.multiple_of(j * GRAD_TILE, GRAD_TILE), GRAD_TILE)
        dw[pl.ds(s, n), cols] = bf16(dot_nn(gt[at, :], na[:, cols]))
        dw[pl.ds(units + s, n), cols] = bf16(dot_nn(ut[at, :], na[:, cols]))
        dd[cols, pl.ds(s, n)] = bf16(dot_nt(oc_t[cols, :], ht[at, :]))


def first_chunk_kernel(units, ranks, *refs):
    ins = {"na": refs[:ranks], "oc": refs[ranks : 2 * ranks]}
    refs = refs[2 * ranks :]
    ins["w"], ins["d"] = refs[:2]
    back_out, mixed_out, dw_out, dd_out = refs[2:6]
    na, oc, oc_t, w, d, dw, dd, back, mixed, gt, ut, ht, in_sem, out_sem = refs[6:]
    tokens = na.shape[0]
    later = load_chunk(units, ranks, ins, na, oc, w, d, in_sem)
    transpose_tokens(oc, oc_t, tokens)
    blocks = unit_blocks(units)
    outs = []
    for b, (s, n) in enumerate(blocks):
        if b:
            later[2 * b - 2].wait()
            later[2 * b - 1].wait()
        unit_block(
            units, s, n, tokens, na, oc, w, d, back, mixed, gt, ut, ht, 0, bool(b), False
        )
        if b == len(blocks) - 1:
            outs.append(fetch(back, back_out, out_sem.at[0]))
            outs.append(fetch(mixed, mixed_out, out_sem.at[1]))
        gradient_block(units, s, n, na, oc_t, gt, ut, ht, 0, dw, dd)
        for half in range(2):
            at = pl.ds(half * units + s, n)
            outs.append(fetch(dw.at[at], dw_out.at[at], out_sem.at[3 + 2 * b + half]))
    outs.append(fetch(dd, dd_out, out_sem.at[2]))
    for copy in outs:
        copy.wait()


def last_chunk_kernel(units, ranks, carried, *refs):
    ins = {"na": refs[:ranks], "oc": refs[ranks : 2 * ranks]}
    refs = refs[2 * ranks :]
    ins["w"], ins["d"] = refs[:2]
    refs = refs[2:]
    if carried:
        ins["back"], ins["mixed"] = refs[:2]
        refs = refs[2:]
    back_out = refs[:ranks]
    mixed_out = refs[ranks : 2 * ranks]
    gt_out, ut_out, ht_out = refs[2 * ranks : 2 * ranks + 3]
    na, oc, w, d, back, mixed, gt, ut, ht, in_sem, out_sem = refs[2 * ranks + 3 :]
    tokens = na.shape[0]
    rows = tokens // ranks
    if carried:
        later = load_chunk(units, ranks, ins, na, oc, w, d, in_sem, back, mixed)
    else:
        later = load_chunk(units, ranks, ins, na, oc, w, d, in_sem)
    blocks = unit_blocks(units)
    outs = []
    for b, (s, n) in enumerate(blocks):
        if b:
            later[2 * b - 2].wait()
            later[2 * b - 1].wait()
        unit_block(
            units,
            s,
            n,
            tokens,
            na,
            oc,
            w,
            d,
            back,
            mixed,
            gt,
            ut,
            ht,
            s,
            carried or bool(b),
            b == len(blocks) - 1,
        )
        for i, (kept, target) in enumerate(((gt, gt_out), (ut, ut_out), (ht, ht_out))):
            at = pl.ds(s, n)
            outs.append(fetch(kept.at[at], target.at[at], out_sem.at[2 * ranks + 3 * b + i]))
    for k in range(ranks):
        at = pl.ds(k * rows, rows)
        outs.append(fetch(na.at[at], back_out[k], out_sem.at[k]))
        outs.append(fetch(oc.at[at], mixed_out[k], out_sem.at[ranks + k]))
    for copy in outs:
        copy.wait()


def gradient_kernel(units, ranks, *refs):
    na_in = refs[:ranks]
    oc_in = refs[ranks : 2 * ranks]
    gt_in, ut_in, ht_in, dw_out, dd_out = refs[2 * ranks : 2 * ranks + 5]
    na, oc, oc_t, gt, ut, ht, dw, dd, in_sem, out_sem = refs[2 * ranks + 5 :]
    tokens = na.shape[0]
    rows = tokens // ranks
    copies = []
    for k in range(ranks):
        at = pl.ds(k * rows, rows)
        copies.append(fetch(oc_in[k], oc.at[at], in_sem.at[k]))
    for k in range(ranks):
        at = pl.ds(k * rows, rows)
        copies.append(fetch(na_in[k], na.at[at], in_sem.at[ranks + k]))
    for i, (source, kept) in enumerate(((gt_in, gt), (ut_in, ut), (ht_in, ht))):
        copies.append(fetch(source, kept, in_sem.at[2 * ranks + i]))
    for copy in copies[:ranks]:
        copy.wait()
    transpose_tokens(oc, oc_t, tokens)
    for copy in copies[ranks:]:
        copy.wait()
    outs = []
    for b, (s, n) in enumerate(unit_blocks(units)):
        gradient_block(units, s, n, na, oc_t, gt, ut, ht, s, dw, dd)
        for half in range(2):
            at = pl.ds(half * units + s, n)
            outs.append(fetch(dw.at[at], dw_out.at[at], out_sem.at[1 + 2 * b + half]))
    outs.append(fetch(dd, dd_out, out_sem.at[0]))
    for copy in outs:
        copy.wait()


def hbm_call(kernel, args, outs, scratch, flops):
    moved = sum(math.prod(a.shape) * a.dtype.itemsize for a in args)
    moved += sum(math.prod(a.shape) * a.dtype.itemsize for a in outs)
    anywhere = pl.BlockSpec(memory_space=pl.ANY)
    return pl.pallas_call(
        kernel,
        out_shape=tuple(outs),
        in_specs=[anywhere] * len(args),
        out_specs=(anywhere,) * len(outs),
        scratch_shapes=scratch,
        compiler_params=pltpu.CompilerParams(vmem_limit_bytes=VMEM_LIMIT),
        cost_estimate=pl.CostEstimate(flops=flops, bytes_accessed=moved, transcendentals=0),
    )(*args)


def vmem_bf16(*shape):
    return pltpu.VMEM(shape, jnp.bfloat16)


def vmem_f32(*shape):
    return pltpu.VMEM(shape, jnp.float32)


def first_chunk(na, oc, w, d):
    ranks = len(na)
    tokens = ranks * na[0].shape[0]
    units = d.shape[1]
    blocks = len(unit_blocks(units))
    scratch = [
        vmem_bf16(tokens, D),
        vmem_bf16(tokens, D),
        vmem_bf16(D, tokens),
        vmem_bf16(2 * units, D),
        vmem_bf16(D, units),
        vmem_bf16(2 * units, D),
        vmem_bf16(D, units),
        vmem_f32(tokens, D),
        vmem_f32(tokens, D),
        vmem_bf16(UNIT_TILE, tokens),
        vmem_bf16(UNIT_TILE, tokens),
        vmem_bf16(UNIT_TILE, tokens),
        pltpu.SemaphoreType.DMA((2 * ranks + 1 + 2 * blocks,)),
        pltpu.SemaphoreType.DMA((3 + 2 * blocks,)),
    ]
    outs = [
        f32_like(tokens, D),
        f32_like(tokens, D),
        bf16_like(2 * units, D),
        bf16_like(D, units),
    ]
    kernel = functools.partial(first_chunk_kernel, units, ranks)
    return hbm_call(kernel, [*na, *oc, w, d], outs, scratch, 18 * tokens * D * units)


def last_chunk(na, oc, w, d, carry):
    ranks = len(na)
    rows = na[0].shape[0]
    tokens = ranks * rows
    units = d.shape[1]
    blocks = len(unit_blocks(units))
    scratch = [
        vmem_bf16(tokens, D),
        vmem_bf16(tokens, D),
        vmem_bf16(2 * units, D),
        vmem_bf16(D, units),
        vmem_f32(tokens, D),
        vmem_f32(tokens, D),
        vmem_bf16(units, tokens),
        vmem_bf16(units, tokens),
        vmem_bf16(units, tokens),
        pltpu.SemaphoreType.DMA((2 * ranks + 3 + 2 * blocks,)),
        pltpu.SemaphoreType.DMA((2 * ranks + 3 * blocks,)),
    ]
    outs = [bf16_like(rows, D)] * (2 * ranks) + [bf16_like(units, tokens)] * 3
    kernel = functools.partial(last_chunk_kernel, units, ranks, bool(carry))
    got = hbm_call(kernel, [*na, *oc, w, d, *carry], outs, scratch, 12 * tokens * D * units)
    return got[:ranks], got[ranks : 2 * ranks], got[2 * ranks :]


def chunk_gradients(na, oc, kept):
    ranks = len(na)
    tokens = ranks * na[0].shape[0]
    units = kept[0].shape[0]
    blocks = len(unit_blocks(units))
    scratch = [
        vmem_bf16(tokens, D),
        vmem_bf16(tokens, D),
        vmem_bf16(D, tokens),
        vmem_bf16(units, tokens),
        vmem_bf16(units, tokens),
        vmem_bf16(units, tokens),
        vmem_bf16(2 * units, D),
        vmem_bf16(D, units),
        pltpu.SemaphoreType.DMA((2 * ranks + 3,)),
        pltpu.SemaphoreType.DMA((1 + 2 * blocks,)),
    ]
    outs = [bf16_like(2 * units, D), bf16_like(D, units)]
    kernel = functools.partial(gradient_kernel, units, ranks)
    return hbm_call(kernel, [*na, *oc, *kept], outs, scratch, 6 * tokens * D * units)


def sharded_pass(tokens, cotangent, lengths, half_qkv, half_out, half_in, half_down, half_small):
    ranks = lax.axis_size("dp")
    lines = lax.axis_size("fsdp")
    place = lax.axis_index("dp")
    rows = tokens.shape[1]
    slices = lines // 2
    block = D // ranks
    inputs = tokens[0]
    info = jnp.stack([place, lax.rem(lax.axis_index("fsdp"), 2), lengths[0]])

    small_rows, small_columns = half_small.shape
    small_size = small_rows * small_columns
    columns = half_qkv.shape[1]
    small_part = jnp.pad(half_small.reshape(1, small_size), ((0, 15), (0, block - small_size)))
    qkv_along = gather_line(jnp.concatenate([half_qkv.T, small_part]))
    exchange = exchange_weights(half_in, half_down)
    sent = next(exchange)
    sent, qkv_along = lax.optimization_barrier((sent, qkv_along))
    got = dp_exchange(sent)
    qkv_own, qkv_other = gather_rest(qkv_along)
    half_out, qkv_own[1] = lax.optimization_barrier((half_out, qkv_own[1]))
    out_along = gather_line(half_out.T)
    out_along, qkv_own[ranks - 1] = lax.optimization_barrier((out_along, qkv_own[ranks - 1]))
    out_own, out_other = gather_rest(out_along)

    small_pairs = []
    for mine, theirs in zip(qkv_own, qkv_other):
        mine, theirs = (
            part.reshape(slices, columns + 16, block)[:, columns, :small_size]
            for part in (mine, theirs)
        )
        even = jnp.where(is_even(), mine, theirs)
        odd = jnp.where(is_even(), theirs, mine)
        small_pairs.append(jnp.stack([even, odd], axis=1))
    small_stack = jnp.stack(small_pairs)
    small_vec = jnp.stack(
        [
            lax.dynamic_index_in_dim(small_stack, place ^ a, 0, keepdims=False)
            for a in range(ranks)
        ]
    )
    small_vec = small_vec.reshape(ranks, lines, small_rows, small_columns)
    small_vec = small_vec.transpose(0, 2, 1, 3).reshape(-1).astype(jnp.float32)
    gain_attn, gain_mlp, biases = unpack_small(small_vec)
    gain_attn = gain_attn[None]
    gain_mlp = gain_mlp[None]

    in_piece, down_piece = exchange.send(got)
    in_chunks = []
    down_chunks = []
    start = 0
    for size in CHUNKS:
        width = size // slices
        down_chunks.append(
            lax.all_gather(
                down_piece[:, :, start : start + width].reshape(-1, size),
                "fsdp",
                axis=0,
                tiled=True,
            )
        )
        in_chunks.append(
            lax.all_gather(in_piece[start : start + width], "fsdp", axis=0, tiled=True)
        )
        start += width

    query_places = place * rows + jnp.arange(rows, dtype=jnp.int32)
    cosine, sine = rope_tables(query_places.astype(jnp.float32))
    sine = jnp.where(jnp.arange(HEAD) < HEAD // 2, -sine, sine)
    normed, queries, kv = call(
        functools.partial(project_kernel, ranks, slices),
        [info, inputs, gain_attn, biases[None], cosine, sine, *qkv_own, *qkv_other],
        [bf16_like(rows, D), bf16_like(rows, D), bf16_like(rows, 2 * KV_WIDTH)],
        [vmem_f32(rows, QKV)],
        2 * rows * D * QKV,
    )
    kv_blocks = dp_gather(kv)

    valid = query_places < lengths[0]
    out_cot = jnp.where(valid[:, None], cotangent[0], jnp.zeros_like(cotangent[0]))
    out_cot, *kv_blocks = lax.optimization_barrier((out_cot, *kv_blocks))
    cot_blocks = dp_gather(out_cot)

    attended, totals, middle, normed_again = call(
        functools.partial(attend_kernel, ranks, slices),
        [info, inputs, gain_mlp, queries, *kv_blocks, *out_own, *out_other],
        [bf16_like(rows, D), f32_like(16, rows), f32_like(rows, D), bf16_like(rows, D)],
        [
            vmem_f32(ranks * rows, rows),
            vmem_bf16(ranks * rows, KV_WIDTH),
            vmem_bf16(ranks * rows, KV_WIDTH),
            vmem_bf16(KV_WIDTH, ranks * rows),
        ],
        2 * rows * D * D + 4 * rows * D * ranks * rows,
    )
    normed_blocks = dp_gather(normed_again)

    carry = ()
    in_terms = []
    down_terms = []
    for index, size in enumerate(CHUNKS):
        in_mat = in_chunks[index]
        down_mat = down_chunks[index]
        if index < len(CHUNKS) - 1:
            back, mixed, in_term, down_term = first_chunk(
                normed_blocks, cot_blocks, in_mat, down_mat
            )
            carry = (back, mixed)
        else:
            back_blocks, mixed_blocks, kept = last_chunk(
                normed_blocks, cot_blocks, in_mat, down_mat, carry
            )
            back_got = [dp_send(back_blocks[k], k) for k in range(1, ranks)]
            in_term, down_term = chunk_gradients(normed_blocks, cot_blocks, kept)
        in_terms.append(in_term)
        down_terms.append(down_term)
    in_terms[-1], down_terms[-1], back_blocks, back_got, mixed_blocks = lax.optimization_barrier(
        (in_terms[-1], down_terms[-1], back_blocks, back_got, mixed_blocks)
    )
    mixed = middle + mixed_blocks[0].astype(jnp.float32)
    for k in range(1, ranks):
        mixed = mixed + dp_send(mixed_blocks[k], k).astype(jnp.float32)
    in_parts = []
    down_parts = []
    for in_term, down_term, size in zip(in_terms, down_terms, CHUNKS):
        down_sum = lax.psum_scatter(down_term, "fsdp", scatter_dimension=0, tiled=True)
        in_sum = lax.psum_scatter(in_term, "fsdp", scatter_dimension=0, tiled=True)
        down_sum = down_sum.reshape(-1, slices, size // slices)
        in_part, down_part = exchange_gradients(in_sum, down_sum, half_down.shape[1])
        in_parts.append(in_part)
        down_parts.append(down_part)
    in_grad = jnp.concatenate(in_parts, axis=1)
    in_grad = in_grad.transpose(2, 0, 1).reshape(half_in.shape).astype(jnp.float32)
    down_grad = jnp.concatenate(down_parts, axis=1)
    down_grad = down_grad.transpose(2, 0, 1, 3).reshape(half_down.shape).astype(jnp.float32)

    middle_cot, middle_low, gain_mlp_grad, query_cot, *kv_cot = call(
        functools.partial(attend_back_kernel, ranks, slices),
        [
            info,
            middle,
            out_cot,
            gain_mlp,
            queries,
            totals,
            back_blocks[0],
            *back_got,
            *kv_blocks,
            *out_own,
            *out_other,
        ],
        [f32_like(rows, D), bf16_like(rows, D), f32_like(1, D), f32_like(rows, D)]
        + [bf16_like(rows, 2 * KV_WIDTH)] * ranks,
        [
            vmem_f32(ranks * rows, rows),
            vmem_bf16(ranks * rows, KV_WIDTH),
            vmem_bf16(ranks * rows, KV_WIDTH),
            vmem_bf16(KV_WIDTH, ranks * rows),
            vmem_bf16(rows, D),
            vmem_f32(ranks * rows, KV_WIDTH),
            vmem_f32(ranks * rows, KV_WIDTH),
            vmem_bf16(rows, D // 2),
            vmem_bf16(rows, D // 2),
        ],
        2 * rows * D * D + 10 * rows * D * ranks * rows,
    )
    kv_got = [dp_send(kv_cot[k], k) for k in range(1, ranks)]

    def outer(left, right):
        columns = right.shape[1]
        terms = call(
            functools.partial(outer_kernel, ranks, slices),
            [info, left, right],
            [bf16_like(columns // 2, block)] * (2 * ranks),
            [vmem_bf16(columns, rows)],
            2 * rows * D * columns,
        )
        return reduce_matrix(terms[:ranks], terms[ranks:])

    out_grad = outer(attended, middle_low)
    projected_low, bias_grad = call(
        functools.partial(project_back_kernel, ranks),
        [info, query_cot, cosine, sine, kv_cot[0], *kv_got],
        [bf16_like(rows, QKV), f32_like(1, QKV)],
        [],
        0,
    )
    qkv_grad = outer(normed, projected_low)
    input_grad, gain_attn_grad = call(
        functools.partial(input_back_kernel, ranks, slices),
        [info, projected_low, inputs, gain_attn, middle_cot, *qkv_own, *qkv_other],
        [bf16_like(rows, D), f32_like(1, D)],
        [vmem_bf16(rows, QKV // 2), vmem_bf16(rows, QKV // 2), vmem_f32(rows, D)],
        2 * rows * D * QKV,
    )
    small_term = group_small(gain_attn_grad[0], gain_mlp_grad[0], bias_grad[0])
    small_sum = sum_everywhere(small_term)
    small_grad = lax.dynamic_slice(
        small_sum,
        (place * small_rows, lax.axis_index("fsdp") * small_columns),
        (small_rows, small_columns),
    )
    return (bf16(mixed), input_grad, qkv_grad, out_grad, in_grad, down_grad, small_sum, small_grad)


def per_device(
    tokens,
    cotangent,
    lengths,
    qkv_weight,
    qkv_first,
    qkv_second,
    out_weight,
    out_first,
    out_second,
    mlp_in_weight,
    mlp_in_first,
    mlp_in_second,
    down_weight,
    down_first,
    down_second,
    small_params,
    small_first,
    small_second,
):
    results = sharded_pass(
        tokens,
        cotangent,
        lengths,
        bf16(qkv_weight),
        bf16(out_weight),
        bf16(mlp_in_weight),
        bf16(down_weight),
        bf16(small_params),
    )
    mixed, input_cot, qkv_grad, out_grad, in_grad, down_grad, small_sum, small_grad = results
    local_squares = sum(
        (jnp.sum(piece * piece) for piece in (qkv_grad, out_grad, in_grad, down_grad))
    )
    total_squares = sum_everywhere(local_squares) + jnp.sum(small_sum * small_sum)
    grad_norm = jnp.sqrt(total_squares)
    clip_factor = CLIP_NORM / jnp.maximum(grad_norm, CLIP_NORM)
    outs = [mixed[None], input_cot[None], grad_norm]
    for weight, first, second, gradient, rate, decay in (
        (qkv_weight, qkv_first, qkv_second, qkv_grad, MATRIX_RATE, MATRIX_DECAY),
        (out_weight, out_first, out_second, out_grad, MATRIX_RATE, MATRIX_DECAY),
        (mlp_in_weight, mlp_in_first, mlp_in_second, in_grad, MATRIX_RATE, MATRIX_DECAY),
        (down_weight, down_first, down_second, down_grad, MATRIX_RATE, MATRIX_DECAY),
        (small_params, small_first, small_second, small_grad, SMALL_RATE, 0.0),
    ):
        outs.extend(update(weight, first, second, gradient, clip_factor, rate, decay))
    return tuple(outs)


def solution(mesh):
    rows = P("fsdp", "dp", None)
    shard = P("dp", "fsdp")
    return jax.shard_map(
        per_device,
        mesh=mesh,
        in_specs=(rows, rows, P("fsdp")) + (shard,) * 15,
        out_specs=(rows, rows, P()) + (shard,) * 20,
        check_vma=False,
    )
```

```python
import functools
import math

import jax
import jax.numpy as jnp
from jax import lax
from jax.experimental import pallas as pl
from jax.experimental.pallas import tpu as pltpu
from jax.sharding import PartitionSpec as P

D = 1536
HEADS = 12
KV_HEADS = 2
HEAD = 128
FF = 8960
STEP = 5
GROUP = 6
SMALL = 5120
QKV = 2048
KV_WIDTH = KV_HEADS * HEAD


NORM_EPS = 1e-06
ROPE_BASE = 1000000.0
BETA_FIRST = 0.5
BETA_SECOND = 0.5
ADAM_EPS = 1e-08
MATRIX_RATE = 0.03
SMALL_RATE = 0.3
MATRIX_DECAY = 0.1
CLIP_NORM = 1.0
MASKED = -1e30
SCALE = HEAD ** (-0.5)
CHUNKS = (1536, 704)
UNIT_TILE = 512
TOKEN_TILE = 640
GRAD_TILE = 512
TURN_TILE = 256
VMEM_LIMIT = 60 * 2**20
FLOPS_PER_MICRO = 1_150_000_000


def unpack_small(small_vec):
    grouped = small_vec.reshape(KV_HEADS * HEAD, 3 * GROUP + 2)
    gain_attn = grouped[:, :GROUP].reshape(-1)
    gain_mlp = grouped[:, GROUP : 2 * GROUP].reshape(-1)
    biases = jnp.concatenate(
        [
            grouped[:, 2 * GROUP : 3 * GROUP].reshape(-1),
            grouped[:, 3 * GROUP],
            grouped[:, 3 * GROUP + 1],
        ]
    )
    return (gain_attn, gain_mlp, biases)


def group_small(gain_attn, gain_mlp, biases):
    count = KV_HEADS * HEAD
    pieces = [
        gain_attn.reshape(count, GROUP),
        gain_mlp.reshape(count, GROUP),
        biases[:D].reshape(count, GROUP),
        biases[D : D + count][:, None],
        biases[D + count :][:, None],
    ]
    return jnp.concatenate(pieces, axis=1).reshape(8, SMALL // 8)


def rope_tables(positions):
    pair_index = jnp.arange(HEAD // 2, dtype=jnp.float32)
    inverse = jnp.power(jnp.float32(ROPE_BASE), -2.0 * pair_index / HEAD)
    angles = positions[:, None] * inverse[None, :]
    angles = jnp.concatenate([angles, angles], axis=-1)
    return (jnp.cos(angles), jnp.sin(angles))


def bf16(array):
    return array.astype(jnp.bfloat16)


def scoped(name, function, *args):
    with jax.named_scope(name):
        return function(*args)


def dot_nn(left, right):
    return jnp.dot(left, right, preferred_element_type=jnp.float32)


def dot_nt(left, right):
    return lax.dot_general(
        left, right, (((1,), (1,)), ((), ())), preferred_element_type=jnp.float32
    )


def dot_tn(left, right):
    return lax.dot_general(
        left, right, (((0,), (0,)), ((), ())), preferred_element_type=jnp.float32
    )


def update(weight, first, second, gradient, clip_factor, rate, decay):
    step_grad = gradient * clip_factor
    first_new = BETA_FIRST * first + (1.0 - BETA_FIRST) * step_grad
    second_new = BETA_SECOND * second + (1.0 - BETA_SECOND) * step_grad * step_grad
    first_fix = 1.0 - BETA_FIRST**STEP
    second_fix = 1.0 - BETA_SECOND**STEP
    weight_new = weight - rate * (
        first_new / first_fix / (jnp.sqrt(second_new / second_fix) + ADAM_EPS) + decay * weight
    )
    return (weight_new, first_new, second_new, weight_new.astype(jnp.bfloat16))


def dp_send(block, k):
    count = lax.axis_size("dp")
    return lax.ppermute(block, "dp", [(i, i ^ k) for i in range(count)])


def core_swap(block):
    count = lax.axis_size("fsdp")
    return lax.ppermute(block, "fsdp", [(i, i ^ 1) for i in range(count)])


def gather_near(block):
    return [block, dp_send(block, 1), dp_send(block, 2)]


def gather_far(near):
    _, one, two = near
    half = one.shape[0] // 2
    return [*near, jnp.concatenate([dp_send(one[:half], 2), dp_send(two[half:], 1)])]


def dp_gather(block):
    return gather_far(gather_near(block))


def dp_own(array, k):
    return lax.dynamic_index_in_dim(array, lax.axis_index("dp") ^ k, 0, keepdims=False)


def dp_exchange(array):
    count = lax.axis_size("dp")
    place = lax.axis_index("dp")
    got = jnp.stack([dp_own(array, 0)] + [dp_send(dp_own(array, k), k) for k in range(1, count)])
    return jnp.stack(
        [lax.dynamic_index_in_dim(got, place ^ a, 0, keepdims=False) for a in range(count)]
    )


def line_send(block, r):
    count = lax.axis_size("fsdp")
    return lax.ppermute(block, "fsdp", [(i, i ^ (2 * r)) for i in range(count)])


def line_gather(block):
    count = lax.axis_size("fsdp") // 2
    place = lax.axis_index("fsdp") // 2
    got = jnp.stack([block] + [line_send(block, r) for r in range(1, count)])
    return jnp.stack(
        [lax.dynamic_index_in_dim(got, place ^ a, 0, keepdims=False) for a in range(count)]
    )


def sum_of_squares(array):
    array = array.astype(jnp.float32)
    return jnp.sum(array * array)


def sum_over_core(term):
    return term + core_swap(term)


def sum_over_line(term):
    return term + sum(line_send(term, r) for r in range(1, lax.axis_size("fsdp") // 2))


def sum_over_dp(term):
    return term + sum(dp_send(term, k) for k in range(1, lax.axis_size("dp")))


def sum_everywhere(term):
    return sum_over_dp(sum_over_line(sum_over_core(term)))


def is_even():
    return lax.rem(lax.axis_index("fsdp"), 2) == 0


def sum_blocks(own, got):
    return [own[k].astype(jnp.float32) + got[k].astype(jnp.float32) for k in range(own.shape[0])]


def reduce_over_dp(summed):
    return [summed[0]] + [dp_send(bf16(summed[k]), k) for k in range(1, len(summed))]


def reduce_over_line(got):
    total = sum(block.astype(jnp.float32) for block in got)
    count = lax.axis_size("fsdp") // 2
    place = lax.axis_index("fsdp") // 2
    parts = total.reshape(count, -1, total.shape[1])
    shard = [lax.dynamic_index_in_dim(parts, place, 0, keepdims=False)]
    for r in range(1, count):
        part = lax.dynamic_index_in_dim(parts, place ^ r, 0, keepdims=False)
        shard.append(line_send(bf16(part), r))
    return shard


def total_shard(shard):
    return sum(block.astype(jnp.float32) for block in shard).T


def exchange_weights(half_in, half_down):
    ranks = lax.axis_size("dp")
    rows, columns = half_in.shape
    part = columns // ranks
    width = half_down.shape[1]
    slices = half_down.shape[0] // (ranks * part)
    in_sent = half_in.reshape(rows, ranks, part).transpose(1, 2, 0)
    down_sent = half_down.reshape(slices, ranks, part, width).transpose(1, 2, 0, 3)
    sent = jnp.concatenate([in_sent, down_sent.reshape(ranks, part, slices * width)], axis=2)
    got = yield sent
    in_piece = got[:, :, :rows].transpose(1, 0, 2).reshape(part, ranks * rows)
    down_piece = got[:, :, rows:].reshape(ranks, part, slices, width).transpose(3, 0, 2, 1)
    yield in_piece, down_piece.reshape(width, ranks * slices, part)


def pack_gradients(in_grad, down_grad):
    ranks = lax.axis_size("dp")
    part = in_grad.shape[0]
    columns = down_grad.shape[0]
    rows = in_grad.shape[1] // ranks
    slices = down_grad.shape[1] // ranks
    in_sent = in_grad.reshape(part, ranks, rows).transpose(1, 0, 2)
    down_sent = down_grad.reshape(columns, ranks, slices, part).transpose(1, 3, 2, 0)
    return jnp.concatenate([in_sent, down_sent.reshape(ranks, part, slices * columns)], axis=2)


def unpack_gradients(got, rows, columns):
    ranks, part, width = got.shape
    return got[:, :, :rows], got[:, :, rows:].reshape(ranks, part, -1, columns)


def column_slices(own, other, first, target, width, slices):
    for j in range(slices):
        mine = own(j)
        theirs = other(j)
        target[:, pl.ds(2 * j * width, width)] = jnp.where(first, mine, theirs)
        target[:, pl.ds((2 * j + 1) * width, width)] = jnp.where(first, theirs, mine)


def block_columns(ref, place, k, width):
    return ref[:, pl.ds(pl.multiple_of((place ^ k) * width, 128), width)]


def project_kernel(ranks, slices, *refs):
    info, tokens, gain, bias, cosine, sine = refs[:6]
    own = refs[6 : 6 + ranks]
    other = refs[6 + ranks : 6 + 2 * ranks]
    normed, queries, kv, proj = refs[6 + 2 * ranks :]
    place = info[0]
    first = info[1] == 0
    width = own[0].shape[1]
    step = own[0].shape[0] // slices
    part = QKV // (2 * slices)
    x = tokens[...].astype(jnp.float32)
    scale = lax.rsqrt(jnp.mean(x * x, axis=-1, keepdims=True) + NORM_EPS)
    normed[...] = bf16(x * scale * gain[...])

    def product(mats, j):
        return sum(
            dot_nt(block_columns(normed, place, k, width), mats[k][pl.ds(j * step, part), :])
            for k in range(ranks)
        )

    column_slices(
        lambda j: product(own, j), lambda j: product(other, j), first, proj, part, slices
    )
    for h in range(HEADS + KV_HEADS):
        cols = pl.ds(h * HEAD, HEAD)
        u = proj[:, cols] + bias[:, cols]
        turned = bf16(u * cosine[...] + pltpu.roll(u, HEAD // 2, 1) * sine[...])
        if h < HEADS:
            queries[:, cols] = turned
        else:
            kv[:, pl.ds((h - HEADS) * HEAD, HEAD)] = turned
    cols = pl.ds(D + KV_WIDTH, KV_WIDTH)
    kv[:, pl.ds(KV_WIDTH, KV_WIDTH)] = bf16(proj[:, cols] + bias[:, cols])


def score_bias(info, rows, ranks, target):
    place = info[0]
    length = info[2]
    query = place * rows + lax.broadcasted_iota(jnp.int32, (rows, rows), 1)
    for k in range(ranks):
        key = (place ^ k) * rows + lax.broadcasted_iota(jnp.int32, (rows, rows), 0)
        seen = (key <= query) & (key < length)
        target[pl.ds(k * rows, rows), :] = jnp.where(seen, 0.0, MASKED)


def attend_kernel(ranks, slices, *refs):
    info, tokens, gain, queries = refs[:4]
    kv = refs[4 : 4 + ranks]
    own = refs[4 + ranks : 4 + 2 * ranks]
    other = [refs[4 + 2 * ranks].at[k] for k in range(ranks)]
    attended, totals, middle, normed_again, bias, keys, values, values_t = refs[5 + 2 * ranks :]
    place = info[0]
    first = info[1] == 0
    rows = tokens.shape[0]
    width = own[0].shape[1]
    part = own[0].shape[0] // slices
    score_bias(info, rows, ranks, bias)
    for k in range(ranks):
        keys[pl.ds(k * rows, rows), :] = kv[k][:, pl.ds(0, KV_WIDTH)]
        values[pl.ds(k * rows, rows), :] = kv[k][:, pl.ds(KV_WIDTH, KV_WIDTH)]
    values_t[...] = values[...].T

    @pl.loop(0, HEADS)
    def _(h):
        cols = pl.ds(pl.multiple_of(h * HEAD, HEAD), HEAD)
        kv_cols = pl.ds(pl.multiple_of((h // GROUP) * HEAD, HEAD), HEAD)
        scores = dot_nt(keys[:, kv_cols], queries[:, cols]) * SCALE + bias[...]
        peak = jnp.max(scores, axis=0, keepdims=True)
        exponent = jnp.exp(scores - peak)
        total = jnp.sum(exponent, axis=0, keepdims=True)
        totals[pl.ds(h, 1), :] = peak + jnp.log(total)
        probs = bf16(exponent * (1.0 / total))
        attended[:, cols] = bf16(dot_nn(values_t[kv_cols, :], probs).T)

    def product(mats, j):
        return sum(
            dot_nt(block_columns(attended, place, k, width), mats[k][pl.ds(j * part, part), :])
            for k in range(ranks)
        )

    column_slices(
        lambda j: product(own, j), lambda j: product(other, j), first, middle, part, slices
    )
    total = middle[...] + tokens[...].astype(jnp.float32)
    middle[...] = total
    scale = lax.rsqrt(jnp.mean(total * total, axis=-1, keepdims=True) + NORM_EPS)
    normed_again[...] = bf16(total * scale * gain[...])


def attend_back_kernel(ranks, slices, *refs):
    info, middle, cotangent, gain, queries, totals = refs[:6]
    got = refs[6 : 6 + ranks]
    kv = refs[6 + ranks : 6 + 2 * ranks]
    own = refs[6 + 2 * ranks : 6 + 3 * ranks]
    other = [refs[6 + 3 * ranks].at[k] for k in range(ranks)]
    refs = refs[7 + 3 * ranks :]
    middle_cot, middle_low, gain_grad, query_cot = refs[:4]
    kv_cot = refs[4 : 4 + ranks]
    bias, keys, values, keys_t, attended_cot, key_sum, value_sum, low_own, low_other = refs[
        4 + ranks :
    ]
    place = info[0]
    first = info[1] == 0
    rows = middle.shape[0]
    width = own[0].shape[1]
    part = own[0].shape[0] // slices
    position = place * rows + lax.broadcasted_iota(jnp.int32, (rows, 1), 0)
    valid = jnp.where(position < info[2], 1.0, 0.0)
    cot = got[0][...].astype(jnp.float32)
    for k in range(1, ranks):
        cot = cot + got[k][...].astype(jnp.float32)
    v = middle[...]
    scale = lax.rsqrt(jnp.mean(v * v, axis=-1, keepdims=True) + NORM_EPS)
    n = v * scale
    gain_grad[...] = jnp.sum(cot * n, axis=0, keepdims=True)
    scaled = cot * gain[...]
    back = scale * (scaled - n * jnp.mean(scaled * n, axis=-1, keepdims=True))
    back = back + cotangent[...].astype(jnp.float32) * valid
    middle_cot[...] = back
    middle_low[...] = bf16(back)
    for j in range(slices):
        even = middle_low[:, pl.ds(2 * j * part, part)]
        odd = middle_low[:, pl.ds((2 * j + 1) * part, part)]
        low_own[:, pl.ds(j * part, part)] = jnp.where(first, even, odd)
        low_other[:, pl.ds(j * part, part)] = jnp.where(first, odd, even)
    for k in range(ranks):
        cols = pl.ds(pl.multiple_of((place ^ k) * width, 128), width)
        attended_cot[:, cols] = bf16(
            dot_nn(low_own[...], own[k][...]) + dot_nn(low_other[...], other[k][...])
        )
    score_bias(info, rows, ranks, bias)
    for k in range(ranks):
        keys[pl.ds(k * rows, rows), :] = kv[k][:, pl.ds(0, KV_WIDTH)]
        values[pl.ds(k * rows, rows), :] = kv[k][:, pl.ds(KV_WIDTH, KV_WIDTH)]
    keys_t[...] = keys[...].T
    key_sum[...] = jnp.zeros_like(key_sum)
    value_sum[...] = jnp.zeros_like(value_sum)

    @pl.loop(0, HEADS)
    def _(h):
        cols = pl.ds(pl.multiple_of(h * HEAD, HEAD), HEAD)
        kv_cols = pl.ds(pl.multiple_of((h // GROUP) * HEAD, HEAD), HEAD)
        query = queries[:, cols]
        out_cot = attended_cot[:, cols]
        scores = dot_nt(keys[:, kv_cols], query) * SCALE + bias[...]
        probs = jnp.exp(scores - totals[pl.ds(h, 1), :])
        probs_cot = dot_nt(values[:, kv_cols], out_cot)
        row_dot = jnp.sum(probs * probs_cot, axis=0, keepdims=True)
        scores_cot = bf16(probs * (probs_cot - row_dot))
        value_sum[:, kv_cols] += dot_nn(bf16(probs), out_cot)
        key_sum[:, kv_cols] += dot_nn(scores_cot, query)
        query_cot[:, cols] = dot_nn(keys_t[kv_cols, :], scores_cot).T * SCALE

    for k in range(ranks):
        at = pl.ds(k * rows, rows)
        kv_cot[k][:, pl.ds(0, KV_WIDTH)] = bf16(key_sum[at, :] * SCALE)
        kv_cot[k][:, pl.ds(KV_WIDTH, KV_WIDTH)] = bf16(value_sum[at, :])


def outer_kernel(ranks, slices, *refs):
    info, left, right, own, other, turned = refs
    place = info[0]
    parity = info[1]
    width = own.shape[2]
    part = own.shape[1] // slices
    turned[...] = right[...].T
    for k in range(ranks):
        block = block_columns(left, place, k, width)
        for j in range(slices):
            at = pl.ds(j * part, part)
            mine = pl.ds(pl.multiple_of((2 * j + parity) * part, 16), part)
            theirs = pl.ds(pl.multiple_of((2 * j + 1 - parity) * part, 16), part)
            own[k, at, :] = bf16(dot_nn(turned[mine, :], block))
            other[k, at, :] = bf16(dot_nn(turned[theirs, :], block))


def project_back_kernel(ranks, *refs):
    info, query_cot, cosine, sine = refs[:4]
    got = refs[4 : 4 + ranks]
    projected_low, bias_grad = refs[4 + ranks :]
    kv_cot = got[0][...].astype(jnp.float32)
    for k in range(1, ranks):
        kv_cot = kv_cot + got[k][...].astype(jnp.float32)
    for h in range(HEADS + 2 * KV_HEADS):
        cols = pl.ds(h * HEAD, HEAD)
        if h < HEADS:
            u = query_cot[:, cols]
        else:
            u = kv_cot[:, (h - HEADS) * HEAD : (h - HEADS + 1) * HEAD]
        if h < HEADS + KV_HEADS:
            u = u * cosine[...] + pltpu.roll(u * sine[...], HEAD // 2, 1)
        bias_grad[:, cols] = jnp.sum(u, axis=0, keepdims=True)
        projected_low[:, cols] = bf16(u)


def input_back_kernel(ranks, slices, *refs):
    info, projected_low, tokens, gain, middle_cot = refs[:5]
    own = refs[5 : 5 + ranks]
    other = refs[5 + ranks : 5 + 2 * ranks]
    input_grad, gain_grad, low_own, low_other, normed_cot = refs[5 + 2 * ranks :]
    place = info[0]
    first = info[1] == 0
    width = own[0].shape[1]
    step = own[0].shape[0] // slices
    part = QKV // (2 * slices)
    for j in range(slices):
        even = projected_low[:, pl.ds(2 * j * part, part)]
        odd = projected_low[:, pl.ds((2 * j + 1) * part, part)]
        low_own[:, pl.ds(j * part, part)] = jnp.where(first, even, odd)
        low_other[:, pl.ds(j * part, part)] = jnp.where(first, odd, even)
    for k in range(ranks):
        cols = pl.ds(pl.multiple_of((place ^ k) * width, 128), width)
        normed_cot[:, cols] = sum(
            dot_nn(low[:, pl.ds(j * part, part)], mats[k][pl.ds(j * step, part), :])
            for low, mats in ((low_own, own), (low_other, other))
            for j in range(slices)
        )
    x = tokens[...].astype(jnp.float32)
    scale = lax.rsqrt(jnp.mean(x * x, axis=-1, keepdims=True) + NORM_EPS)
    n = x * scale
    cot = normed_cot[...]
    gain_grad[...] = jnp.sum(cot * n, axis=0, keepdims=True)
    scaled = cot * gain[...]
    back = scale * (scaled - n * jnp.mean(scaled * n, axis=-1, keepdims=True))
    input_grad[...] = bf16(middle_cot[...] + back)


def call(kernel, args, outs, scratch, micros):
    vmem = pl.BlockSpec(memory_space=pltpu.VMEM)
    moved = sum(math.prod(a.shape) * a.dtype.itemsize for a in args)
    moved += sum(math.prod(a.shape) * a.dtype.itemsize for a in outs)
    moved *= min(micros, 1)
    return pl.pallas_call(
        kernel,
        out_shape=tuple(outs),
        in_specs=[pl.BlockSpec(memory_space=pltpu.SMEM)] + [vmem] * (len(args) - 1),
        out_specs=(vmem,) * len(outs),
        scratch_shapes=scratch,
        compiler_params=pltpu.CompilerParams(vmem_limit_bytes=VMEM_LIMIT),
        cost_estimate=pl.CostEstimate(
            flops=micros * FLOPS_PER_MICRO, bytes_accessed=moved, transcendentals=0
        ),
    )(*args)


def f32_like(*shape):
    return jax.ShapeDtypeStruct(shape, jnp.float32)


def bf16_like(*shape):
    return jax.ShapeDtypeStruct(shape, jnp.bfloat16)


class Chunk:
    def __init__(self, size, lines):
        self.lines = lines
        self.slices = lines // 2
        self.real = size // self.slices
        self.deep = -(-self.real // 16) * 16
        self.units = self.slices * self.deep
        self.wide = -(-self.units // 128) * 128
        self.columns = D // lines
        self.folds = D // self.wide if self.columns * self.wide % (16 * D) == 0 else 1
        self.low = self.columns // self.folds
        self.step = self.deep + self.low
        self.rows = lines * self.step
        self.blocks = [
            (s, min(UNIT_TILE, self.units - s)) for s in range(0, self.units, UNIT_TILE)
        ]

    def pack(self, in_piece, down_piece):
        extra = self.deep - self.real
        in_piece = jnp.pad(in_piece, ((0, extra), (0, 0)))
        down_piece = jnp.pad(down_piece, ((0, 0), (0, 0), (0, extra)))
        down_piece = down_piece.reshape(self.columns, self.units)
        down_piece = jnp.pad(down_piece, ((0, 0), (0, self.wide - self.units)))
        parts = [down_piece[i * self.low : (i + 1) * self.low] for i in range(self.folds)]
        down_piece = jnp.concatenate(parts, axis=1)
        down_piece = jnp.pad(down_piece, ((0, 0), (0, D - down_piece.shape[1])))
        return jnp.concatenate([in_piece, down_piece])

    def unpack(self, shard):
        in_piece = shard[: self.real]
        down_piece = shard[self.deep :]
        parts = [
            down_piece[:, i * self.wide : i * self.wide + self.units] for i in range(self.folds)
        ]
        down_piece = jnp.concatenate(parts)
        down_piece = down_piece.reshape(self.columns, self.slices, self.deep)
        return in_piece, down_piece[:, :, : self.real]

    def in_parts(self, s, n, half):
        parts = []
        at = s
        while at < s + n:
            k = at // self.deep
            count = min(s + n, (k + 1) * self.deep) - at
            line = half * self.slices + k
            parts.append((at - s, count, line * self.step + at - k * self.deep))
            at += count
        return parts

    def down_parts(self, s, n):
        width = min(self.wide, s + UNIT_TILE) - s
        return [
            (
                line * self.columns + i * self.low,
                line * self.step + self.deep,
                i * self.wide + s,
                width,
            )
            for line in range(self.lines)
            for i in range(self.folds)
        ]


class Copies:
    def __init__(self, sems):
        self.sems = sems
        self.used = 0

    def start(self, source, target):
        copy = pltpu.make_async_copy(source, target, self.sems.at[self.used])
        self.used += 1
        copy.start()
        return copy


def wait_all(copies):
    for copy in copies:
        copy.wait()


def transpose_tokens(source, target, tokens):
    @pl.loop(0, tokens // TURN_TILE)
    def _(t):
        at = pl.multiple_of(t * TURN_TILE, TURN_TILE)
        target[:, pl.ds(at, TURN_TILE)] = source[pl.ds(at, TURN_TILE), :].T


def load_tokens(blocks, target, copies):
    rows = blocks[0].shape[0]
    return [
        copies.start(block, target.at[pl.ds(k * rows, rows)]) for k, block in enumerate(blocks)
    ]


def load_chunk(chunk, ranks, na_in, oc_in, weights, na, oc, w, d, copies):
    first = load_tokens(na_in, na, copies)
    block_copies = []
    for b, (s, n) in enumerate(chunk.blocks):
        mine = []
        for half in range(2):
            for offset, count, row in chunk.in_parts(s, n, half):
                target = w.at[pl.ds(half * chunk.units + s + offset, count)]
                mine.append(copies.start(weights.at[pl.ds(row, count)], target))
        if b == 0:
            first += load_tokens(oc_in, oc, copies)
        for column, row, at, width in chunk.down_parts(s, n):
            source = weights.at[pl.ds(row, chunk.low), pl.ds(at, width)]
            target = d.at[pl.ds(column, chunk.low), pl.ds(s, width)]
            mine.append(copies.start(source, target))
        block_copies.append(mine)
    return first, block_copies


def store_in(chunk, s, n, half, dw, at, weights_out, copies):
    return [
        copies.start(dw.at[pl.ds(at + offset, count)], weights_out.at[pl.ds(row, count)])
        for offset, count, row in chunk.in_parts(s, n, half)
    ]


def store_down(chunk, s, n, dd, at, weights_out, copies):
    return [
        copies.start(
            dd.at[pl.ds(column, chunk.low), pl.ds(at, width)],
            weights_out.at[pl.ds(row, chunk.low), pl.ds(place, width)],
        )
        for column, row, place, width in chunk.down_parts(s, n)
    ]


def copy_count(chunk):
    parts = sum(len(chunk.in_parts(s, n, 0)) for s, n in chunk.blocks)
    return 2 * parts + len(chunk.blocks) * chunk.lines * chunk.folds


def unit_block(units, s, n, tokens, na, oc, w, d, back, mixed, gt, ut, ht, at_row, add, final):
    wg = w.at[pl.ds(s, n)]
    wu = w.at[pl.ds(units + s, n)]
    db = d.at[:, pl.ds(s, n)]

    @pl.loop(0, tokens // TOKEN_TILE)
    def _(t):
        at = pl.ds(pl.multiple_of(t * TOKEN_TILE, TOKEN_TILE), TOKEN_TILE)
        gate = dot_nt(na[at, :], wg[...])
        up = dot_nt(na[at, :], wu[...])
        hidden_cot = dot_nn(oc[at, :], db[...])
        sigmoid = 1.0 / (1.0 + jnp.exp(-gate))
        activated = gate * sigmoid
        hidden = bf16(activated * up)
        gate_cot = bf16(hidden_cot * up * sigmoid * (1.0 + gate * (1.0 - sigmoid)))
        up_cot = bf16(hidden_cot * activated)
        ht[pl.ds(at_row, n), at] = hidden.T
        gt[pl.ds(at_row, n), at] = gate_cot.T
        ut[pl.ds(at_row, n), at] = up_cot.T
        back_term = dot_nn(gate_cot, wg[...]) + dot_nn(up_cot, wu[...])
        mixed_term = dot_nt(hidden, db[...])
        if add:
            back_term = back_term + back[at, :]
            mixed_term = mixed_term + mixed[at, :]
        if final:
            na[at, :] = bf16(back_term)
            oc[at, :] = bf16(mixed_term)
        else:
            back[at, :] = back_term
            mixed[at, :] = mixed_term


def gradient_block(n, na, oc_t, gt, ut, ht, at_row, dw, dw_gate, dw_up, dd, dd_at):
    at = pl.ds(at_row, n)

    @pl.loop(0, D // GRAD_TILE)
    def _(j):
        cols = pl.ds(pl.multiple_of(j * GRAD_TILE, GRAD_TILE), GRAD_TILE)
        dw[pl.ds(dw_gate, n), cols] = bf16(dot_nn(gt[at, :], na[:, cols]))
        dw[pl.ds(dw_up, n), cols] = bf16(dot_nn(ut[at, :], na[:, cols]))
        dd[cols, pl.ds(dd_at, n)] = bf16(dot_nt(oc_t[cols, :], ht[at, :]))


def first_chunk_kernel(chunk, ranks, carried, *refs):
    na_in = refs[:ranks]
    oc_in = refs[ranks : 2 * ranks]
    weights = refs[2 * ranks]
    refs = refs[2 * ranks + 1 :]
    if carried:
        back_in, mixed_in = refs[:2]
        refs = refs[2:]
    back_out, mixed_out, weights_out = refs[:3]
    na, oc, oc_t, w, d, dw, dd, back, mixed, gt, ut, ht, in_sem, out_sem = refs[3:]
    tokens = na.shape[0]
    copies = Copies(in_sem)
    first, block_copies = load_chunk(chunk, ranks, na_in, oc_in, weights, na, oc, w, d, copies)
    if carried:
        first.append(copies.start(back_in, back))
        first.append(copies.start(mixed_in, mixed))
    wait_all(first)
    transpose_tokens(oc, oc_t, tokens)
    copies = Copies(out_sem)
    outs = []
    stored = []
    for b, (s, n) in enumerate(chunk.blocks):
        wait_all(block_copies[b])
        add = carried or bool(b)
        unit_block(
            chunk.units, s, n, tokens, na, oc, w, d, back, mixed, gt, ut, ht, 0, add, False
        )
        if b == len(chunk.blocks) - 1:
            outs.append(copies.start(back, back_out))
            outs.append(copies.start(mixed, mixed_out))
        wait_all(stored)
        gradient_block(n, na, oc_t, gt, ut, ht, 0, dw, 0, UNIT_TILE, dd, 0)
        stored = store_in(chunk, s, n, 0, dw, 0, weights_out, copies)
        stored += store_in(chunk, s, n, 1, dw, UNIT_TILE, weights_out, copies)
        stored += store_down(chunk, s, n, dd, 0, weights_out, copies)
    wait_all(outs + stored)


def last_chunk_kernel(chunk, ranks, carried, *refs):
    na_in = refs[:ranks]
    oc_in = refs[ranks : 2 * ranks]
    weights = refs[2 * ranks]
    refs = refs[2 * ranks + 1 :]
    if carried:
        back_in, mixed_in = refs[:2]
        refs = refs[2:]
    back_out = refs[:ranks]
    mixed_out = refs[ranks : 2 * ranks]
    kept_out = refs[2 * ranks : 2 * ranks + 3]
    na, oc, w, d, back, mixed, gt, ut, ht, in_sem, out_sem = refs[2 * ranks + 3 :]
    tokens = na.shape[0]
    rows = tokens // ranks
    copies = Copies(in_sem)
    first, block_copies = load_chunk(chunk, ranks, na_in, oc_in, weights, na, oc, w, d, copies)
    if carried:
        first.append(copies.start(back_in, back))
        first.append(copies.start(mixed_in, mixed))
    wait_all(first)
    copies = Copies(out_sem)
    outs = []
    for b, (s, n) in enumerate(chunk.blocks):
        wait_all(block_copies[b])
        unit_block(
            chunk.units,
            s,
            n,
            tokens,
            na,
            oc,
            w,
            d,
            back,
            mixed,
            gt,
            ut,
            ht,
            s,
            carried or bool(b),
            b == len(chunk.blocks) - 1,
        )
        for kept, target in zip((gt, ut, ht), kept_out):
            at = pl.ds(s, n)
            outs.append(copies.start(kept.at[at], target.at[at]))
    for k in range(ranks):
        at = pl.ds(k * rows, rows)
        outs.append(copies.start(na.at[at], back_out[k]))
        outs.append(copies.start(oc.at[at], mixed_out[k]))
    wait_all(outs)


def gradient_kernel(chunk, ranks, *refs):
    na_in = refs[:ranks]
    oc_in = refs[ranks : 2 * ranks]
    kept_in = refs[2 * ranks : 2 * ranks + 3]
    weights_out, na, oc, oc_t, gt, ut, ht, dw, dd, in_sem, out_sem = refs[2 * ranks + 3 :]
    tokens = na.shape[0]
    copies = Copies(in_sem)
    first = load_tokens(oc_in, oc, copies)
    later = load_tokens(na_in, na, copies)
    later += [copies.start(source, kept) for source, kept in zip(kept_in, (gt, ut, ht))]
    wait_all(first)
    transpose_tokens(oc, oc_t, tokens)
    if chunk.wide > chunk.units:
        spare = chunk.wide - chunk.units
        dd[:, pl.ds(chunk.units, spare)] = jnp.zeros((D, spare), jnp.bfloat16)
    wait_all(later)
    copies = Copies(out_sem)
    outs = []
    for s, n in chunk.blocks:
        gradient_block(n, na, oc_t, gt, ut, ht, s, dw, s, chunk.units + s, dd, s)
        outs += store_in(chunk, s, n, 0, dw, s, weights_out, copies)
        outs += store_in(chunk, s, n, 1, dw, chunk.units + s, weights_out, copies)
        outs += store_down(chunk, s, n, dd, s, weights_out, copies)
    wait_all(outs)


def hbm_call(kernel, args, outs, scratch, micros):
    moved = sum(math.prod(a.shape) * a.dtype.itemsize for a in args)
    moved += sum(math.prod(a.shape) * a.dtype.itemsize for a in outs)
    anywhere = pl.BlockSpec(memory_space=pl.ANY)
    return pl.pallas_call(
        kernel,
        out_shape=tuple(outs),
        in_specs=[anywhere] * len(args),
        out_specs=(anywhere,) * len(outs),
        scratch_shapes=scratch,
        compiler_params=pltpu.CompilerParams(vmem_limit_bytes=VMEM_LIMIT),
        cost_estimate=pl.CostEstimate(
            flops=micros * FLOPS_PER_MICRO, bytes_accessed=moved, transcendentals=0
        ),
    )(*args)


def vmem_bf16(*shape):
    return pltpu.VMEM(shape, jnp.bfloat16)


def vmem_f32(*shape):
    return pltpu.VMEM(shape, jnp.float32)


def first_chunk(chunk, na, oc, weights, carry):
    ranks = len(na)
    tokens = ranks * na[0].shape[0]
    scratch = [
        vmem_bf16(tokens, D),
        vmem_bf16(tokens, D),
        vmem_bf16(D, tokens),
        vmem_bf16(2 * chunk.units, D),
        vmem_bf16(D, chunk.wide),
        vmem_bf16(2 * UNIT_TILE, D),
        vmem_bf16(D, UNIT_TILE),
        vmem_f32(tokens, D),
        vmem_f32(tokens, D),
        vmem_bf16(UNIT_TILE, tokens),
        vmem_bf16(UNIT_TILE, tokens),
        vmem_bf16(UNIT_TILE, tokens),
        pltpu.SemaphoreType.DMA((2 * ranks + 2 + copy_count(chunk),)),
        pltpu.SemaphoreType.DMA((2 + copy_count(chunk),)),
    ]
    outs = [f32_like(tokens, D), f32_like(tokens, D), bf16_like(chunk.rows, D)]
    kernel = functools.partial(first_chunk_kernel, chunk, ranks, bool(carry))
    return hbm_call(kernel, [*na, *oc, weights, *carry], outs, scratch, 68)


def last_chunk(chunk, na, oc, weights, carry):
    ranks = len(na)
    rows = na[0].shape[0]
    tokens = ranks * rows
    scratch = [
        vmem_bf16(tokens, D),
        vmem_bf16(tokens, D),
        vmem_bf16(2 * chunk.units, D),
        vmem_bf16(D, chunk.wide),
        vmem_f32(tokens, D),
        vmem_f32(tokens, D),
        vmem_bf16(chunk.units, tokens),
        vmem_bf16(chunk.units, tokens),
        vmem_bf16(chunk.units, tokens),
        pltpu.SemaphoreType.DMA((2 * ranks + 2 + copy_count(chunk),)),
        pltpu.SemaphoreType.DMA((2 * ranks + 3 * len(chunk.blocks),)),
    ]
    outs = [bf16_like(rows, D)] * (2 * ranks) + [bf16_like(chunk.units, tokens)] * 3
    kernel = functools.partial(last_chunk_kernel, chunk, ranks, bool(carry))
    got = hbm_call(
        kernel, [*na, *oc, weights, *carry], outs, scratch, 35
    )
    return got[:ranks], got[ranks : 2 * ranks], got[2 * ranks :]


def chunk_gradients(chunk, na, oc, kept):
    ranks = len(na)
    tokens = ranks * na[0].shape[0]
    scratch = [
        vmem_bf16(tokens, D),
        vmem_bf16(tokens, D),
        vmem_bf16(D, tokens),
        vmem_bf16(chunk.units, tokens),
        vmem_bf16(chunk.units, tokens),
        vmem_bf16(chunk.units, tokens),
        vmem_bf16(2 * chunk.units, D),
        vmem_bf16(D, chunk.wide),
        pltpu.SemaphoreType.DMA((2 * ranks + 3,)),
        pltpu.SemaphoreType.DMA((copy_count(chunk),)),
    ]
    kernel = functools.partial(gradient_kernel, chunk, ranks)
    (terms,) = hbm_call(
        kernel,
        [*na, *oc, *kept],
        [bf16_like(chunk.rows, D)],
        scratch,
        16,
    )
    return terms


def sharded_pass(tokens, cotangent, lengths, half_qkv, half_out, half_in, half_down, half_small):
    ranks = lax.axis_size("dp")
    lines = lax.axis_size("fsdp")
    place = lax.axis_index("dp")
    rows = tokens.shape[1]
    slices = lines // 2
    block = D // ranks
    inputs = tokens[0]
    info = jnp.stack([place, lax.rem(lax.axis_index("fsdp"), 2), lengths[0]])

    small_rows, small_columns = half_small.shape
    columns = half_qkv.shape[1]
    line = jnp.concatenate([half_qkv.T, half_out.T])
    line = scoped("matrix_line", line_gather, line)
    qkv_along = line[:, :columns].reshape(-1, block)
    out_along = line[:, columns:].reshape(-1, block)
    half_small, qkv_along = lax.optimization_barrier((half_small, qkv_along))
    small_line = scoped("small_gather", line_gather, half_small)
    small_other = scoped("small_gather", core_swap, small_line)
    small_line = jnp.stack(
        [
            jnp.where(is_even(), small_line, small_other),
            jnp.where(is_even(), small_other, small_line),
        ],
        axis=1,
    )
    small_line = small_line.reshape(lines, small_rows, small_columns)
    small_stack = jnp.stack(
        [small_line]
        + [scoped("small_gather", dp_send, small_line, k) for k in range(1, ranks)]
    )
    small_vec = jnp.stack(
        [
            lax.dynamic_index_in_dim(small_stack, place ^ a, 0, keepdims=False)
            for a in range(ranks)
        ]
    )
    small_vec = small_vec.transpose(0, 2, 1, 3).reshape(-1).astype(jnp.float32)
    gain_attn, gain_mlp, biases = unpack_small(small_vec)
    gain_attn = gain_attn[None]
    gain_mlp = gain_mlp[None]

    exchange = exchange_weights(half_in, half_down)
    got = scoped("weights_exchange", dp_exchange, next(exchange))
    got, out_along, qkv_along = lax.optimization_barrier((got, out_along, qkv_along))
    qkv_own = scoped("qkv_gather", dp_gather, qkv_along)
    qkv_other = [scoped("qkv_swap", core_swap, block) for block in qkv_own]
    out_along, qkv_other = lax.optimization_barrier((out_along, qkv_other))
    out_near = scoped("out_gather", gather_near, out_along)

    in_piece, down_piece = exchange.send(got)
    chunks = [Chunk(size, lines) for size in CHUNKS]
    gathered = []
    start = 0
    for chunk in chunks:
        stop = start + chunk.real
        packed = chunk.pack(in_piece[start:stop], down_piece[:, :, start:stop])
        gathered.append(lax.all_gather(packed, "fsdp", axis=0, tiled=True))
        start = stop

    query_places = place * rows + jnp.arange(rows, dtype=jnp.int32)
    cosine, sine = rope_tables(query_places.astype(jnp.float32))
    sine = jnp.where(jnp.arange(HEAD) < HEAD // 2, -sine, sine)
    normed, queries, kv = call(
        functools.partial(project_kernel, ranks, slices),
        [info, inputs, gain_attn, biases[None], cosine, sine, *qkv_own, *qkv_other],
        [bf16_like(rows, D), bf16_like(rows, D), bf16_like(rows, 2 * KV_WIDTH)],
        [vmem_f32(rows, QKV)],
        7,
    )
    kv, out_near = lax.optimization_barrier((kv, out_near))
    out_own = scoped("out_gather", gather_far, out_near)
    kv_blocks = scoped("kv_gather", dp_gather, kv)
    out_other = scoped("out_swap", core_swap, jnp.stack(out_own))

    valid = query_places < lengths[0]
    out_cot = jnp.where(valid[:, None], cotangent[0], jnp.zeros_like(cotangent[0]))
    out_cot, *kv_blocks = lax.optimization_barrier((out_cot, *kv_blocks))
    cot_blocks = scoped("cot_gather", dp_gather, out_cot)

    attended, totals, middle, normed_again = call(
        functools.partial(attend_kernel, ranks, slices),
        [info, inputs, gain_mlp, queries, *kv_blocks, *out_own, out_other],
        [bf16_like(rows, D), f32_like(16, rows), f32_like(rows, D), bf16_like(rows, D)],
        [
            vmem_f32(ranks * rows, rows),
            vmem_bf16(ranks * rows, KV_WIDTH),
            vmem_bf16(ranks * rows, KV_WIDTH),
            vmem_bf16(KV_WIDTH, ranks * rows),
        ],
        24,
    )
    normed_blocks = scoped("normed_gather", dp_gather, normed_again)

    *before, end = zip(chunks, gathered)
    carry = ()
    terms = []
    for chunk, weights in before:
        back, mixed, term = first_chunk(chunk, normed_blocks, cot_blocks, weights, carry)
        carry = (back, mixed)
        terms.append(term)
    chunk, weights = end
    back_blocks, mixed_blocks, kept = last_chunk(
        chunk, normed_blocks, cot_blocks, weights, carry
    )
    back_got = [scoped("back_reduce", dp_send, back_blocks[k], k) for k in range(1, ranks)]
    term = chunk_gradients(chunk, normed_blocks, cot_blocks, kept)
    term, back_blocks, back_got, mixed_blocks = lax.optimization_barrier(
        (term, back_blocks, back_got, mixed_blocks)
    )
    terms.append(term)
    first_shard = lax.psum_scatter(terms[0], "fsdp", scatter_dimension=0, tiled=True)

    def pack_chunk(chunk, shard):
        return scoped("gradient_exchange", pack_gradients, *chunk.unpack(shard))

    def exchange_chunk(sent):
        got = scoped("gradient_exchange", dp_exchange, sent)
        return unpack_gradients(got, half_in.shape[0], half_down.shape[1])

    mixed_got = [scoped("mixed_reduce", dp_send, mixed_blocks[k], k) for k in range(1, ranks - 1)]
    middle_cot, middle_low, gain_mlp_grad, query_cot, *kv_cot = call(
        functools.partial(attend_back_kernel, ranks, slices),
        [
            info,
            middle,
            out_cot,
            gain_mlp,
            queries,
            totals,
            back_blocks[0],
            *back_got,
            *kv_blocks,
            *out_own,
            out_other,
        ],
        [f32_like(rows, D), bf16_like(rows, D), f32_like(1, D), f32_like(rows, D)]
        + [bf16_like(rows, 2 * KV_WIDTH)] * ranks,
        [
            vmem_f32(ranks * rows, rows),
            vmem_bf16(ranks * rows, KV_WIDTH),
            vmem_bf16(ranks * rows, KV_WIDTH),
            vmem_bf16(KV_WIDTH, ranks * rows),
            vmem_bf16(rows, D),
            vmem_f32(ranks * rows, KV_WIDTH),
            vmem_f32(ranks * rows, KV_WIDTH),
            vmem_bf16(rows, D // 2),
            vmem_bf16(rows, D // 2),
        ],
        31,
    )

    def outer(left, right):
        columns = right.shape[1]
        return call(
            functools.partial(outer_kernel, ranks, slices),
            [info, left, right],
            [bf16_like(ranks, columns // 2, block)] * 2,
            [vmem_bf16(columns, rows)],
            0,
        )

    kv_cot, middle_low, mixed_got = lax.optimization_barrier((kv_cot, middle_low, mixed_got))
    kv_got = [scoped("kv_reduce", dp_send, kv_cot[k], k) for k in range(1, ranks)]
    out_own_term, out_other_term = outer(attended, middle_low)


    kv_got, out_own_term, out_other_term = lax.optimization_barrier(
        (kv_got, out_own_term, out_other_term)
    )
    out_swapped = scoped("out_core", core_swap, out_other_term)
    projected_low, bias_grad = call(
        functools.partial(project_back_kernel, ranks),
        [info, query_cot, cosine, sine, kv_cot[0], *kv_got],
        [bf16_like(rows, QKV), f32_like(1, QKV)],
        [],
        0,
    )
    projected_low, out_swapped = lax.optimization_barrier((projected_low, out_swapped))
    out_got = scoped("out_dp", reduce_over_dp, sum_blocks(out_own_term, out_swapped))
    qkv_own_term, qkv_other_term = outer(normed, projected_low)

    projected_low, qkv_own_term, qkv_other_term, first_shard, last_term = (
        lax.optimization_barrier(
            (projected_low, qkv_own_term, qkv_other_term, first_shard, terms[1])
        )
    )
    last_shard = lax.psum_scatter(last_term, "fsdp", scatter_dimension=0, tiled=True)
    qkv_swapped = scoped("qkv_core", core_swap, qkv_other_term)
    input_grad, gain_attn_grad = call(
        functools.partial(input_back_kernel, ranks, slices),
        [info, projected_low, inputs, gain_attn, middle_cot, *qkv_own, *qkv_other],
        [bf16_like(rows, D), f32_like(1, D)],
        [vmem_bf16(rows, QKV // 2), vmem_bf16(rows, QKV // 2), vmem_f32(rows, D)],
        0,
    )

    small_term = group_small(gain_attn_grad[0], gain_mlp_grad[0], bias_grad[0])
    small_term = small_term.reshape(ranks, small_rows, slices, 2, small_columns)
    small_term = small_term.transpose(3, 0, 2, 1, 4).reshape(2, ranks, slices, -1)
    small_parity = lax.rem(lax.axis_index("fsdp"), 2)
    small_own = lax.dynamic_index_in_dim(small_term, small_parity, 0, keepdims=False)
    small_other = lax.dynamic_index_in_dim(small_term, 1 - small_parity, 0, keepdims=False)
    small_sums = small_own + scoped("small_core", core_swap, small_other)

    qkv_swapped, out_got, small_sums, first_shard = lax.optimization_barrier(
        (qkv_swapped, out_got, small_sums, first_shard)
    )
    small_rest = ((0, 0), (0, 15), (0, block - small_sums.shape[2]))
    qkv_sums = []
    for k, total in enumerate(sum_blocks(qkv_own_term, qkv_swapped)):
        extra = jnp.pad(dp_own(small_sums, k)[:, None], small_rest)
        total = jnp.concatenate([total.reshape(slices, -1, block), extra], axis=1)
        qkv_sums.append(total.reshape(-1, block))
    qkv_got = scoped("qkv_dp", reduce_over_dp, qkv_sums)
    out_shard = scoped("out_line", reduce_over_line, out_got)
    squares = sum_of_squares(first_shard)
    first_sent = pack_chunk(chunks[0], first_shard)

    qkv_got, out_shard, squares, first_sent = lax.optimization_barrier(
        (qkv_got, out_shard, squares, first_sent)
    )
    qkv_shard = scoped("qkv_line", reduce_over_line, qkv_got)
    out_grad = total_shard(out_shard)
    squares = squares + sum_of_squares(out_grad) + sum_of_squares(last_shard)

    qkv_shard, squares, last_shard, first_sent = lax.optimization_barrier(
        (qkv_shard, squares, last_shard, first_sent)
    )
    qkv_shard = sum(part.astype(jnp.float32) for part in qkv_shard)
    squares = squares + sum_of_squares(qkv_shard)
    squares = scoped("norm_sum", sum_over_dp, squares)
    first_sent, last_shard, squares = lax.optimization_barrier((first_sent, last_shard, squares))
    total_squares = scoped("norm_sum", sum_over_line, scoped("norm_sum", sum_over_core, squares))
    qkv_grad = lax.optimization_barrier(qkv_shard[:columns].T)
    small_grad = qkv_shard[columns, : small_rows * small_columns]
    small_grad = small_grad.reshape(small_rows, small_columns)
    in_first, down_first = exchange_chunk(first_sent)
    in_last, down_last = exchange_chunk(pack_chunk(chunks[1], last_shard))
    in_grad = jnp.concatenate([in_first, in_last], axis=1)
    in_grad = in_grad.transpose(2, 0, 1).reshape(half_in.shape)
    down_grad = jnp.concatenate([down_first, down_last], axis=1)
    down_grad = down_grad.transpose(2, 0, 1, 3).reshape(half_down.shape)
    in_grad, down_grad, mixed_last = lax.optimization_barrier(
        (in_grad, down_grad, mixed_blocks[-1])
    )
    in_grad = in_grad.astype(jnp.float32)
    down_grad = down_grad.astype(jnp.float32)
    mixed_got.append(scoped("mixed_reduce", dp_send, mixed_last, ranks - 1))
    mixed = middle + mixed_blocks[0].astype(jnp.float32)
    for got in mixed_got:
        mixed = mixed + got.astype(jnp.float32)
    mixed = bf16(mixed)
    return (mixed, input_grad, total_squares, qkv_grad, out_grad, in_grad, down_grad, small_grad)


def per_device(
    tokens,
    cotangent,
    lengths,
    qkv_weight,
    qkv_first,
    qkv_second,
    out_weight,
    out_first,
    out_second,
    mlp_in_weight,
    mlp_in_first,
    mlp_in_second,
    down_weight,
    down_first,
    down_second,
    small_params,
    small_first,
    small_second,
):
    results = sharded_pass(
        tokens,
        cotangent,
        lengths,
        bf16(qkv_weight),
        bf16(out_weight),
        bf16(mlp_in_weight),
        bf16(down_weight),
        bf16(small_params),
    )
    mixed, input_cot, total_squares, qkv_grad, out_grad, in_grad, down_grad, small_grad = results
    grad_norm = jnp.sqrt(total_squares)
    clip_factor = CLIP_NORM / jnp.maximum(grad_norm, CLIP_NORM)
    outs = [mixed[None], input_cot[None], grad_norm]
    for weight, first, second, gradient, rate, decay in (
        (qkv_weight, qkv_first, qkv_second, qkv_grad, MATRIX_RATE, MATRIX_DECAY),
        (out_weight, out_first, out_second, out_grad, MATRIX_RATE, MATRIX_DECAY),
        (mlp_in_weight, mlp_in_first, mlp_in_second, in_grad, MATRIX_RATE, MATRIX_DECAY),
        (down_weight, down_first, down_second, down_grad, MATRIX_RATE, MATRIX_DECAY),
        (small_params, small_first, small_second, small_grad, SMALL_RATE, 0.0),
    ):
        outs.extend(update(weight, first, second, gradient, clip_factor, rate, decay))
    return tuple(outs)


def solution(mesh):
    rows = P("fsdp", "dp", None)
    shard = P("dp", "fsdp")
    return jax.shard_map(
        per_device,
        mesh=mesh,
        in_specs=(rows, rows, P("fsdp")) + (shard,) * 15,
        out_specs=(rows, rows, P()) + (shard,) * 20,
        check_vma=False,
    )
```

```python
import functools
import math

import jax
import jax.numpy as jnp
from jax import lax
from jax.experimental import pallas as pl
from jax.experimental.pallas import tpu as pltpu
from jax.sharding import PartitionSpec as P

D = 1536
HEADS = 12
KV_HEADS = 2
HEAD = 128
FF = 8960
STEP = 5
GROUP = 6
SMALL = 5120
QKV = 2048
KV_WIDTH = KV_HEADS * HEAD


NORM_EPS = 1e-06
ROPE_BASE = 1000000.0
BETA_FIRST = 0.5
BETA_SECOND = 0.5
ADAM_EPS = 1e-08
MATRIX_RATE = 0.03
SMALL_RATE = 0.3
MATRIX_DECAY = 0.1
CLIP_NORM = 1.0
MASKED = -1e30
SCALE = HEAD ** (-0.5)
CHUNKS = (1536, 704)
UNIT_TILE = 512
TOKEN_TILE = 640
GRAD_TILE = 512
TURN_TILE = 256
VMEM_LIMIT = 60 * 2**20
FLOPS_PER_MICRO = 1_150_000_000


def unpack_small(small_vec):
    grouped = small_vec.reshape(KV_HEADS * HEAD, 3 * GROUP + 2)
    gain_attn = grouped[:, :GROUP].reshape(-1)
    gain_mlp = grouped[:, GROUP : 2 * GROUP].reshape(-1)
    biases = jnp.concatenate(
        [
            grouped[:, 2 * GROUP : 3 * GROUP].reshape(-1),
            grouped[:, 3 * GROUP],
            grouped[:, 3 * GROUP + 1],
        ]
    )
    return (gain_attn, gain_mlp, biases)


def group_small(gain_attn, gain_mlp, biases):
    count = KV_HEADS * HEAD
    pieces = [
        gain_attn.reshape(count, GROUP),
        gain_mlp.reshape(count, GROUP),
        biases[:D].reshape(count, GROUP),
        biases[D : D + count][:, None],
        biases[D + count :][:, None],
    ]
    return jnp.concatenate(pieces, axis=1).reshape(8, SMALL // 8)


def rope_tables(positions):
    pair_index = jnp.arange(HEAD // 2, dtype=jnp.float32)
    inverse = jnp.power(jnp.float32(ROPE_BASE), -2.0 * pair_index / HEAD)
    angles = positions[:, None] * inverse[None, :]
    angles = jnp.concatenate([angles, angles], axis=-1)
    return (jnp.cos(angles), jnp.sin(angles))


def bf16(array):
    return array.astype(jnp.bfloat16)


def scoped(name, function, *args):
    with jax.named_scope(name):
        return function(*args)


def dot_nn(left, right):
    return jnp.dot(left, right, preferred_element_type=jnp.float32)


def dot_nt(left, right):
    return lax.dot_general(
        left, right, (((1,), (1,)), ((), ())), preferred_element_type=jnp.float32
    )


def dot_tn(left, right):
    return lax.dot_general(
        left, right, (((0,), (0,)), ((), ())), preferred_element_type=jnp.float32
    )


def update(weight, first, second, gradient, clip_factor, rate, decay):
    step_grad = gradient * clip_factor
    first_new = BETA_FIRST * first + (1.0 - BETA_FIRST) * step_grad
    second_new = BETA_SECOND * second + (1.0 - BETA_SECOND) * step_grad * step_grad
    first_fix = 1.0 - BETA_FIRST**STEP
    second_fix = 1.0 - BETA_SECOND**STEP
    weight_new = weight - rate * (
        first_new / first_fix / (jnp.sqrt(second_new / second_fix) + ADAM_EPS) + decay * weight
    )
    return (weight_new, first_new, second_new, weight_new.astype(jnp.bfloat16))


def dp_send(block, k):
    count = lax.axis_size("dp")
    return lax.ppermute(block, "dp", [(i, i ^ k) for i in range(count)])


def core_swap(block):
    count = lax.axis_size("fsdp")
    return lax.ppermute(block, "fsdp", [(i, i ^ 1) for i in range(count)])


def gather_near(block):
    return [block, dp_send(block, 1), dp_send(block, 2)]


def gather_far(near):
    _, one, two = near
    half = one.shape[0] // 2
    return [*near, jnp.concatenate([dp_send(one[:half], 2), dp_send(two[half:], 1)])]


def dp_gather(block):
    return gather_far(gather_near(block))


def dp_own(array, k):
    return lax.dynamic_index_in_dim(array, lax.axis_index("dp") ^ k, 0, keepdims=False)


def dp_exchange(array):
    count = lax.axis_size("dp")
    place = lax.axis_index("dp")
    got = jnp.stack([dp_own(array, 0)] + [dp_send(dp_own(array, k), k) for k in range(1, count)])
    return jnp.stack(
        [lax.dynamic_index_in_dim(got, place ^ a, 0, keepdims=False) for a in range(count)]
    )


def line_send(block, r):
    count = lax.axis_size("fsdp")
    return lax.ppermute(block, "fsdp", [(i, i ^ (2 * r)) for i in range(count)])


def line_gather(block):
    count = lax.axis_size("fsdp") // 2
    place = lax.axis_index("fsdp") // 2
    got = jnp.stack([block] + [line_send(block, r) for r in range(1, count)])
    return jnp.stack(
        [lax.dynamic_index_in_dim(got, place ^ a, 0, keepdims=False) for a in range(count)]
    )


def sum_of_squares(array):
    array = array.astype(jnp.float32)
    return jnp.sum(array * array)


def sum_over_core(term):
    return term + core_swap(term)


def sum_over_line(term):
    return term + sum(line_send(term, r) for r in range(1, lax.axis_size("fsdp") // 2))


def sum_over_dp(term):
    return term + sum(dp_send(term, k) for k in range(1, lax.axis_size("dp")))


def sum_everywhere(term):
    return sum_over_dp(sum_over_line(sum_over_core(term)))


def is_even():
    return lax.rem(lax.axis_index("fsdp"), 2) == 0


def sum_blocks(own, got):
    return [own[k].astype(jnp.float32) + got[k].astype(jnp.float32) for k in range(own.shape[0])]


def reduce_over_dp(summed):
    return [summed[0]] + [dp_send(bf16(summed[k]), k) for k in range(1, len(summed))]


def reduce_over_line(got):
    total = sum(block.astype(jnp.float32) for block in got)
    count = lax.axis_size("fsdp") // 2
    place = lax.axis_index("fsdp") // 2
    parts = total.reshape(count, -1, total.shape[1])
    shard = [lax.dynamic_index_in_dim(parts, place, 0, keepdims=False)]
    for r in range(1, count):
        part = lax.dynamic_index_in_dim(parts, place ^ r, 0, keepdims=False)
        shard.append(line_send(bf16(part), r))
    return shard


def total_shard(shard):
    return sum(block.astype(jnp.float32) for block in shard).T


def exchange_weights(half_in, half_down):
    ranks = lax.axis_size("dp")
    rows, columns = half_in.shape
    part = columns // ranks
    width = half_down.shape[1]
    slices = half_down.shape[0] // (ranks * part)
    in_sent = half_in.reshape(rows, ranks, part).transpose(1, 2, 0)
    down_sent = half_down.reshape(slices, ranks, part, width).transpose(1, 2, 0, 3)
    sent = jnp.concatenate([in_sent, down_sent.reshape(ranks, part, slices * width)], axis=2)
    got = yield sent
    in_piece = got[:, :, :rows].transpose(1, 0, 2).reshape(part, ranks * rows)
    down_piece = got[:, :, rows:].reshape(ranks, part, slices, width).transpose(3, 0, 2, 1)
    yield in_piece, down_piece.reshape(width, ranks * slices, part)


def unpack_gradients(got, rows, columns):
    ranks, part, width = got.shape
    return got[:, :, :rows], got[:, :, rows:].reshape(ranks, part, -1, columns)


def column_slices(own, other, first, target, width, slices):
    for j in range(slices):
        mine = own(j)
        theirs = other(j)
        target[:, pl.ds(2 * j * width, width)] = jnp.where(first, mine, theirs)
        target[:, pl.ds((2 * j + 1) * width, width)] = jnp.where(first, theirs, mine)


def block_columns(ref, place, k, width):
    return ref[:, pl.ds(pl.multiple_of((place ^ k) * width, 128), width)]


def project_kernel(ranks, slices, *refs):
    info, tokens, gain, bias, cosine, sine = refs[:6]
    own = refs[6 : 6 + ranks]
    other = refs[6 + ranks : 6 + 2 * ranks]
    normed, queries, kv, proj = refs[6 + 2 * ranks :]
    place = info[0]
    first = info[1] == 0
    width = own[0].shape[1]
    step = own[0].shape[0] // slices
    part = QKV // (2 * slices)
    x = tokens[...].astype(jnp.float32)
    scale = lax.rsqrt(jnp.mean(x * x, axis=-1, keepdims=True) + NORM_EPS)
    normed[...] = bf16(x * scale * gain[...])

    def product(mats, j):
        return sum(
            dot_nt(block_columns(normed, place, k, width), mats[k][pl.ds(j * step, part), :])
            for k in range(ranks)
        )

    column_slices(
        lambda j: product(own, j), lambda j: product(other, j), first, proj, part, slices
    )
    for h in range(HEADS + KV_HEADS):
        cols = pl.ds(h * HEAD, HEAD)
        u = proj[:, cols] + bias[:, cols]
        turned = bf16(u * cosine[...] + pltpu.roll(u, HEAD // 2, 1) * sine[...])
        if h < HEADS:
            queries[:, cols] = turned
        else:
            kv[:, pl.ds((h - HEADS) * HEAD, HEAD)] = turned
    cols = pl.ds(D + KV_WIDTH, KV_WIDTH)
    kv[:, pl.ds(KV_WIDTH, KV_WIDTH)] = bf16(proj[:, cols] + bias[:, cols])


def score_bias(info, rows, ranks, target):
    place = info[0]
    length = info[2]
    query = place * rows + lax.broadcasted_iota(jnp.int32, (rows, rows), 1)
    for k in range(ranks):
        key = (place ^ k) * rows + lax.broadcasted_iota(jnp.int32, (rows, rows), 0)
        seen = (key <= query) & (key < length)
        target[pl.ds(k * rows, rows), :] = jnp.where(seen, 0.0, MASKED)


def attend_kernel(ranks, slices, *refs):
    info, tokens, gain, queries = refs[:4]
    kv = refs[4 : 4 + ranks]
    own = refs[4 + ranks : 4 + 2 * ranks]
    other = [refs[4 + 2 * ranks].at[k] for k in range(ranks)]
    attended, totals, middle, normed_again, bias, keys, values, values_t = refs[5 + 2 * ranks :]
    place = info[0]
    first = info[1] == 0
    rows = tokens.shape[0]
    width = own[0].shape[1]
    part = own[0].shape[0] // slices
    score_bias(info, rows, ranks, bias)
    for k in range(ranks):
        keys[pl.ds(k * rows, rows), :] = kv[k][:, pl.ds(0, KV_WIDTH)]
        values[pl.ds(k * rows, rows), :] = kv[k][:, pl.ds(KV_WIDTH, KV_WIDTH)]
    values_t[...] = values[...].T

    @pl.loop(0, HEADS, unroll=2)
    def _(h):
        cols = pl.ds(pl.multiple_of(h * HEAD, HEAD), HEAD)
        kv_cols = pl.ds(pl.multiple_of((h // GROUP) * HEAD, HEAD), HEAD)
        scores = dot_nt(keys[:, kv_cols], queries[:, cols]) * SCALE + bias[...]
        peak = jnp.max(scores, axis=0, keepdims=True)
        exponent = jnp.exp(scores - peak)
        total = jnp.sum(exponent, axis=0, keepdims=True)
        totals[pl.ds(h, 1), :] = peak + jnp.log(total)
        probs = bf16(exponent * (1.0 / total))
        attended[:, cols] = bf16(dot_nn(values_t[kv_cols, :], probs).T)

    def product(mats, j):
        return sum(
            dot_nt(block_columns(attended, place, k, width), mats[k][pl.ds(j * part, part), :])
            for k in range(ranks)
        )

    column_slices(
        lambda j: product(own, j), lambda j: product(other, j), first, middle, part, slices
    )
    total = middle[...] + tokens[...].astype(jnp.float32)
    middle[...] = total
    scale = lax.rsqrt(jnp.mean(total * total, axis=-1, keepdims=True) + NORM_EPS)
    normed_again[...] = bf16(total * scale * gain[...])


def attend_back_kernel(ranks, slices, *refs):
    info, middle, cotangent, gain, queries, totals = refs[:6]
    got = refs[6 : 6 + ranks]
    kv = refs[6 + ranks : 6 + 2 * ranks]
    own = refs[6 + 2 * ranks : 6 + 3 * ranks]
    other = [refs[6 + 3 * ranks].at[k] for k in range(ranks)]
    refs = refs[7 + 3 * ranks :]
    middle_cot, middle_low, gain_grad, query_cot = refs[:4]
    kv_cot = refs[4 : 4 + ranks]
    bias, keys, values, keys_t, attended_cot, key_sum, value_sum, low_own, low_other = refs[
        4 + ranks :
    ]
    place = info[0]
    first = info[1] == 0
    rows = middle.shape[0]
    width = own[0].shape[1]
    part = own[0].shape[0] // slices
    position = place * rows + lax.broadcasted_iota(jnp.int32, (rows, 1), 0)
    valid = jnp.where(position < info[2], 1.0, 0.0)
    cot = got[0][...].astype(jnp.float32)
    for k in range(1, ranks):
        cot = cot + got[k][...].astype(jnp.float32)
    v = middle[...]
    scale = lax.rsqrt(jnp.mean(v * v, axis=-1, keepdims=True) + NORM_EPS)
    n = v * scale
    gain_grad[...] = jnp.sum(cot * n, axis=0, keepdims=True)
    scaled = cot * gain[...]
    back = scale * (scaled - n * jnp.mean(scaled * n, axis=-1, keepdims=True))
    back = back + cotangent[...].astype(jnp.float32) * valid
    middle_cot[...] = back
    middle_low[...] = bf16(back)
    for j in range(slices):
        even = middle_low[:, pl.ds(2 * j * part, part)]
        odd = middle_low[:, pl.ds((2 * j + 1) * part, part)]
        low_own[:, pl.ds(j * part, part)] = jnp.where(first, even, odd)
        low_other[:, pl.ds(j * part, part)] = jnp.where(first, odd, even)
    for k in range(ranks):
        cols = pl.ds(pl.multiple_of((place ^ k) * width, 128), width)
        attended_cot[:, cols] = bf16(
            dot_nn(low_own[...], own[k][...]) + dot_nn(low_other[...], other[k][...])
        )
    score_bias(info, rows, ranks, bias)
    for k in range(ranks):
        keys[pl.ds(k * rows, rows), :] = kv[k][:, pl.ds(0, KV_WIDTH)]
        values[pl.ds(k * rows, rows), :] = kv[k][:, pl.ds(KV_WIDTH, KV_WIDTH)]
    keys_t[...] = keys[...].T
    key_sum[...] = jnp.zeros_like(key_sum)
    value_sum[...] = jnp.zeros_like(value_sum)

    @pl.loop(0, HEADS, unroll=2)
    def _(h):
        cols = pl.ds(pl.multiple_of(h * HEAD, HEAD), HEAD)
        kv_cols = pl.ds(pl.multiple_of((h // GROUP) * HEAD, HEAD), HEAD)
        query = queries[:, cols]
        out_cot = attended_cot[:, cols]
        scores = dot_nt(keys[:, kv_cols], query) * SCALE + bias[...]
        probs = jnp.exp(scores - totals[pl.ds(h, 1), :])
        probs_cot = dot_nt(values[:, kv_cols], out_cot)
        row_dot = jnp.sum(probs * probs_cot, axis=0, keepdims=True)
        scores_cot = bf16(probs * (probs_cot - row_dot))
        value_sum[:, kv_cols] += dot_nn(bf16(probs), out_cot)
        key_sum[:, kv_cols] += dot_nn(scores_cot, query)
        query_cot[:, cols] = dot_nn(keys_t[kv_cols, :], scores_cot).T * SCALE

    for k in range(ranks):
        at = pl.ds(k * rows, rows)
        kv_cot[k][:, pl.ds(0, KV_WIDTH)] = bf16(key_sum[at, :] * SCALE)
        kv_cot[k][:, pl.ds(KV_WIDTH, KV_WIDTH)] = bf16(value_sum[at, :])


def outer_kernel(ranks, slices, *refs):
    info, left, right, own, other, turned = refs
    place = info[0]
    parity = info[1]
    width = own.shape[2]
    part = own.shape[1] // slices
    turned[...] = right[...].T
    for k in range(ranks):
        block = block_columns(left, place, k, width)
        for j in range(slices):
            at = pl.ds(j * part, part)
            mine = pl.ds(pl.multiple_of((2 * j + parity) * part, 16), part)
            theirs = pl.ds(pl.multiple_of((2 * j + 1 - parity) * part, 16), part)
            own[k, at, :] = bf16(dot_nn(turned[mine, :], block))
            other[k, at, :] = bf16(dot_nn(turned[theirs, :], block))


def project_back_kernel(ranks, *refs):
    info, query_cot, cosine, sine = refs[:4]
    got = refs[4 : 4 + ranks]
    projected_low, bias_grad = refs[4 + ranks :]
    kv_cot = got[0][...].astype(jnp.float32)
    for k in range(1, ranks):
        kv_cot = kv_cot + got[k][...].astype(jnp.float32)
    for h in range(HEADS + 2 * KV_HEADS):
        cols = pl.ds(h * HEAD, HEAD)
        if h < HEADS:
            u = query_cot[:, cols]
        else:
            u = kv_cot[:, (h - HEADS) * HEAD : (h - HEADS + 1) * HEAD]
        if h < HEADS + KV_HEADS:
            u = u * cosine[...] + pltpu.roll(u * sine[...], HEAD // 2, 1)
        bias_grad[:, cols] = jnp.sum(u, axis=0, keepdims=True)
        projected_low[:, cols] = bf16(u)


def input_back_kernel(ranks, slices, *refs):
    info, projected_low, tokens, gain, middle_cot = refs[:5]
    own = refs[5 : 5 + ranks]
    other = refs[5 + ranks : 5 + 2 * ranks]
    input_grad, gain_grad, low_own, low_other, normed_cot = refs[5 + 2 * ranks :]
    place = info[0]
    first = info[1] == 0
    width = own[0].shape[1]
    step = own[0].shape[0] // slices
    part = QKV // (2 * slices)
    for j in range(slices):
        even = projected_low[:, pl.ds(2 * j * part, part)]
        odd = projected_low[:, pl.ds((2 * j + 1) * part, part)]
        low_own[:, pl.ds(j * part, part)] = jnp.where(first, even, odd)
        low_other[:, pl.ds(j * part, part)] = jnp.where(first, odd, even)
    for k in range(ranks):
        cols = pl.ds(pl.multiple_of((place ^ k) * width, 128), width)
        normed_cot[:, cols] = sum(
            dot_nn(low[:, pl.ds(j * part, part)], mats[k][pl.ds(j * step, part), :])
            for low, mats in ((low_own, own), (low_other, other))
            for j in range(slices)
        )
    x = tokens[...].astype(jnp.float32)
    scale = lax.rsqrt(jnp.mean(x * x, axis=-1, keepdims=True) + NORM_EPS)
    n = x * scale
    cot = normed_cot[...]
    gain_grad[...] = jnp.sum(cot * n, axis=0, keepdims=True)
    scaled = cot * gain[...]
    back = scale * (scaled - n * jnp.mean(scaled * n, axis=-1, keepdims=True))
    input_grad[...] = bf16(middle_cot[...] + back)


def finish_kernel(info, *refs):
    *terms, grad, small, squares = refs
    total = terms[0][...].astype(jnp.float32)
    for term in terms[1:]:
        total = total + term[...].astype(jnp.float32)
    columns = grad.shape[1]
    grad[...] = total[:columns].T
    small[...] = total[columns : columns + 1]
    squares[...] = jnp.sum(total * total, keepdims=True)


def pack_kernel(chunk, ranks, info, shard, *refs):
    outs = refs[:ranks]
    squares, turned = refs[ranks:]
    place = info[0]
    block = D // ranks
    each = chunk.slices // ranks
    rows = shard[pl.ds(0, chunk.real), :].astype(jnp.float32)
    total = jnp.sum(rows * rows, keepdims=True)
    low = shard[pl.ds(chunk.deep, chunk.low), :].astype(jnp.float32)
    for s in range(chunk.slices):
        for i in range(chunk.folds):
            start = i * chunk.wide + s * chunk.deep
            part = low[:, start : start + chunk.real]
            total = total + jnp.sum(part * part, keepdims=True)
            at = (s % each) * chunk.columns + i * chunk.low
            turned[s // each, :, pl.ds(at, chunk.low)] = part.T
    squares[...] = total
    for k in range(ranks):
        cols = pl.ds(pl.multiple_of((place ^ k) * block, 128), block)
        outs[k][:, pl.ds(0, block)] = shard[pl.ds(0, chunk.real), cols]
        outs[k][:, pl.ds(block, each * chunk.columns)] = bf16(turned[place ^ k])


def call(kernel, args, outs, scratch, micros):
    vmem = pl.BlockSpec(memory_space=pltpu.VMEM)
    moved = sum(math.prod(a.shape) * a.dtype.itemsize for a in args)
    moved += sum(math.prod(a.shape) * a.dtype.itemsize for a in outs)
    moved *= min(micros, 1)
    return pl.pallas_call(
        kernel,
        out_shape=tuple(outs),
        in_specs=[pl.BlockSpec(memory_space=pltpu.SMEM)] + [vmem] * (len(args) - 1),
        out_specs=(vmem,) * len(outs),
        scratch_shapes=scratch,
        compiler_params=pltpu.CompilerParams(vmem_limit_bytes=VMEM_LIMIT),
        cost_estimate=pl.CostEstimate(
            flops=micros * FLOPS_PER_MICRO, bytes_accessed=moved, transcendentals=0
        ),
    )(*args)


def f32_like(*shape):
    return jax.ShapeDtypeStruct(shape, jnp.float32)


def bf16_like(*shape):
    return jax.ShapeDtypeStruct(shape, jnp.bfloat16)


class Chunk:
    def __init__(self, size, lines):
        self.lines = lines
        self.slices = lines // 2
        self.real = size // self.slices
        self.deep = -(-self.real // 16) * 16
        self.units = self.slices * self.deep
        self.wide = -(-self.units // 128) * 128
        self.columns = D // lines
        self.folds = D // self.wide if self.columns * self.wide % (16 * D) == 0 else 1
        self.low = self.columns // self.folds
        self.step = self.deep + self.low
        self.rows = lines * self.step
        self.blocks = [
            (s, min(UNIT_TILE, self.units - s)) for s in range(0, self.units, UNIT_TILE)
        ]

    def pack(self, in_piece, down_piece):
        extra = self.deep - self.real
        in_piece = jnp.pad(in_piece, ((0, extra), (0, 0)))
        down_piece = jnp.pad(down_piece, ((0, 0), (0, 0), (0, extra)))
        down_piece = down_piece.reshape(self.columns, self.units)
        down_piece = jnp.pad(down_piece, ((0, 0), (0, self.wide - self.units)))
        parts = [down_piece[i * self.low : (i + 1) * self.low] for i in range(self.folds)]
        down_piece = jnp.concatenate(parts, axis=1)
        down_piece = jnp.pad(down_piece, ((0, 0), (0, D - down_piece.shape[1])))
        return jnp.concatenate([in_piece, down_piece])

    def unpack(self, shard):
        in_piece = shard[: self.real]
        down_piece = shard[self.deep :]
        parts = [
            down_piece[:, i * self.wide : i * self.wide + self.units] for i in range(self.folds)
        ]
        down_piece = jnp.concatenate(parts)
        down_piece = down_piece.reshape(self.columns, self.slices, self.deep)
        return in_piece, down_piece[:, :, : self.real]

    def in_parts(self, s, n, half):
        parts = []
        at = s
        while at < s + n:
            k = at // self.deep
            count = min(s + n, (k + 1) * self.deep) - at
            line = half * self.slices + k
            parts.append((at - s, count, line * self.step + at - k * self.deep))
            at += count
        return parts

    def down_parts(self, s, n):
        width = min(self.wide, s + UNIT_TILE) - s
        return [
            (
                line * self.columns + i * self.low,
                line * self.step + self.deep,
                i * self.wide + s,
                width,
            )
            for line in range(self.lines)
            for i in range(self.folds)
        ]


class Copies:
    def __init__(self, sems):
        self.sems = sems
        self.used = 0

    def start(self, source, target):
        copy = pltpu.make_async_copy(source, target, self.sems.at[self.used])
        self.used += 1
        copy.start()
        return copy


def wait_all(copies):
    for copy in copies:
        copy.wait()


def transpose_tokens(source, target, tokens):
    @pl.loop(0, tokens // TURN_TILE)
    def _(t):
        at = pl.multiple_of(t * TURN_TILE, TURN_TILE)
        target[:, pl.ds(at, TURN_TILE)] = source[pl.ds(at, TURN_TILE), :].T


def load_tokens(blocks, target, copies):
    rows = blocks[0].shape[0]
    return [
        copies.start(block, target.at[pl.ds(k * rows, rows)]) for k, block in enumerate(blocks)
    ]


def load_chunk(chunk, ranks, na_in, oc_in, weights, na, oc, w, d, copies):
    first = load_tokens(na_in, na, copies)
    block_copies = []
    for b, (s, n) in enumerate(chunk.blocks):
        mine = []
        for half in range(2):
            for offset, count, row in chunk.in_parts(s, n, half):
                target = w.at[pl.ds(half * chunk.units + s + offset, count)]
                mine.append(copies.start(weights.at[pl.ds(row, count)], target))
        if b == 0:
            first += load_tokens(oc_in, oc, copies)
        for column, row, at, width in chunk.down_parts(s, n):
            source = weights.at[pl.ds(row, chunk.low), pl.ds(at, width)]
            target = d.at[pl.ds(column, chunk.low), pl.ds(s, width)]
            mine.append(copies.start(source, target))
        block_copies.append(mine)
    return first, block_copies


def store_in(chunk, s, n, half, dw, at, weights_out, copies):
    return [
        copies.start(dw.at[pl.ds(at + offset, count)], weights_out.at[pl.ds(row, count)])
        for offset, count, row in chunk.in_parts(s, n, half)
    ]


def store_down(chunk, s, n, dd, at, weights_out, copies):
    return [
        copies.start(
            dd.at[pl.ds(column, chunk.low), pl.ds(at, width)],
            weights_out.at[pl.ds(row, chunk.low), pl.ds(place, width)],
        )
        for column, row, place, width in chunk.down_parts(s, n)
    ]


def copy_count(chunk):
    parts = sum(len(chunk.in_parts(s, n, 0)) for s, n in chunk.blocks)
    return 2 * parts + len(chunk.blocks) * chunk.lines * chunk.folds


def unit_block(units, s, n, tokens, na, oc, w, d, back, mixed, gt, ut, ht, at_row, add, final):
    wg = w.at[pl.ds(s, n)]
    wu = w.at[pl.ds(units + s, n)]
    db = d.at[:, pl.ds(s, n)]

    @pl.loop(0, tokens // TOKEN_TILE)
    def _(t):
        at = pl.ds(pl.multiple_of(t * TOKEN_TILE, TOKEN_TILE), TOKEN_TILE)
        gate = dot_nt(na[at, :], wg[...])
        up = dot_nt(na[at, :], wu[...])
        hidden_cot = dot_nn(oc[at, :], db[...])
        sigmoid = 1.0 / (1.0 + jnp.exp(-gate))
        activated = gate * sigmoid
        hidden = bf16(activated * up)
        gate_cot = bf16(hidden_cot * up * sigmoid * (1.0 + gate * (1.0 - sigmoid)))
        up_cot = bf16(hidden_cot * activated)
        ht[pl.ds(at_row, n), at] = hidden.T
        gt[pl.ds(at_row, n), at] = gate_cot.T
        ut[pl.ds(at_row, n), at] = up_cot.T
        back_term = dot_nn(gate_cot, wg[...]) + dot_nn(up_cot, wu[...])
        mixed_term = dot_nt(hidden, db[...])
        if add:
            back_term = back_term + back[at, :]
            mixed_term = mixed_term + mixed[at, :]
        if final:
            na[at, :] = bf16(back_term)
            oc[at, :] = bf16(mixed_term)
        else:
            back[at, :] = back_term
            mixed[at, :] = mixed_term


def gradient_block(n, na, oc_t, gt, ut, ht, at_row, dw, dw_gate, dw_up, dd, dd_at):
    at = pl.ds(at_row, n)

    @pl.loop(0, D // GRAD_TILE)
    def _(j):
        cols = pl.ds(pl.multiple_of(j * GRAD_TILE, GRAD_TILE), GRAD_TILE)
        dw[pl.ds(dw_gate, n), cols] = bf16(dot_nn(gt[at, :], na[:, cols]))
        dw[pl.ds(dw_up, n), cols] = bf16(dot_nn(ut[at, :], na[:, cols]))
        dd[cols, pl.ds(dd_at, n)] = bf16(dot_nt(oc_t[cols, :], ht[at, :]))


def first_chunk_kernel(chunk, ranks, carried, *refs):
    na_in = refs[:ranks]
    oc_in = refs[ranks : 2 * ranks]
    weights = refs[2 * ranks]
    refs = refs[2 * ranks + 1 :]
    if carried:
        back_in, mixed_in = refs[:2]
        refs = refs[2:]
    back_out, mixed_out, weights_out = refs[:3]
    na, oc, oc_t, w, d, dw, dd, back, mixed, gt, ut, ht, in_sem, out_sem = refs[3:]
    tokens = na.shape[0]
    copies = Copies(in_sem)
    first, block_copies = load_chunk(chunk, ranks, na_in, oc_in, weights, na, oc, w, d, copies)
    if carried:
        first.append(copies.start(back_in, back))
        first.append(copies.start(mixed_in, mixed))
    wait_all(first)
    transpose_tokens(oc, oc_t, tokens)
    copies = Copies(out_sem)
    outs = []
    stored = []
    for b, (s, n) in enumerate(chunk.blocks):
        wait_all(block_copies[b])
        add = carried or bool(b)
        unit_block(
            chunk.units, s, n, tokens, na, oc, w, d, back, mixed, gt, ut, ht, 0, add, False
        )
        if b == len(chunk.blocks) - 1:
            outs.append(copies.start(back, back_out))
            outs.append(copies.start(mixed, mixed_out))
        wait_all(stored)
        gradient_block(n, na, oc_t, gt, ut, ht, 0, dw, 0, UNIT_TILE, dd, 0)
        stored = store_in(chunk, s, n, 0, dw, 0, weights_out, copies)
        stored += store_in(chunk, s, n, 1, dw, UNIT_TILE, weights_out, copies)
        stored += store_down(chunk, s, n, dd, 0, weights_out, copies)
    wait_all(outs + stored)


def last_chunk_kernel(chunk, ranks, carried, start, *refs):
    na_in = refs[:ranks]
    oc_in = refs[ranks : 2 * ranks]
    weights = refs[2 * ranks]
    refs = refs[2 * ranks + 1 :]
    if carried:
        back_in, mixed_in = refs[:2]
        refs = refs[2:]
    back_out = refs[:ranks]
    mixed_out = refs[ranks : 2 * ranks]
    kept_out = refs[2 * ranks : 2 * ranks + 3]
    na, oc, w, d, back, mixed, gt, ut, ht, in_sem, out_sem = refs[2 * ranks + 3 :]
    tokens = na.shape[0]
    rows = tokens // ranks
    copies = Copies(in_sem)
    first, block_copies = load_chunk(chunk, ranks, na_in, oc_in, weights, na, oc, w, d, copies)
    if carried:
        at = pl.ds(start * rows, tokens)
        first.append(copies.start(back_in.at[at], back))
        first.append(copies.start(mixed_in.at[at], mixed))
    wait_all(first)
    copies = Copies(out_sem)
    outs = []
    for b, (s, n) in enumerate(chunk.blocks):
        wait_all(block_copies[b])
        unit_block(
            chunk.units,
            s,
            n,
            tokens,
            na,
            oc,
            w,
            d,
            back,
            mixed,
            gt,
            ut,
            ht,
            s,
            carried or bool(b),
            b == len(chunk.blocks) - 1,
        )
        for kept, target in zip((gt, ut, ht), kept_out):
            at = pl.ds(s, n)
            outs.append(copies.start(kept.at[at], target.at[at]))
    for k in range(ranks):
        at = pl.ds(k * rows, rows)
        outs.append(copies.start(na.at[at], back_out[k]))
        outs.append(copies.start(oc.at[at], mixed_out[k]))
    wait_all(outs)


def gradient_kernel(chunk, ranks, *refs):
    na_in = refs[:ranks]
    oc_in = refs[ranks : 2 * ranks]
    kept_in = refs[2 * ranks : 2 * ranks + 6]
    weights_out, na, oc, oc_t, gt, ut, ht, dw, dd, in_sem, out_sem = refs[2 * ranks + 6 :]
    tokens = na.shape[0]
    copies = Copies(in_sem)
    first = load_tokens(oc_in, oc, copies)
    later = load_tokens(na_in, na, copies)
    half = tokens // 2
    for i, source in enumerate(kept_in):
        kept = (gt, ut, ht)[i % 3].at[:, pl.ds(i // 3 * half, half)]
        later.append(copies.start(source, kept))
    wait_all(first)
    transpose_tokens(oc, oc_t, tokens)
    if chunk.wide > chunk.units:
        spare = chunk.wide - chunk.units
        dd[:, pl.ds(chunk.units, spare)] = jnp.zeros((D, spare), jnp.bfloat16)
    wait_all(later)
    copies = Copies(out_sem)
    outs = []
    for s, n in chunk.blocks:
        gradient_block(n, na, oc_t, gt, ut, ht, s, dw, s, chunk.units + s, dd, s)
        outs += store_in(chunk, s, n, 0, dw, s, weights_out, copies)
        outs += store_in(chunk, s, n, 1, dw, chunk.units + s, weights_out, copies)
        outs += store_down(chunk, s, n, dd, s, weights_out, copies)
    wait_all(outs)


def hbm_call(kernel, args, outs, scratch, micros):
    moved = sum(math.prod(a.shape) * a.dtype.itemsize for a in args)
    moved += sum(math.prod(a.shape) * a.dtype.itemsize for a in outs)
    anywhere = pl.BlockSpec(memory_space=pl.ANY)
    return pl.pallas_call(
        kernel,
        out_shape=tuple(outs),
        in_specs=[anywhere] * len(args),
        out_specs=(anywhere,) * len(outs),
        scratch_shapes=scratch,
        compiler_params=pltpu.CompilerParams(vmem_limit_bytes=VMEM_LIMIT),
        cost_estimate=pl.CostEstimate(
            flops=micros * FLOPS_PER_MICRO, bytes_accessed=moved, transcendentals=0
        ),
    )(*args)


def vmem_bf16(*shape):
    return pltpu.VMEM(shape, jnp.bfloat16)


def vmem_f32(*shape):
    return pltpu.VMEM(shape, jnp.float32)


def first_chunk(chunk, na, oc, weights, carry):
    ranks = len(na)
    tokens = ranks * na[0].shape[0]
    scratch = [
        vmem_bf16(tokens, D),
        vmem_bf16(tokens, D),
        vmem_bf16(D, tokens),
        vmem_bf16(2 * chunk.units, D),
        vmem_bf16(D, chunk.wide),
        vmem_bf16(2 * UNIT_TILE, D),
        vmem_bf16(D, UNIT_TILE),
        vmem_f32(tokens, D),
        vmem_f32(tokens, D),
        vmem_bf16(UNIT_TILE, tokens),
        vmem_bf16(UNIT_TILE, tokens),
        vmem_bf16(UNIT_TILE, tokens),
        pltpu.SemaphoreType.DMA((2 * ranks + 2 + copy_count(chunk),)),
        pltpu.SemaphoreType.DMA((2 + copy_count(chunk),)),
    ]
    outs = [f32_like(tokens, D), f32_like(tokens, D), bf16_like(chunk.rows, D)]
    kernel = functools.partial(first_chunk_kernel, chunk, ranks, bool(carry))
    return hbm_call(kernel, [*na, *oc, weights, *carry], outs, scratch, 68)


def last_chunk(chunk, na, oc, weights, carry, start):
    ranks = len(na)
    rows = na[0].shape[0]
    tokens = ranks * rows
    scratch = [
        vmem_bf16(tokens, D),
        vmem_bf16(tokens, D),
        vmem_bf16(2 * chunk.units, D),
        vmem_bf16(D, chunk.wide),
        vmem_f32(tokens, D),
        vmem_f32(tokens, D),
        vmem_bf16(chunk.units, tokens),
        vmem_bf16(chunk.units, tokens),
        vmem_bf16(chunk.units, tokens),
        pltpu.SemaphoreType.DMA((2 * ranks + 2 + copy_count(chunk),)),
        pltpu.SemaphoreType.DMA((2 * ranks + 3 * len(chunk.blocks),)),
    ]
    outs = [bf16_like(rows, D)] * (2 * ranks) + [bf16_like(chunk.units, tokens)] * 3
    kernel = functools.partial(last_chunk_kernel, chunk, ranks, bool(carry), start)
    got = hbm_call(
        kernel, [*na, *oc, weights, *carry], outs, scratch, 20
    )
    return got[:ranks], got[ranks : 2 * ranks], got[2 * ranks :]


def chunk_gradients(chunk, na, oc, kept):
    ranks = len(na)
    tokens = ranks * na[0].shape[0]
    scratch = [
        vmem_bf16(tokens, D),
        vmem_bf16(tokens, D),
        vmem_bf16(D, tokens),
        vmem_bf16(chunk.units, tokens),
        vmem_bf16(chunk.units, tokens),
        vmem_bf16(chunk.units, tokens),
        vmem_bf16(2 * chunk.units, D),
        vmem_bf16(D, chunk.wide),
        pltpu.SemaphoreType.DMA((2 * ranks + 6,)),
        pltpu.SemaphoreType.DMA((copy_count(chunk),)),
    ]
    kernel = functools.partial(gradient_kernel, chunk, ranks)
    (terms,) = hbm_call(
        kernel,
        [*na, *oc, *kept],
        [bf16_like(chunk.rows, D)],
        scratch,
        16,
    )
    return terms


def sharded_pass(tokens, cotangent, lengths, half_qkv, half_out, half_in, half_down, half_small):
    ranks = lax.axis_size("dp")
    lines = lax.axis_size("fsdp")
    place = lax.axis_index("dp")
    rows = tokens.shape[1]
    slices = lines // 2
    block = D // ranks
    inputs = tokens[0]
    info = jnp.stack([place, lax.rem(lax.axis_index("fsdp"), 2), lengths[0]])

    small_rows, small_columns = half_small.shape
    columns = half_qkv.shape[1]
    line = jnp.concatenate([half_qkv.T, half_out.T])
    line = scoped("matrix_line", line_gather, line)
    qkv_along = line[:, :columns].reshape(-1, block)
    out_along = line[:, columns:].reshape(-1, block)
    half_small, qkv_along = lax.optimization_barrier((half_small, qkv_along))
    small_line = scoped("small_gather", line_gather, half_small)
    small_other = scoped("small_gather", core_swap, small_line)
    small_line = jnp.stack(
        [
            jnp.where(is_even(), small_line, small_other),
            jnp.where(is_even(), small_other, small_line),
        ],
        axis=1,
    )
    small_line = small_line.reshape(lines, small_rows, small_columns)
    small_stack = jnp.stack(
        [small_line]
        + [scoped("small_gather", dp_send, small_line, k) for k in range(1, ranks)]
    )
    small_vec = jnp.stack(
        [
            lax.dynamic_index_in_dim(small_stack, place ^ a, 0, keepdims=False)
            for a in range(ranks)
        ]
    )
    small_vec = small_vec.transpose(0, 2, 1, 3).reshape(-1).astype(jnp.float32)
    gain_attn, gain_mlp, biases = unpack_small(small_vec)
    gain_attn = gain_attn[None]
    gain_mlp = gain_mlp[None]

    exchange = exchange_weights(half_in, half_down)
    got = scoped("weights_exchange", dp_exchange, next(exchange))
    got, out_along, qkv_along = lax.optimization_barrier((got, out_along, qkv_along))
    qkv_own = scoped("qkv_gather", dp_gather, qkv_along)
    qkv_other = [scoped("qkv_swap", core_swap, block) for block in qkv_own]
    out_along, qkv_other = lax.optimization_barrier((out_along, qkv_other))
    out_near = scoped("out_gather", gather_near, out_along)

    in_piece, down_piece = exchange.send(got)
    chunks = [Chunk(size, lines) for size in CHUNKS]
    gathered = []
    start = 0
    for chunk in chunks:
        stop = start + chunk.real
        packed = chunk.pack(in_piece[start:stop], down_piece[:, :, start:stop])
        gathered.append(lax.all_gather(packed, "fsdp", axis=0, tiled=True))
        start = stop

    query_places = place * rows + jnp.arange(rows, dtype=jnp.int32)
    cosine, sine = rope_tables(query_places.astype(jnp.float32))
    sine = jnp.where(jnp.arange(HEAD) < HEAD // 2, -sine, sine)
    normed, queries, kv = call(
        functools.partial(project_kernel, ranks, slices),
        [info, inputs, gain_attn, biases[None], cosine, sine, *qkv_own, *qkv_other],
        [bf16_like(rows, D), bf16_like(rows, D), bf16_like(rows, 2 * KV_WIDTH)],
        [vmem_f32(rows, QKV)],
        7,
    )
    kv, out_near = lax.optimization_barrier((kv, out_near))
    out_own = scoped("out_gather", gather_far, out_near)
    kv_blocks = scoped("kv_gather", dp_gather, kv)
    out_other = scoped("out_swap", core_swap, jnp.stack(out_own))

    valid = query_places < lengths[0]
    out_cot = jnp.where(valid[:, None], cotangent[0], jnp.zeros_like(cotangent[0]))
    out_cot, *kv_blocks = lax.optimization_barrier((out_cot, *kv_blocks))
    cot_blocks = scoped("cot_gather", dp_gather, out_cot)

    attended, totals, middle, normed_again = call(
        functools.partial(attend_kernel, ranks, slices),
        [info, inputs, gain_mlp, queries, *kv_blocks, *out_own, out_other],
        [bf16_like(rows, D), f32_like(16, rows), f32_like(rows, D), bf16_like(rows, D)],
        [
            vmem_f32(ranks * rows, rows),
            vmem_bf16(ranks * rows, KV_WIDTH),
            vmem_bf16(ranks * rows, KV_WIDTH),
            vmem_bf16(KV_WIDTH, ranks * rows),
        ],
        24,
    )
    normed_blocks = scoped("normed_gather", dp_gather, normed_again)

    *before, end = zip(chunks, gathered)
    carry = ()
    terms = []
    for chunk, weights in before:
        back, mixed, term = first_chunk(chunk, normed_blocks, cot_blocks, weights, carry)
        carry = (back, mixed)
        terms.append(term)
    chunk, weights = end
    half = ranks // 2
    far_back, far_mixed, far_kept = last_chunk(
        chunk, normed_blocks[half:], cot_blocks[half:], weights, carry, half
    )
    far_got = [scoped("back_reduce", dp_send, far_back[k - half], k) for k in range(half, ranks)]
    near_cot, far_back = lax.optimization_barrier((cot_blocks[:half], far_back))
    near_back, near_mixed, near_kept = last_chunk(
        chunk, normed_blocks[:half], near_cot, weights, carry, 0
    )
    back_got = [scoped("back_reduce", dp_send, near_back[k], k) for k in range(1, half)] + far_got
    back_blocks = near_back
    mixed_blocks = [*near_mixed, *far_mixed]
    kept = [*near_kept, *far_kept]
    term = chunk_gradients(chunk, normed_blocks, cot_blocks, kept)
    term, back_blocks, back_got, mixed_blocks = lax.optimization_barrier(
        (term, back_blocks, back_got, mixed_blocks)
    )
    terms.append(term)
    first_shard = lax.psum_scatter(terms[0], "fsdp", scatter_dimension=0, tiled=True)

    def pack_chunk(chunk, shard):
        width = block + D // ranks // 2
        *sent, squares = call(
            functools.partial(pack_kernel, chunk, ranks),
            [info, shard],
            [bf16_like(chunk.real, width)] * ranks + [f32_like(1, 1)],
            [vmem_f32(ranks, chunk.real, width - block)],
            0,
        )
        return sent, squares[0, 0]

    def exchange_chunk(sent):
        got = sent[:1] + [scoped("gradient_exchange", dp_send, sent[k], k) for k in range(1, ranks)]
        return got

    def place_chunk(got):
        stacked = jnp.stack(got)
        ordered = jnp.stack(
            [
                lax.dynamic_index_in_dim(stacked, place ^ a, 0, keepdims=False)
                for a in range(ranks)
            ]
        )
        return unpack_gradients(ordered, half_in.shape[0], half_down.shape[1])

    mixed_got = [scoped("mixed_reduce", dp_send, mixed_blocks[k], k) for k in range(1, ranks - 1)]
    middle_cot, middle_low, gain_mlp_grad, query_cot, *kv_cot = call(
        functools.partial(attend_back_kernel, ranks, slices),
        [
            info,
            middle,
            out_cot,
            gain_mlp,
            queries,
            totals,
            back_blocks[0],
            *back_got,
            *kv_blocks,
            *out_own,
            out_other,
        ],
        [f32_like(rows, D), bf16_like(rows, D), f32_like(1, D), f32_like(rows, D)]
        + [bf16_like(rows, 2 * KV_WIDTH)] * ranks,
        [
            vmem_f32(ranks * rows, rows),
            vmem_bf16(ranks * rows, KV_WIDTH),
            vmem_bf16(ranks * rows, KV_WIDTH),
            vmem_bf16(KV_WIDTH, ranks * rows),
            vmem_bf16(rows, D),
            vmem_f32(ranks * rows, KV_WIDTH),
            vmem_f32(ranks * rows, KV_WIDTH),
            vmem_bf16(rows, D // 2),
            vmem_bf16(rows, D // 2),
        ],
        31,
    )

    def outer(left, right):
        columns = right.shape[1]
        return call(
            functools.partial(outer_kernel, ranks, slices),
            [info, left, right],
            [bf16_like(ranks, columns // 2, block)] * 2,
            [vmem_bf16(columns, rows)],
            0,
        )

    kv_cot, middle_low, mixed_got = lax.optimization_barrier((kv_cot, middle_low, mixed_got))
    kv_got = [scoped("kv_reduce", dp_send, kv_cot[k], k) for k in range(1, ranks)]
    out_own_term, out_other_term = outer(attended, middle_low)


    kv_got, out_own_term, out_other_term = lax.optimization_barrier(
        (kv_got, out_own_term, out_other_term)
    )
    out_swapped = scoped("out_core", core_swap, out_other_term)
    projected_low, bias_grad = call(
        functools.partial(project_back_kernel, ranks),
        [info, query_cot, cosine, sine, kv_cot[0], *kv_got],
        [bf16_like(rows, QKV), f32_like(1, QKV)],
        [],
        0,
    )
    out_sums = sum_blocks(out_own_term, out_swapped)
    out_sums = [out_sums[0]] + [bf16(total) for total in out_sums[1:]]
    projected_low, out_sums = lax.optimization_barrier((projected_low, out_sums))
    out_got = scoped("out_dp", reduce_over_dp, out_sums)
    qkv_own_term, qkv_other_term = outer(normed, projected_low)

    qkv_own_term, qkv_other_term, projected_low = lax.optimization_barrier(
        (qkv_own_term, qkv_other_term, projected_low)
    )
    qkv_swapped = scoped("qkv_core", core_swap, qkv_other_term)
    input_grad, gain_attn_grad = call(
        functools.partial(input_back_kernel, ranks, slices),
        [info, projected_low, inputs, gain_attn, middle_cot, *qkv_own, *qkv_other],
        [bf16_like(rows, D), f32_like(1, D)],
        [vmem_bf16(rows, QKV // 2), vmem_bf16(rows, QKV // 2), vmem_f32(rows, D)],
        0,
    )

    gain_attn_grad, first_shard, last_term, out_got[1:3] = lax.optimization_barrier(
        (gain_attn_grad, first_shard, terms[1], out_got[1:3])
    )
    last_shard = lax.psum_scatter(last_term, "fsdp", scatter_dimension=0, tiled=True)
    small_term = group_small(gain_attn_grad[0], gain_mlp_grad[0], bias_grad[0])
    small_term = small_term.reshape(ranks, small_rows, slices, 2, small_columns)
    small_term = small_term.transpose(3, 0, 2, 1, 4).reshape(2, ranks, slices, -1)
    small_parity = lax.rem(lax.axis_index("fsdp"), 2)
    small_own = lax.dynamic_index_in_dim(small_term, small_parity, 0, keepdims=False)
    small_other = lax.dynamic_index_in_dim(small_term, 1 - small_parity, 0, keepdims=False)
    small_sums = small_own + scoped("small_core", core_swap, small_other)

    qkv_swapped, out_got, small_sums, first_shard = lax.optimization_barrier(
        (qkv_swapped, out_got, small_sums, first_shard)
    )
    small_rest = ((0, 0), (0, 15), (0, block - small_sums.shape[2]))
    qkv_sums = []
    for k, total in enumerate(sum_blocks(qkv_own_term, qkv_swapped)):
        extra = jnp.pad(dp_own(small_sums, k)[:, None], small_rest)
        total = jnp.concatenate([total.reshape(slices, -1, block), extra], axis=1)
        qkv_sums.append(total.reshape(-1, block))
    qkv_got = scoped("qkv_dp", reduce_over_dp, qkv_sums)
    out_shard = scoped("out_line", reduce_over_line, out_got)
    first_sent, squares = pack_chunk(chunks[0], first_shard)

    qkv_got, out_shard, squares, first_sent = lax.optimization_barrier(
        (qkv_got, out_shard, squares, first_sent)
    )
    qkv_shard = scoped("qkv_line", reduce_over_line, qkv_got)
    out_grad = total_shard(out_shard)
    squares = squares + sum_of_squares(out_grad)
    first_got = exchange_chunk(first_sent)
    mixed_last, first_got = lax.optimization_barrier((mixed_blocks[-1], first_got))
    mixed_got.append(scoped("mixed_reduce", dp_send, mixed_last, ranks - 1))

    qkv_shard, squares, last_shard, first_got = lax.optimization_barrier(
        (qkv_shard, squares, last_shard, first_got)
    )
    last_sent, last_squares = pack_chunk(chunks[1], last_shard)
    last_got = exchange_chunk(last_sent)
    qkv_grad, small_row, qkv_squares = call(
        finish_kernel,
        [info, *qkv_shard],
        [f32_like(block, columns), f32_like(1, block), f32_like(1, 1)],
        [],
        0,
    )
    squares = squares + last_squares + qkv_squares[0, 0]
    squares, last_got[1], mixed_got = lax.optimization_barrier((squares, last_got[1], mixed_got))
    total_squares = scoped("norm_sum", sum_everywhere, squares)
    small_grad = small_row[0, : small_rows * small_columns]
    small_grad = small_grad.reshape(small_rows, small_columns)
    in_first, down_first = place_chunk(first_got)
    in_last, down_last = place_chunk(last_got)
    in_grad = jnp.concatenate([in_first, in_last], axis=1)
    in_grad = in_grad.transpose(2, 0, 1).reshape(half_in.shape)
    down_grad = jnp.concatenate([down_first, down_last], axis=1)
    down_grad = down_grad.transpose(2, 0, 1, 3).reshape(half_down.shape)
    in_grad, down_grad = lax.optimization_barrier((in_grad, down_grad))
    in_grad = in_grad.astype(jnp.float32)
    down_grad = down_grad.astype(jnp.float32)
    mixed = middle + mixed_blocks[0].astype(jnp.float32)
    for got in mixed_got:
        mixed = mixed + got.astype(jnp.float32)
    mixed = bf16(mixed)
    return (mixed, input_grad, total_squares, qkv_grad, out_grad, in_grad, down_grad, small_grad)


def per_device(
    tokens,
    cotangent,
    lengths,
    qkv_weight,
    qkv_first,
    qkv_second,
    out_weight,
    out_first,
    out_second,
    mlp_in_weight,
    mlp_in_first,
    mlp_in_second,
    down_weight,
    down_first,
    down_second,
    small_params,
    small_first,
    small_second,
):
    results = sharded_pass(
        tokens,
        cotangent,
        lengths,
        bf16(qkv_weight),
        bf16(out_weight),
        bf16(mlp_in_weight),
        bf16(down_weight),
        bf16(small_params),
    )
    mixed, input_cot, total_squares, qkv_grad, out_grad, in_grad, down_grad, small_grad = results
    grad_norm = jnp.sqrt(total_squares)
    clip_factor = CLIP_NORM / jnp.maximum(grad_norm, CLIP_NORM)
    outs = [mixed[None], input_cot[None], grad_norm]
    for weight, first, second, gradient, rate, decay in (
        (qkv_weight, qkv_first, qkv_second, qkv_grad, MATRIX_RATE, MATRIX_DECAY),
        (out_weight, out_first, out_second, out_grad, MATRIX_RATE, MATRIX_DECAY),
        (mlp_in_weight, mlp_in_first, mlp_in_second, in_grad, MATRIX_RATE, MATRIX_DECAY),
        (down_weight, down_first, down_second, down_grad, MATRIX_RATE, MATRIX_DECAY),
        (small_params, small_first, small_second, small_grad, SMALL_RATE, 0.0),
    ):
        outs.extend(update(weight, first, second, gradient, clip_factor, rate, decay))
    return tuple(outs)


def solution(mesh):
    rows = P("fsdp", "dp", None)
    shard = P("dp", "fsdp")
    return jax.shard_map(
        per_device,
        mesh=mesh,
        in_specs=(rows, rows, P("fsdp")) + (shard,) * 15,
        out_specs=(rows, rows, P()) + (shard,) * 20,
        check_vma=False,
    )
```

```python
import functools
import math

import jax
import jax.numpy as jnp
from jax import lax
from jax.experimental import pallas as pl
from jax.experimental.pallas import tpu as pltpu
from jax.sharding import PartitionSpec as P

D = 1536
HEADS = 12
KV_HEADS = 2
HEAD = 128
FF = 8960
STEP = 5
GROUP = 6
SMALL = 5120
QKV = 2048
KV_WIDTH = KV_HEADS * HEAD


NORM_EPS = 1e-06
ROPE_BASE = 1000000.0
BETA_FIRST = 0.5
BETA_SECOND = 0.5
ADAM_EPS = 1e-08
MATRIX_RATE = 0.03
SMALL_RATE = 0.3
MATRIX_DECAY = 0.1
CLIP_NORM = 1.0
MASKED = -1e30
SCALE = HEAD ** (-0.5)
CHUNKS = (1536, 704)
UNIT_TILE = 512
TOKEN_TILE = 640
GRAD_TILE = 512
TURN_TILE = 256
VMEM_LIMIT = 60 * 2**20
FLOPS_PER_MICRO = 1_150_000_000


def unpack_small(small_vec):
    grouped = small_vec.reshape(KV_HEADS * HEAD, 3 * GROUP + 2)
    gain_attn = grouped[:, :GROUP].reshape(-1)
    gain_mlp = grouped[:, GROUP : 2 * GROUP].reshape(-1)
    biases = jnp.concatenate(
        [
            grouped[:, 2 * GROUP : 3 * GROUP].reshape(-1),
            grouped[:, 3 * GROUP],
            grouped[:, 3 * GROUP + 1],
        ]
    )
    return (gain_attn, gain_mlp, biases)


def group_small(gain_attn, gain_mlp, biases):
    count = KV_HEADS * HEAD
    pieces = [
        gain_attn.reshape(count, GROUP),
        gain_mlp.reshape(count, GROUP),
        biases[:D].reshape(count, GROUP),
        biases[D : D + count][:, None],
        biases[D + count :][:, None],
    ]
    return jnp.concatenate(pieces, axis=1).reshape(8, SMALL // 8)


def rope_tables(positions):
    pair_index = jnp.arange(HEAD // 2, dtype=jnp.float32)
    inverse = jnp.power(jnp.float32(ROPE_BASE), -2.0 * pair_index / HEAD)
    angles = positions[:, None] * inverse[None, :]
    angles = jnp.concatenate([angles, angles], axis=-1)
    return (jnp.cos(angles), jnp.sin(angles))


def bf16(array):
    return array.astype(jnp.bfloat16)


def scoped(name, function, *args):
    with jax.named_scope(name):
        return function(*args)


def dot_nn(left, right):
    return jnp.dot(left, right, preferred_element_type=jnp.float32)


def dot_nt(left, right):
    return lax.dot_general(
        left, right, (((1,), (1,)), ((), ())), preferred_element_type=jnp.float32
    )


def dot_tn(left, right):
    return lax.dot_general(
        left, right, (((0,), (0,)), ((), ())), preferred_element_type=jnp.float32
    )


def update(weight, first, second, gradient, clip_factor, rate, decay):
    step_grad = gradient * clip_factor
    first_new = BETA_FIRST * first + (1.0 - BETA_FIRST) * step_grad
    second_new = BETA_SECOND * second + (1.0 - BETA_SECOND) * step_grad * step_grad
    first_fix = 1.0 - BETA_FIRST**STEP
    second_fix = 1.0 - BETA_SECOND**STEP
    weight_new = weight - rate * (
        first_new / first_fix / (jnp.sqrt(second_new / second_fix) + ADAM_EPS) + decay * weight
    )
    return (weight_new, first_new, second_new, weight_new.astype(jnp.bfloat16))


def dp_send(block, k):
    count = lax.axis_size("dp")
    return lax.ppermute(block, "dp", [(i, i ^ k) for i in range(count)])


def core_swap(block):
    count = lax.axis_size("fsdp")
    return lax.ppermute(block, "fsdp", [(i, i ^ 1) for i in range(count)])


def gather_near(block):
    return [block, dp_send(block, 1), dp_send(block, 2)]


def gather_far(near):
    _, one, two = near
    half = one.shape[0] // 2
    return [*near, jnp.concatenate([dp_send(one[:half], 2), dp_send(two[half:], 1)])]


def dp_gather(block):
    return gather_far(gather_near(block))


def dp_own(array, k):
    return lax.dynamic_index_in_dim(array, lax.axis_index("dp") ^ k, 0, keepdims=False)


def dp_exchange(array):
    count = lax.axis_size("dp")
    place = lax.axis_index("dp")
    got = jnp.stack([dp_own(array, 0)] + [dp_send(dp_own(array, k), k) for k in range(1, count)])
    return jnp.stack(
        [lax.dynamic_index_in_dim(got, place ^ a, 0, keepdims=False) for a in range(count)]
    )


def line_send(block, r):
    count = lax.axis_size("fsdp")
    return lax.ppermute(block, "fsdp", [(i, i ^ (2 * r)) for i in range(count)])


def line_gather(block):
    count = lax.axis_size("fsdp") // 2
    place = lax.axis_index("fsdp") // 2
    got = jnp.stack([block] + [line_send(block, r) for r in range(1, count)])
    return jnp.stack(
        [lax.dynamic_index_in_dim(got, place ^ a, 0, keepdims=False) for a in range(count)]
    )


def sum_of_squares(array):
    array = array.astype(jnp.float32)
    return jnp.sum(array * array)


def sum_over_core(term):
    return term + core_swap(term)


def sum_over_line(term):
    return term + sum(line_send(term, r) for r in range(1, lax.axis_size("fsdp") // 2))


def sum_over_dp(term):
    return term + sum(dp_send(term, k) for k in range(1, lax.axis_size("dp")))


def sum_everywhere(term):
    return sum_over_dp(sum_over_line(sum_over_core(term)))


def is_even():
    return lax.rem(lax.axis_index("fsdp"), 2) == 0


def sum_blocks(own, got):
    return [own[k].astype(jnp.float32) + got[k].astype(jnp.float32) for k in range(own.shape[0])]


def reduce_over_dp(summed):
    return [summed[0]] + [dp_send(bf16(summed[k]), k) for k in range(1, len(summed))]


def reduce_over_line(got):
    total = sum(block.astype(jnp.float32) for block in got)
    count = lax.axis_size("fsdp") // 2
    place = lax.axis_index("fsdp") // 2
    parts = total.reshape(count, -1, total.shape[1])
    shard = [lax.dynamic_index_in_dim(parts, place, 0, keepdims=False)]
    for r in range(1, count):
        part = lax.dynamic_index_in_dim(parts, place ^ r, 0, keepdims=False)
        shard.append(line_send(bf16(part), r))
    return shard


def total_shard(shard):
    return sum(block.astype(jnp.float32) for block in shard).T


def unpack_gradients(got, rows, columns):
    ranks, part, width = got.shape
    return got[:, :, :rows], got[:, :, rows:].reshape(ranks, part, -1, columns)


def column_slices(own, other, first, target, width, slices):
    for j in range(slices):
        mine = own(j)
        theirs = other(j)
        target[:, pl.ds(2 * j * width, width)] = jnp.where(first, mine, theirs)
        target[:, pl.ds((2 * j + 1) * width, width)] = jnp.where(first, theirs, mine)


def block_columns(ref, place, k, width):
    return ref[:, pl.ds(pl.multiple_of((place ^ k) * width, 128), width)]


def project_kernel(ranks, slices, *refs):
    info, tokens, gain, bias, cosine, sine = refs[:6]
    own = refs[6 : 6 + ranks]
    other = refs[6 + ranks : 6 + 2 * ranks]
    normed, queries, kv, proj = refs[6 + 2 * ranks :]
    place = info[0]
    first = info[1] == 0
    width = own[0].shape[1]
    step = own[0].shape[0] // slices
    part = QKV // (2 * slices)
    x = tokens[...].astype(jnp.float32)
    scale = lax.rsqrt(jnp.mean(x * x, axis=-1, keepdims=True) + NORM_EPS)
    normed[...] = bf16(x * scale * gain[...])

    def product(mats, j):
        return sum(
            dot_nt(block_columns(normed, place, k, width), mats[k][pl.ds(j * step, part), :])
            for k in range(ranks)
        )

    column_slices(
        lambda j: product(own, j), lambda j: product(other, j), first, proj, part, slices
    )
    for h in range(HEADS + KV_HEADS):
        cols = pl.ds(h * HEAD, HEAD)
        u = proj[:, cols] + bias[:, cols]
        turned = bf16(u * cosine[...] + pltpu.roll(u, HEAD // 2, 1) * sine[...])
        if h < HEADS:
            queries[:, cols] = turned
        else:
            kv[:, pl.ds((h - HEADS) * HEAD, HEAD)] = turned
    cols = pl.ds(D + KV_WIDTH, KV_WIDTH)
    kv[:, pl.ds(KV_WIDTH, KV_WIDTH)] = bf16(proj[:, cols] + bias[:, cols])


def score_bias(info, rows, ranks, target):
    place = info[0]
    length = info[2]
    query = place * rows + lax.broadcasted_iota(jnp.int32, (rows, rows), 1)
    for k in range(ranks):
        key = (place ^ k) * rows + lax.broadcasted_iota(jnp.int32, (rows, rows), 0)
        seen = (key <= query) & (key < length)
        target[pl.ds(k * rows, rows), :] = jnp.where(seen, 0.0, MASKED)


def attend_kernel(ranks, slices, *refs):
    info, tokens, gain, queries = refs[:4]
    kv = refs[4 : 4 + ranks]
    own = refs[4 + ranks : 4 + 2 * ranks]
    other = [refs[4 + 2 * ranks].at[k] for k in range(ranks)]
    attended, totals, middle, normed_again, bias, keys, values, values_t = refs[5 + 2 * ranks :]
    place = info[0]
    first = info[1] == 0
    rows = tokens.shape[0]
    width = own[0].shape[1]
    part = own[0].shape[0] // slices
    score_bias(info, rows, ranks, bias)
    for k in range(ranks):
        keys[pl.ds(k * rows, rows), :] = kv[k][:, pl.ds(0, KV_WIDTH)]
        values[pl.ds(k * rows, rows), :] = kv[k][:, pl.ds(KV_WIDTH, KV_WIDTH)]
    values_t[...] = values[...].T

    @pl.loop(0, HEADS, unroll=2)
    def _(h):
        cols = pl.ds(pl.multiple_of(h * HEAD, HEAD), HEAD)
        kv_cols = pl.ds(pl.multiple_of((h // GROUP) * HEAD, HEAD), HEAD)
        scores = dot_nt(keys[:, kv_cols], queries[:, cols]) * SCALE + bias[...]
        peak = jnp.max(scores, axis=0, keepdims=True)
        exponent = jnp.exp(scores - peak)
        total = jnp.sum(exponent, axis=0, keepdims=True)
        totals[pl.ds(h, 1), :] = peak + jnp.log(total)
        probs = bf16(exponent * (1.0 / total))
        attended[:, cols] = bf16(dot_nn(values_t[kv_cols, :], probs).T)

    def product(mats, j):
        return sum(
            dot_nt(block_columns(attended, place, k, width), mats[k][pl.ds(j * part, part), :])
            for k in range(ranks)
        )

    column_slices(
        lambda j: product(own, j), lambda j: product(other, j), first, middle, part, slices
    )
    total = middle[...] + tokens[...].astype(jnp.float32)
    middle[...] = total
    scale = lax.rsqrt(jnp.mean(total * total, axis=-1, keepdims=True) + NORM_EPS)
    normed_again[...] = bf16(total * scale * gain[...])


def attend_back_kernel(ranks, slices, *refs):
    info, middle, cotangent, gain, queries, totals = refs[:6]
    got = refs[6 : 6 + ranks]
    kv = refs[6 + ranks : 6 + 2 * ranks]
    own = refs[6 + 2 * ranks : 6 + 3 * ranks]
    other = [refs[6 + 3 * ranks].at[k] for k in range(ranks)]
    refs = refs[7 + 3 * ranks :]
    middle_cot, middle_low, gain_grad, query_cot = refs[:4]
    kv_cot = refs[4 : 4 + ranks]
    bias, keys, values, keys_t, attended_cot, key_sum, value_sum, low_own, low_other = refs[
        4 + ranks :
    ]
    place = info[0]
    first = info[1] == 0
    rows = middle.shape[0]
    width = own[0].shape[1]
    part = own[0].shape[0] // slices
    position = place * rows + lax.broadcasted_iota(jnp.int32, (rows, 1), 0)
    valid = jnp.where(position < info[2], 1.0, 0.0)
    cot = got[0][...].astype(jnp.float32)
    for k in range(1, ranks):
        cot = cot + got[k][...].astype(jnp.float32)
    v = middle[...]
    scale = lax.rsqrt(jnp.mean(v * v, axis=-1, keepdims=True) + NORM_EPS)
    n = v * scale
    gain_grad[...] = jnp.sum(cot * n, axis=0, keepdims=True)
    scaled = cot * gain[...]
    back = scale * (scaled - n * jnp.mean(scaled * n, axis=-1, keepdims=True))
    back = back + cotangent[...].astype(jnp.float32) * valid
    middle_cot[...] = back
    middle_low[...] = bf16(back)
    for j in range(slices):
        even = middle_low[:, pl.ds(2 * j * part, part)]
        odd = middle_low[:, pl.ds((2 * j + 1) * part, part)]
        low_own[:, pl.ds(j * part, part)] = jnp.where(first, even, odd)
        low_other[:, pl.ds(j * part, part)] = jnp.where(first, odd, even)
    for k in range(ranks):
        cols = pl.ds(pl.multiple_of((place ^ k) * width, 128), width)
        attended_cot[:, cols] = bf16(
            dot_nn(low_own[...], own[k][...]) + dot_nn(low_other[...], other[k][...])
        )
    score_bias(info, rows, ranks, bias)
    for k in range(ranks):
        keys[pl.ds(k * rows, rows), :] = kv[k][:, pl.ds(0, KV_WIDTH)]
        values[pl.ds(k * rows, rows), :] = kv[k][:, pl.ds(KV_WIDTH, KV_WIDTH)]
    keys_t[...] = keys[...].T
    key_sum[...] = jnp.zeros_like(key_sum)
    value_sum[...] = jnp.zeros_like(value_sum)

    @pl.loop(0, HEADS, unroll=2)
    def _(h):
        cols = pl.ds(pl.multiple_of(h * HEAD, HEAD), HEAD)
        kv_cols = pl.ds(pl.multiple_of((h // GROUP) * HEAD, HEAD), HEAD)
        query = queries[:, cols]
        out_cot = attended_cot[:, cols]
        scores = dot_nt(keys[:, kv_cols], query) * SCALE + bias[...]
        probs = jnp.exp(scores - totals[pl.ds(h, 1), :])
        probs_cot = dot_nt(values[:, kv_cols], out_cot)
        row_dot = jnp.sum(probs * probs_cot, axis=0, keepdims=True)
        scores_cot = bf16(probs * (probs_cot - row_dot))
        value_sum[:, kv_cols] += dot_nn(bf16(probs), out_cot)
        key_sum[:, kv_cols] += dot_nn(scores_cot, query)
        query_cot[:, cols] = dot_nn(keys_t[kv_cols, :], scores_cot).T * SCALE

    for k in range(ranks):
        at = pl.ds(k * rows, rows)
        kv_cot[k][:, pl.ds(0, KV_WIDTH)] = bf16(key_sum[at, :] * SCALE)
        kv_cot[k][:, pl.ds(KV_WIDTH, KV_WIDTH)] = bf16(value_sum[at, :])


def outer_kernel(ranks, slices, *refs):
    info, left, right, own, other, turned = refs
    place = info[0]
    parity = info[1]
    width = own.shape[2]
    part = own.shape[1] // slices
    turned[...] = right[...].T
    for k in range(ranks):
        block = block_columns(left, place, k, width)
        for j in range(slices):
            at = pl.ds(j * part, part)
            mine = pl.ds(pl.multiple_of((2 * j + parity) * part, 16), part)
            theirs = pl.ds(pl.multiple_of((2 * j + 1 - parity) * part, 16), part)
            own[k, at, :] = bf16(dot_nn(turned[mine, :], block))
            other[k, at, :] = bf16(dot_nn(turned[theirs, :], block))


def project_back_kernel(ranks, *refs):
    info, query_cot, cosine, sine = refs[:4]
    got = refs[4 : 4 + ranks]
    projected_low, bias_grad = refs[4 + ranks :]
    kv_cot = got[0][...].astype(jnp.float32)
    for k in range(1, ranks):
        kv_cot = kv_cot + got[k][...].astype(jnp.float32)
    for h in range(HEADS + 2 * KV_HEADS):
        cols = pl.ds(h * HEAD, HEAD)
        if h < HEADS:
            u = query_cot[:, cols]
        else:
            u = kv_cot[:, (h - HEADS) * HEAD : (h - HEADS + 1) * HEAD]
        if h < HEADS + KV_HEADS:
            u = u * cosine[...] + pltpu.roll(u * sine[...], HEAD // 2, 1)
        bias_grad[:, cols] = jnp.sum(u, axis=0, keepdims=True)
        projected_low[:, cols] = bf16(u)


def input_back_kernel(ranks, slices, *refs):
    info, projected_low, tokens, gain, middle_cot = refs[:5]
    own = refs[5 : 5 + ranks]
    other = refs[5 + ranks : 5 + 2 * ranks]
    input_grad, gain_grad, low_own, low_other, normed_cot = refs[5 + 2 * ranks :]
    place = info[0]
    first = info[1] == 0
    width = own[0].shape[1]
    step = own[0].shape[0] // slices
    part = QKV // (2 * slices)
    for j in range(slices):
        even = projected_low[:, pl.ds(2 * j * part, part)]
        odd = projected_low[:, pl.ds((2 * j + 1) * part, part)]
        low_own[:, pl.ds(j * part, part)] = jnp.where(first, even, odd)
        low_other[:, pl.ds(j * part, part)] = jnp.where(first, odd, even)
    for k in range(ranks):
        cols = pl.ds(pl.multiple_of((place ^ k) * width, 128), width)
        normed_cot[:, cols] = sum(
            dot_nn(low[:, pl.ds(j * part, part)], mats[k][pl.ds(j * step, part), :])
            for low, mats in ((low_own, own), (low_other, other))
            for j in range(slices)
        )
    x = tokens[...].astype(jnp.float32)
    scale = lax.rsqrt(jnp.mean(x * x, axis=-1, keepdims=True) + NORM_EPS)
    n = x * scale
    cot = normed_cot[...]
    gain_grad[...] = jnp.sum(cot * n, axis=0, keepdims=True)
    scaled = cot * gain[...]
    back = scale * (scaled - n * jnp.mean(scaled * n, axis=-1, keepdims=True))
    input_grad[...] = bf16(middle_cot[...] + back)


def finish_kernel(info, *refs):
    *terms, grad, small, squares = refs
    total = terms[0][...].astype(jnp.float32)
    for term in terms[1:]:
        total = total + term[...].astype(jnp.float32)
    columns = grad.shape[1]
    grad[...] = total[:columns].T
    small[...] = total[columns : columns + 1]
    squares[...] = jnp.sum(total * total, keepdims=True)


def send_kernel(ranks, info, w_in, w_down, *refs):
    outs = refs[:ranks]
    (turned,) = refs[ranks:]
    place = info[0]
    rows = w_in.shape[1]
    part = w_in.shape[0] // ranks
    columns = w_down.shape[0]
    for p in range(ranks):
        turned[p, :, pl.ds(0, rows)] = bf16(w_in[pl.ds(p * part, part), :])
        for s in range(w_down.shape[1] // (ranks * part)):
            source = w_down[:, pl.ds((s * ranks + p) * part, part)]
            turned[p, :, pl.ds(rows + s * columns, columns)] = bf16(source.T)
    for k in range(ranks):
        outs[k][...] = turned[place ^ k]


def place_kernel(chunks, ranks, info, *refs):
    got = refs[:ranks]
    outs = refs[ranks : ranks + len(chunks)]
    stacked, *lows = refs[ranks + len(chunks) :]
    place = info[0]
    rows = D // ranks
    for k in range(ranks):
        stacked[k] = got[k][...]
    for chunk, out, low in zip(chunks, outs, lows):
        low[...] = jnp.zeros_like(low)
        if chunk.deep > chunk.real:
            out[...] = jnp.zeros_like(out)
    for a in range(ranks):
        start = 0
        for chunk, out, low in zip(chunks, outs, lows):
            each = chunk.slices // ranks
            piece = stacked[place ^ a, pl.ds(start, chunk.real), :]
            out[pl.ds(0, chunk.real), pl.ds(a * rows, rows)] = piece[:, :rows]
            for s in range(each):
                at = rows + s * chunk.columns
                turned = piece[:, at : at + chunk.columns].astype(jnp.float32).T
                for i in range(chunk.folds):
                    lane = i * chunk.wide + (a * each + s) * chunk.deep
                    low[:, pl.ds(lane, chunk.real)] = turned[i * chunk.low : (i + 1) * chunk.low]
            start += chunk.real
    for chunk, out, low in zip(chunks, outs, lows):
        out[pl.ds(chunk.deep, chunk.low), :] = bf16(low[...])


def pack_kernel(chunk, ranks, info, shard, *refs):
    outs = refs[:ranks]
    squares, turned = refs[ranks:]
    place = info[0]
    block = D // ranks
    each = chunk.slices // ranks
    rows = shard[pl.ds(0, chunk.real), :].astype(jnp.float32)
    total = jnp.sum(rows * rows, keepdims=True)
    low = shard[pl.ds(chunk.deep, chunk.low), :].astype(jnp.float32)
    for s in range(chunk.slices):
        for i in range(chunk.folds):
            start = i * chunk.wide + s * chunk.deep
            part = low[:, start : start + chunk.real]
            total = total + jnp.sum(part * part, keepdims=True)
            at = (s % each) * chunk.columns + i * chunk.low
            turned[s // each, :, pl.ds(at, chunk.low)] = part.T
    squares[...] = total
    for k in range(ranks):
        cols = pl.ds(pl.multiple_of((place ^ k) * block, 128), block)
        outs[k][:, pl.ds(0, block)] = shard[pl.ds(0, chunk.real), cols]
        outs[k][:, pl.ds(block, each * chunk.columns)] = bf16(turned[place ^ k])


def call(kernel, args, outs, scratch, micros):
    vmem = pl.BlockSpec(memory_space=pltpu.VMEM)
    moved = sum(math.prod(a.shape) * a.dtype.itemsize for a in args)
    moved += sum(math.prod(a.shape) * a.dtype.itemsize for a in outs)
    moved *= min(micros, 1)
    return pl.pallas_call(
        kernel,
        out_shape=tuple(outs),
        in_specs=[pl.BlockSpec(memory_space=pltpu.SMEM)] + [vmem] * (len(args) - 1),
        out_specs=(vmem,) * len(outs),
        scratch_shapes=scratch,
        compiler_params=pltpu.CompilerParams(vmem_limit_bytes=VMEM_LIMIT),
        cost_estimate=pl.CostEstimate(
            flops=micros * FLOPS_PER_MICRO, bytes_accessed=moved, transcendentals=0
        ),
    )(*args)


def f32_like(*shape):
    return jax.ShapeDtypeStruct(shape, jnp.float32)


def bf16_like(*shape):
    return jax.ShapeDtypeStruct(shape, jnp.bfloat16)


class Chunk:
    def __init__(self, size, lines):
        self.lines = lines
        self.slices = lines // 2
        self.real = size // self.slices
        self.deep = -(-self.real // 16) * 16
        self.units = self.slices * self.deep
        self.wide = -(-self.units // 128) * 128
        self.columns = D // lines
        self.folds = D // self.wide if self.columns * self.wide % (16 * D) == 0 else 1
        self.low = self.columns // self.folds
        self.step = self.deep + self.low
        self.rows = lines * self.step
        self.blocks = [
            (s, min(UNIT_TILE, self.units - s)) for s in range(0, self.units, UNIT_TILE)
        ]

    def in_parts(self, s, n, half):
        parts = []
        at = s
        while at < s + n:
            k = at // self.deep
            count = min(s + n, (k + 1) * self.deep) - at
            line = half * self.slices + k
            parts.append((at - s, count, line * self.step + at - k * self.deep))
            at += count
        return parts

    def down_parts(self, s, n):
        width = min(self.wide, s + UNIT_TILE) - s
        return [
            (
                line * self.columns + i * self.low,
                line * self.step + self.deep,
                i * self.wide + s,
                width,
            )
            for line in range(self.lines)
            for i in range(self.folds)
        ]


class Copies:
    def __init__(self, sems):
        self.sems = sems
        self.used = 0

    def start(self, source, target):
        copy = pltpu.make_async_copy(source, target, self.sems.at[self.used])
        self.used += 1
        copy.start()
        return copy


def wait_all(copies):
    for copy in copies:
        copy.wait()


def transpose_tokens(source, target, tokens):
    @pl.loop(0, tokens // TURN_TILE)
    def _(t):
        at = pl.multiple_of(t * TURN_TILE, TURN_TILE)
        target[:, pl.ds(at, TURN_TILE)] = source[pl.ds(at, TURN_TILE), :].T


def load_tokens(blocks, target, copies):
    rows = blocks[0].shape[0]
    return [
        copies.start(block, target.at[pl.ds(k * rows, rows)]) for k, block in enumerate(blocks)
    ]


def load_chunk(chunk, ranks, na_in, oc_in, weights, na, oc, w, d, copies):
    first = load_tokens(na_in, na, copies)
    block_copies = []
    for b, (s, n) in enumerate(chunk.blocks):
        mine = []
        for half in range(2):
            for offset, count, row in chunk.in_parts(s, n, half):
                target = w.at[pl.ds(half * chunk.units + s + offset, count)]
                mine.append(copies.start(weights.at[pl.ds(row, count)], target))
        if b == 0:
            first += load_tokens(oc_in, oc, copies)
        for column, row, at, width in chunk.down_parts(s, n):
            source = weights.at[pl.ds(row, chunk.low), pl.ds(at, width)]
            target = d.at[pl.ds(column, chunk.low), pl.ds(s, width)]
            mine.append(copies.start(source, target))
        block_copies.append(mine)
    return first, block_copies


def store_in(chunk, s, n, half, dw, at, weights_out, copies):
    return [
        copies.start(dw.at[pl.ds(at + offset, count)], weights_out.at[pl.ds(row, count)])
        for offset, count, row in chunk.in_parts(s, n, half)
    ]


def store_down(chunk, s, n, dd, at, weights_out, copies):
    return [
        copies.start(
            dd.at[pl.ds(column, chunk.low), pl.ds(at, width)],
            weights_out.at[pl.ds(row, chunk.low), pl.ds(place, width)],
        )
        for column, row, place, width in chunk.down_parts(s, n)
    ]


def copy_count(chunk):
    parts = sum(len(chunk.in_parts(s, n, 0)) for s, n in chunk.blocks)
    return 2 * parts + len(chunk.blocks) * chunk.lines * chunk.folds


def unit_block(units, s, n, tokens, na, oc, w, d, back, mixed, gt, ut, ht, at_row, add, final):
    wg = w.at[pl.ds(s, n)]
    wu = w.at[pl.ds(units + s, n)]
    db = d.at[:, pl.ds(s, n)]

    @pl.loop(0, tokens // TOKEN_TILE)
    def _(t):
        at = pl.ds(pl.multiple_of(t * TOKEN_TILE, TOKEN_TILE), TOKEN_TILE)
        gate = dot_nt(na[at, :], wg[...])
        up = dot_nt(na[at, :], wu[...])
        hidden_cot = dot_nn(oc[at, :], db[...])
        sigmoid = 1.0 / (1.0 + jnp.exp(-gate))
        activated = gate * sigmoid
        hidden = bf16(activated * up)
        gate_cot = bf16(hidden_cot * up * sigmoid * (1.0 + gate * (1.0 - sigmoid)))
        up_cot = bf16(hidden_cot * activated)
        ht[pl.ds(at_row, n), at] = hidden.T
        gt[pl.ds(at_row, n), at] = gate_cot.T
        ut[pl.ds(at_row, n), at] = up_cot.T
        back_term = dot_nn(gate_cot, wg[...]) + dot_nn(up_cot, wu[...])
        mixed_term = dot_nt(hidden, db[...])
        if add:
            back_term = back_term + back[at, :]
            mixed_term = mixed_term + mixed[at, :]
        if final:
            na[at, :] = bf16(back_term)
            oc[at, :] = bf16(mixed_term)
        else:
            back[at, :] = back_term
            mixed[at, :] = mixed_term


def gradient_block(n, na, oc_t, gt, ut, ht, at_row, dw, dw_gate, dw_up, dd, dd_at):
    at = pl.ds(at_row, n)

    @pl.loop(0, D // GRAD_TILE)
    def _(j):
        cols = pl.ds(pl.multiple_of(j * GRAD_TILE, GRAD_TILE), GRAD_TILE)
        dw[pl.ds(dw_gate, n), cols] = bf16(dot_nn(gt[at, :], na[:, cols]))
        dw[pl.ds(dw_up, n), cols] = bf16(dot_nn(ut[at, :], na[:, cols]))
        dd[cols, pl.ds(dd_at, n)] = bf16(dot_nt(oc_t[cols, :], ht[at, :]))


def first_chunk_kernel(chunk, ranks, carried, *refs):
    na_in = refs[:ranks]
    oc_in = refs[ranks : 2 * ranks]
    weights = refs[2 * ranks]
    refs = refs[2 * ranks + 1 :]
    if carried:
        back_in, mixed_in = refs[:2]
        refs = refs[2:]
    back_out, mixed_out, weights_out = refs[:3]
    na, oc, oc_t, w, d, dw, dd, back, mixed, gt, ut, ht, in_sem, out_sem = refs[3:]
    tokens = na.shape[0]
    copies = Copies(in_sem)
    first, block_copies = load_chunk(chunk, ranks, na_in, oc_in, weights, na, oc, w, d, copies)
    if carried:
        first.append(copies.start(back_in, back))
        first.append(copies.start(mixed_in, mixed))
    wait_all(first)
    transpose_tokens(oc, oc_t, tokens)
    copies = Copies(out_sem)
    outs = []
    stored = []
    for b, (s, n) in enumerate(chunk.blocks):
        wait_all(block_copies[b])
        add = carried or bool(b)
        unit_block(
            chunk.units, s, n, tokens, na, oc, w, d, back, mixed, gt, ut, ht, 0, add, False
        )
        if b == len(chunk.blocks) - 1:
            outs.append(copies.start(back, back_out))
            outs.append(copies.start(mixed, mixed_out))
        wait_all(stored)
        gradient_block(n, na, oc_t, gt, ut, ht, 0, dw, 0, UNIT_TILE, dd, 0)
        stored = store_in(chunk, s, n, 0, dw, 0, weights_out, copies)
        stored += store_in(chunk, s, n, 1, dw, UNIT_TILE, weights_out, copies)
        stored += store_down(chunk, s, n, dd, 0, weights_out, copies)
    wait_all(outs + stored)


def last_chunk_kernel(chunk, ranks, carried, start, *refs):
    na_in = refs[:ranks]
    oc_in = refs[ranks : 2 * ranks]
    weights = refs[2 * ranks]
    refs = refs[2 * ranks + 1 :]
    if carried:
        back_in, mixed_in = refs[:2]
        refs = refs[2:]
    back_out = refs[:ranks]
    mixed_out = refs[ranks : 2 * ranks]
    kept_out = refs[2 * ranks : 2 * ranks + 3]
    na, oc, w, d, back, mixed, gt, ut, ht, in_sem, out_sem = refs[2 * ranks + 3 :]
    tokens = na.shape[0]
    rows = tokens // ranks
    copies = Copies(in_sem)
    first, block_copies = load_chunk(chunk, ranks, na_in, oc_in, weights, na, oc, w, d, copies)
    if carried:
        at = pl.ds(start * rows, tokens)
        first.append(copies.start(back_in.at[at], back))
        first.append(copies.start(mixed_in.at[at], mixed))
    wait_all(first)
    copies = Copies(out_sem)
    outs = []
    for b, (s, n) in enumerate(chunk.blocks):
        wait_all(block_copies[b])
        unit_block(
            chunk.units,
            s,
            n,
            tokens,
            na,
            oc,
            w,
            d,
            back,
            mixed,
            gt,
            ut,
            ht,
            s,
            carried or bool(b),
            b == len(chunk.blocks) - 1,
        )
        for kept, target in zip((gt, ut, ht), kept_out):
            at = pl.ds(s, n)
            outs.append(copies.start(kept.at[at], target.at[at]))
    for k in range(ranks):
        at = pl.ds(k * rows, rows)
        outs.append(copies.start(na.at[at], back_out[k]))
        outs.append(copies.start(oc.at[at], mixed_out[k]))
    wait_all(outs)


def gradient_kernel(chunk, ranks, *refs):
    na_in = refs[:ranks]
    oc_in = refs[ranks : 2 * ranks]
    kept_in = refs[2 * ranks : 2 * ranks + 6]
    weights_out, na, oc, oc_t, gt, ut, ht, dw, dd, in_sem, out_sem = refs[2 * ranks + 6 :]
    tokens = na.shape[0]
    copies = Copies(in_sem)
    first = load_tokens(oc_in, oc, copies)
    later = load_tokens(na_in, na, copies)
    half = tokens // 2
    for i, source in enumerate(kept_in):
        kept = (gt, ut, ht)[i % 3].at[:, pl.ds(i // 3 * half, half)]
        later.append(copies.start(source, kept))
    wait_all(first)
    transpose_tokens(oc, oc_t, tokens)
    if chunk.wide > chunk.units:
        spare = chunk.wide - chunk.units
        dd[:, pl.ds(chunk.units, spare)] = jnp.zeros((D, spare), jnp.bfloat16)
    wait_all(later)
    copies = Copies(out_sem)
    outs = []
    for s, n in chunk.blocks:
        gradient_block(n, na, oc_t, gt, ut, ht, s, dw, s, chunk.units + s, dd, s)
        outs += store_in(chunk, s, n, 0, dw, s, weights_out, copies)
        outs += store_in(chunk, s, n, 1, dw, chunk.units + s, weights_out, copies)
        outs += store_down(chunk, s, n, dd, s, weights_out, copies)
    wait_all(outs)


def hbm_call(kernel, args, outs, scratch, micros):
    moved = sum(math.prod(a.shape) * a.dtype.itemsize for a in args)
    moved += sum(math.prod(a.shape) * a.dtype.itemsize for a in outs)
    anywhere = pl.BlockSpec(memory_space=pl.ANY)
    return pl.pallas_call(
        kernel,
        out_shape=tuple(outs),
        in_specs=[anywhere] * len(args),
        out_specs=(anywhere,) * len(outs),
        scratch_shapes=scratch,
        compiler_params=pltpu.CompilerParams(vmem_limit_bytes=VMEM_LIMIT),
        cost_estimate=pl.CostEstimate(
            flops=micros * FLOPS_PER_MICRO, bytes_accessed=moved, transcendentals=0
        ),
    )(*args)


def vmem_bf16(*shape):
    return pltpu.VMEM(shape, jnp.bfloat16)


def vmem_f32(*shape):
    return pltpu.VMEM(shape, jnp.float32)


def first_chunk(chunk, na, oc, weights, carry):
    ranks = len(na)
    tokens = ranks * na[0].shape[0]
    scratch = [
        vmem_bf16(tokens, D),
        vmem_bf16(tokens, D),
        vmem_bf16(D, tokens),
        vmem_bf16(2 * chunk.units, D),
        vmem_bf16(D, chunk.wide),
        vmem_bf16(2 * UNIT_TILE, D),
        vmem_bf16(D, UNIT_TILE),
        vmem_f32(tokens, D),
        vmem_f32(tokens, D),
        vmem_bf16(UNIT_TILE, tokens),
        vmem_bf16(UNIT_TILE, tokens),
        vmem_bf16(UNIT_TILE, tokens),
        pltpu.SemaphoreType.DMA((2 * ranks + 2 + copy_count(chunk),)),
        pltpu.SemaphoreType.DMA((2 + copy_count(chunk),)),
    ]
    outs = [f32_like(tokens, D), f32_like(tokens, D), bf16_like(chunk.rows, D)]
    kernel = functools.partial(first_chunk_kernel, chunk, ranks, bool(carry))
    return hbm_call(kernel, [*na, *oc, weights, *carry], outs, scratch, 68)


def last_chunk(chunk, na, oc, weights, carry, start):
    ranks = len(na)
    rows = na[0].shape[0]
    tokens = ranks * rows
    scratch = [
        vmem_bf16(tokens, D),
        vmem_bf16(tokens, D),
        vmem_bf16(2 * chunk.units, D),
        vmem_bf16(D, chunk.wide),
        vmem_f32(tokens, D),
        vmem_f32(tokens, D),
        vmem_bf16(chunk.units, tokens),
        vmem_bf16(chunk.units, tokens),
        vmem_bf16(chunk.units, tokens),
        pltpu.SemaphoreType.DMA((2 * ranks + 2 + copy_count(chunk),)),
        pltpu.SemaphoreType.DMA((2 * ranks + 3 * len(chunk.blocks),)),
    ]
    outs = [bf16_like(rows, D)] * (2 * ranks) + [bf16_like(chunk.units, tokens)] * 3
    kernel = functools.partial(last_chunk_kernel, chunk, ranks, bool(carry), start)
    got = hbm_call(
        kernel, [*na, *oc, weights, *carry], outs, scratch, 20
    )
    return got[:ranks], got[ranks : 2 * ranks], got[2 * ranks :]


def chunk_gradients(chunk, na, oc, kept):
    ranks = len(na)
    tokens = ranks * na[0].shape[0]
    scratch = [
        vmem_bf16(tokens, D),
        vmem_bf16(tokens, D),
        vmem_bf16(D, tokens),
        vmem_bf16(chunk.units, tokens),
        vmem_bf16(chunk.units, tokens),
        vmem_bf16(chunk.units, tokens),
        vmem_bf16(2 * chunk.units, D),
        vmem_bf16(D, chunk.wide),
        pltpu.SemaphoreType.DMA((2 * ranks + 6,)),
        pltpu.SemaphoreType.DMA((copy_count(chunk),)),
    ]
    kernel = functools.partial(gradient_kernel, chunk, ranks)
    (terms,) = hbm_call(
        kernel,
        [*na, *oc, *kept],
        [bf16_like(chunk.rows, D)],
        scratch,
        16,
    )
    return terms


def sharded_pass(tokens, cotangent, lengths, half_qkv, half_out, half_in, half_down, half_small):
    ranks = lax.axis_size("dp")
    lines = lax.axis_size("fsdp")
    place = lax.axis_index("dp")
    rows = tokens.shape[1]
    slices = lines // 2
    block = D // ranks
    inputs = tokens[0]
    info = jnp.stack([place, lax.rem(lax.axis_index("fsdp"), 2), lengths[0]])

    small_rows, small_columns = half_small.shape
    columns = half_qkv.shape[1]
    line = jnp.concatenate([half_qkv.T, half_out.T])
    line = scoped("matrix_line", line_gather, line)
    qkv_along = line[:, :columns].reshape(-1, block)
    out_along = line[:, columns:].reshape(-1, block)
    half_small, qkv_along = lax.optimization_barrier((half_small, qkv_along))
    small_line = scoped("small_gather", line_gather, half_small)
    small_other = scoped("small_gather", core_swap, small_line)
    small_line = jnp.stack(
        [
            jnp.where(is_even(), small_line, small_other),
            jnp.where(is_even(), small_other, small_line),
        ],
        axis=1,
    )
    small_line = small_line.reshape(lines, small_rows, small_columns)
    small_stack = jnp.stack(
        [small_line]
        + [scoped("small_gather", dp_send, small_line, k) for k in range(1, ranks)]
    )
    small_vec = jnp.stack(
        [
            lax.dynamic_index_in_dim(small_stack, place ^ a, 0, keepdims=False)
            for a in range(ranks)
        ]
    )
    small_vec = small_vec.transpose(0, 2, 1, 3).reshape(-1).astype(jnp.float32)
    gain_attn, gain_mlp, biases = unpack_small(small_vec)
    gain_attn = gain_attn[None]
    gain_mlp = gain_mlp[None]

    part = half_in.shape[1] // ranks
    width = block + D // ranks // 2
    sent = call(
        functools.partial(send_kernel, ranks),
        [info, half_in.T, half_down.T],
        [bf16_like(part, width)] * ranks,
        [vmem_bf16(ranks, part, width)],
        1,
    )
    got = [sent[0]] + [
        scoped("weights_exchange", dp_send, sent[k], k) for k in range(1, ranks)
    ]
    got, out_along, qkv_along = lax.optimization_barrier((got, out_along, qkv_along))
    qkv_own = scoped("qkv_gather", dp_gather, qkv_along)
    qkv_other = [scoped("qkv_swap", core_swap, block) for block in qkv_own]
    out_along, qkv_other = lax.optimization_barrier((out_along, qkv_other))
    out_near = scoped("out_gather", gather_near, out_along)

    chunks = [Chunk(size, lines) for size in CHUNKS]
    packed = call(
        functools.partial(place_kernel, chunks, ranks),
        [info, *got],
        [bf16_like(chunk.step, D) for chunk in chunks],
        [vmem_bf16(ranks, part, width)] + [vmem_f32(chunk.low, D) for chunk in chunks],
        1,
    )
    gathered = [lax.all_gather(array, "fsdp", axis=0, tiled=True) for array in packed]

    query_places = place * rows + jnp.arange(rows, dtype=jnp.int32)
    cosine, sine = rope_tables(query_places.astype(jnp.float32))
    sine = jnp.where(jnp.arange(HEAD) < HEAD // 2, -sine, sine)
    normed, queries, kv = call(
        functools.partial(project_kernel, ranks, slices),
        [info, inputs, gain_attn, biases[None], cosine, sine, *qkv_own, *qkv_other],
        [bf16_like(rows, D), bf16_like(rows, D), bf16_like(rows, 2 * KV_WIDTH)],
        [vmem_f32(rows, QKV)],
        7,
    )
    kv, out_near = lax.optimization_barrier((kv, out_near))
    out_own = scoped("out_gather", gather_far, out_near)
    kv_blocks = scoped("kv_gather", dp_gather, kv)
    out_other = scoped("out_swap", core_swap, jnp.stack(out_own))

    valid = query_places < lengths[0]
    out_cot = jnp.where(valid[:, None], cotangent[0], jnp.zeros_like(cotangent[0]))
    out_cot, *kv_blocks = lax.optimization_barrier((out_cot, *kv_blocks))
    cot_blocks = scoped("cot_gather", dp_gather, out_cot)

    attended, totals, middle, normed_again = call(
        functools.partial(attend_kernel, ranks, slices),
        [info, inputs, gain_mlp, queries, *kv_blocks, *out_own, out_other],
        [bf16_like(rows, D), f32_like(16, rows), f32_like(rows, D), bf16_like(rows, D)],
        [
            vmem_f32(ranks * rows, rows),
            vmem_bf16(ranks * rows, KV_WIDTH),
            vmem_bf16(ranks * rows, KV_WIDTH),
            vmem_bf16(KV_WIDTH, ranks * rows),
        ],
        24,
    )
    normed_blocks = scoped("normed_gather", dp_gather, normed_again)

    *before, end = zip(chunks, gathered)
    carry = ()
    terms = []
    for chunk, weights in before:
        back, mixed, term = first_chunk(chunk, normed_blocks, cot_blocks, weights, carry)
        carry = (back, mixed)
        terms.append(term)
    chunk, weights = end
    half = ranks // 2
    far_back, far_mixed, far_kept = last_chunk(
        chunk, normed_blocks[half:], cot_blocks[half:], weights, carry, half
    )
    far_got = [scoped("back_reduce", dp_send, far_back[k - half], k) for k in range(half, ranks)]
    near_cot, far_back = lax.optimization_barrier((cot_blocks[:half], far_back))
    near_back, near_mixed, near_kept = last_chunk(
        chunk, normed_blocks[:half], near_cot, weights, carry, 0
    )
    back_got = [scoped("back_reduce", dp_send, near_back[k], k) for k in range(1, half)] + far_got
    back_blocks = near_back
    mixed_blocks = [*near_mixed, *far_mixed]
    kept = [*near_kept, *far_kept]
    term = chunk_gradients(chunk, normed_blocks, cot_blocks, kept)
    term, back_blocks, back_got, mixed_blocks = lax.optimization_barrier(
        (term, back_blocks, back_got, mixed_blocks)
    )
    terms.append(term)
    first_shard = lax.psum_scatter(terms[0], "fsdp", scatter_dimension=0, tiled=True)

    def pack_chunk(chunk, shard):
        width = block + D // ranks // 2
        *sent, squares = call(
            functools.partial(pack_kernel, chunk, ranks),
            [info, shard],
            [bf16_like(chunk.real, width)] * ranks + [f32_like(1, 1)],
            [vmem_f32(ranks, chunk.real, width - block)],
            0,
        )
        return sent, squares[0, 0]

    def exchange_chunk(sent):
        got = sent[:1] + [scoped("gradient_exchange", dp_send, sent[k], k) for k in range(1, ranks)]
        return got

    def place_chunk(got):
        stacked = jnp.stack(got)
        ordered = jnp.stack(
            [
                lax.dynamic_index_in_dim(stacked, place ^ a, 0, keepdims=False)
                for a in range(ranks)
            ]
        )
        return unpack_gradients(ordered, half_in.shape[0], half_down.shape[1])

    mixed_got = [scoped("mixed_reduce", dp_send, mixed_blocks[k], k) for k in range(1, ranks - 1)]
    middle_cot, middle_low, gain_mlp_grad, query_cot, *kv_cot = call(
        functools.partial(attend_back_kernel, ranks, slices),
        [
            info,
            middle,
            out_cot,
            gain_mlp,
            queries,
            totals,
            back_blocks[0],
            *back_got,
            *kv_blocks,
            *out_own,
            out_other,
        ],
        [f32_like(rows, D), bf16_like(rows, D), f32_like(1, D), f32_like(rows, D)]
        + [bf16_like(rows, 2 * KV_WIDTH)] * ranks,
        [
            vmem_f32(ranks * rows, rows),
            vmem_bf16(ranks * rows, KV_WIDTH),
            vmem_bf16(ranks * rows, KV_WIDTH),
            vmem_bf16(KV_WIDTH, ranks * rows),
            vmem_bf16(rows, D),
            vmem_f32(ranks * rows, KV_WIDTH),
            vmem_f32(ranks * rows, KV_WIDTH),
            vmem_bf16(rows, D // 2),
            vmem_bf16(rows, D // 2),
        ],
        31,
    )

    def outer(left, right):
        columns = right.shape[1]
        return call(
            functools.partial(outer_kernel, ranks, slices),
            [info, left, right],
            [bf16_like(ranks, columns // 2, block)] * 2,
            [vmem_bf16(columns, rows)],
            0,
        )

    kv_cot, middle_low, mixed_got = lax.optimization_barrier((kv_cot, middle_low, mixed_got))
    kv_got = [scoped("kv_reduce", dp_send, kv_cot[k], k) for k in range(1, ranks)]
    out_own_term, out_other_term = outer(attended, middle_low)


    kv_got, out_own_term, out_other_term = lax.optimization_barrier(
        (kv_got, out_own_term, out_other_term)
    )
    out_swapped = scoped("out_core", core_swap, out_other_term)
    projected_low, bias_grad = call(
        functools.partial(project_back_kernel, ranks),
        [info, query_cot, cosine, sine, kv_cot[0], *kv_got],
        [bf16_like(rows, QKV), f32_like(1, QKV)],
        [],
        0,
    )
    out_sums = sum_blocks(out_own_term, out_swapped)
    out_sums = [out_sums[0]] + [bf16(total) for total in out_sums[1:]]
    projected_low, out_sums = lax.optimization_barrier((projected_low, out_sums))
    out_got = scoped("out_dp", reduce_over_dp, out_sums)
    qkv_own_term, qkv_other_term = outer(normed, projected_low)

    qkv_own_term, qkv_other_term, projected_low = lax.optimization_barrier(
        (qkv_own_term, qkv_other_term, projected_low)
    )
    qkv_swapped = scoped("qkv_core", core_swap, qkv_other_term)
    input_grad, gain_attn_grad = call(
        functools.partial(input_back_kernel, ranks, slices),
        [info, projected_low, inputs, gain_attn, middle_cot, *qkv_own, *qkv_other],
        [bf16_like(rows, D), f32_like(1, D)],
        [vmem_bf16(rows, QKV // 2), vmem_bf16(rows, QKV // 2), vmem_f32(rows, D)],
        0,
    )

    gain_attn_grad, first_shard, last_term, out_got[1:3] = lax.optimization_barrier(
        (gain_attn_grad, first_shard, terms[1], out_got[1:3])
    )
    last_shard = lax.psum_scatter(last_term, "fsdp", scatter_dimension=0, tiled=True)
    small_term = group_small(gain_attn_grad[0], gain_mlp_grad[0], bias_grad[0])
    small_term = small_term.reshape(ranks, small_rows, slices, 2, small_columns)
    small_term = small_term.transpose(3, 0, 2, 1, 4).reshape(2, ranks, slices, -1)
    small_parity = lax.rem(lax.axis_index("fsdp"), 2)
    small_own = lax.dynamic_index_in_dim(small_term, small_parity, 0, keepdims=False)
    small_other = lax.dynamic_index_in_dim(small_term, 1 - small_parity, 0, keepdims=False)
    small_sums = small_own + scoped("small_core", core_swap, small_other)

    qkv_swapped, out_got, small_sums, first_shard = lax.optimization_barrier(
        (qkv_swapped, out_got, small_sums, first_shard)
    )
    small_rest = ((0, 0), (0, 15), (0, block - small_sums.shape[2]))
    qkv_sums = []
    for k, total in enumerate(sum_blocks(qkv_own_term, qkv_swapped)):
        extra = jnp.pad(dp_own(small_sums, k)[:, None], small_rest)
        total = jnp.concatenate([total.reshape(slices, -1, block), extra], axis=1)
        qkv_sums.append(total.reshape(-1, block))
    qkv_got = scoped("qkv_dp", reduce_over_dp, qkv_sums)
    out_shard = scoped("out_line", reduce_over_line, out_got)
    first_sent, squares = pack_chunk(chunks[0], first_shard)

    qkv_got, out_shard, squares, first_sent = lax.optimization_barrier(
        (qkv_got, out_shard, squares, first_sent)
    )
    qkv_shard = scoped("qkv_line", reduce_over_line, qkv_got)
    out_grad = total_shard(out_shard)
    squares = squares + sum_of_squares(out_grad)
    first_got = exchange_chunk(first_sent)
    mixed_last, first_got = lax.optimization_barrier((mixed_blocks[-1], first_got))
    mixed_got.append(scoped("mixed_reduce", dp_send, mixed_last, ranks - 1))

    qkv_shard, squares, last_shard, first_got = lax.optimization_barrier(
        (qkv_shard, squares, last_shard, first_got)
    )
    last_sent, last_squares = pack_chunk(chunks[1], last_shard)
    last_got = exchange_chunk(last_sent)
    qkv_grad, small_row, qkv_squares = call(
        finish_kernel,
        [info, *qkv_shard],
        [f32_like(block, columns), f32_like(1, block), f32_like(1, 1)],
        [],
        0,
    )
    squares = squares + last_squares + qkv_squares[0, 0]
    squares, last_got[1], mixed_got = lax.optimization_barrier((squares, last_got[1], mixed_got))
    total_squares = scoped("norm_sum", sum_everywhere, squares)
    small_grad = small_row[0, : small_rows * small_columns]
    small_grad = small_grad.reshape(small_rows, small_columns)
    in_first, down_first = place_chunk(first_got)
    in_last, down_last = place_chunk(last_got)
    in_grad = jnp.concatenate([in_first, in_last], axis=1)
    in_grad = in_grad.transpose(2, 0, 1).reshape(half_in.shape)
    down_grad = jnp.concatenate([down_first, down_last], axis=1)
    down_grad = down_grad.transpose(2, 0, 1, 3).reshape(half_down.shape)
    in_grad, down_grad = lax.optimization_barrier((in_grad, down_grad))
    in_grad = in_grad.astype(jnp.float32)
    down_grad = down_grad.astype(jnp.float32)
    mixed = middle + mixed_blocks[0].astype(jnp.float32)
    for got in mixed_got:
        mixed = mixed + got.astype(jnp.float32)
    mixed = bf16(mixed)
    return (mixed, input_grad, total_squares, qkv_grad, out_grad, in_grad, down_grad, small_grad)


def per_device(
    tokens,
    cotangent,
    lengths,
    qkv_weight,
    qkv_first,
    qkv_second,
    out_weight,
    out_first,
    out_second,
    mlp_in_weight,
    mlp_in_first,
    mlp_in_second,
    down_weight,
    down_first,
    down_second,
    small_params,
    small_first,
    small_second,
):
    results = sharded_pass(
        tokens,
        cotangent,
        lengths,
        bf16(qkv_weight),
        bf16(out_weight),
        mlp_in_weight,
        down_weight,
        bf16(small_params),
    )
    mixed, input_cot, total_squares, qkv_grad, out_grad, in_grad, down_grad, small_grad = results
    grad_norm = jnp.sqrt(total_squares)
    clip_factor = CLIP_NORM / jnp.maximum(grad_norm, CLIP_NORM)
    outs = [mixed[None], input_cot[None], grad_norm]
    for weight, first, second, gradient, rate, decay in (
        (qkv_weight, qkv_first, qkv_second, qkv_grad, MATRIX_RATE, MATRIX_DECAY),
        (out_weight, out_first, out_second, out_grad, MATRIX_RATE, MATRIX_DECAY),
        (mlp_in_weight, mlp_in_first, mlp_in_second, in_grad, MATRIX_RATE, MATRIX_DECAY),
        (down_weight, down_first, down_second, down_grad, MATRIX_RATE, MATRIX_DECAY),
        (small_params, small_first, small_second, small_grad, SMALL_RATE, 0.0),
    ):
        outs.extend(update(weight, first, second, gradient, clip_factor, rate, decay))
    return tuple(outs)


def solution(mesh):
    rows = P("fsdp", "dp", None)
    shard = P("dp", "fsdp")
    return jax.shard_map(
        per_device,
        mesh=mesh,
        in_specs=(rows, rows, P("fsdp")) + (shard,) * 15,
        out_specs=(rows, rows, P()) + (shard,) * 20,
        check_vma=False,
    )
```

```python
import functools
import math

import jax
import jax.numpy as jnp
from jax import lax
from jax.experimental import pallas as pl
from jax.experimental.pallas import tpu as pltpu
from jax.sharding import PartitionSpec as P

D = 1536
HEADS = 12
KV_HEADS = 2
HEAD = 128
FF = 8960
STEP = 5
GROUP = 6
SMALL = 5120
QKV = 2048
KV_WIDTH = KV_HEADS * HEAD


NORM_EPS = 1e-06
ROPE_BASE = 1000000.0
BETA_FIRST = 0.5
BETA_SECOND = 0.5
ADAM_EPS = 1e-08
MATRIX_RATE = 0.03
SMALL_RATE = 0.3
MATRIX_DECAY = 0.1
CLIP_NORM = 1.0
MASKED = -1e30
SCALE = HEAD ** (-0.5)
CHUNKS = (1536, 704)
UNIT_TILE = 512
TOKEN_TILE = 640
GRAD_TILE = 512
TURN_TILE = 256
VMEM_LIMIT = 60 * 2**20
FLOPS_PER_MICRO = 1_150_000_000


def unpack_small(small_vec):
    grouped = small_vec.reshape(KV_HEADS * HEAD, 3 * GROUP + 2)
    gain_attn = grouped[:, :GROUP].reshape(-1)
    gain_mlp = grouped[:, GROUP : 2 * GROUP].reshape(-1)
    biases = jnp.concatenate(
        [
            grouped[:, 2 * GROUP : 3 * GROUP].reshape(-1),
            grouped[:, 3 * GROUP],
            grouped[:, 3 * GROUP + 1],
        ]
    )
    return (gain_attn, gain_mlp, biases)


def group_small(gain_attn, gain_mlp, biases):
    count = KV_HEADS * HEAD
    pieces = [
        gain_attn.reshape(count, GROUP),
        gain_mlp.reshape(count, GROUP),
        biases[:D].reshape(count, GROUP),
        biases[D : D + count][:, None],
        biases[D + count :][:, None],
    ]
    return jnp.concatenate(pieces, axis=1).reshape(8, SMALL // 8)


def rope_tables(positions):
    pair_index = jnp.arange(HEAD // 2, dtype=jnp.float32)
    inverse = jnp.power(jnp.float32(ROPE_BASE), -2.0 * pair_index / HEAD)
    angles = positions[:, None] * inverse[None, :]
    angles = jnp.concatenate([angles, angles], axis=-1)
    return (jnp.cos(angles), jnp.sin(angles))


def bf16(array):
    return array.astype(jnp.bfloat16)


def scoped(name, function, *args):
    with jax.named_scope(name):
        return function(*args)


def dot_nn(left, right):
    return jnp.dot(left, right, preferred_element_type=jnp.float32)


def dot_nt(left, right):
    return lax.dot_general(
        left, right, (((1,), (1,)), ((), ())), preferred_element_type=jnp.float32
    )


def dot_tn(left, right):
    return lax.dot_general(
        left, right, (((0,), (0,)), ((), ())), preferred_element_type=jnp.float32
    )


def update(weight, first, second, gradient, clip_factor, rate, decay):
    step_grad = gradient * clip_factor
    first_new = BETA_FIRST * first + (1.0 - BETA_FIRST) * step_grad
    second_new = BETA_SECOND * second + (1.0 - BETA_SECOND) * step_grad * step_grad
    first_fix = 1.0 - BETA_FIRST**STEP
    second_fix = 1.0 - BETA_SECOND**STEP
    weight_new = weight - rate * (
        first_new / first_fix / (jnp.sqrt(second_new / second_fix) + ADAM_EPS) + decay * weight
    )
    return (weight_new, first_new, second_new, weight_new.astype(jnp.bfloat16))


def dp_send(block, k):
    count = lax.axis_size("dp")
    return lax.ppermute(block, "dp", [(i, i ^ k) for i in range(count)])


def core_swap(block):
    count = lax.axis_size("fsdp")
    return lax.ppermute(block, "fsdp", [(i, i ^ 1) for i in range(count)])


def gather_near(block):
    return [block, dp_send(block, 1), dp_send(block, 2)]


def gather_far(near):
    _, one, two = near
    half = one.shape[0] // 2
    return [*near, jnp.concatenate([dp_send(one[:half], 2), dp_send(two[half:], 1)])]


def dp_gather(block):
    return gather_far(gather_near(block))


def dp_own(array, k):
    return lax.dynamic_index_in_dim(array, lax.axis_index("dp") ^ k, 0, keepdims=False)


def dp_exchange(array):
    count = lax.axis_size("dp")
    place = lax.axis_index("dp")
    got = jnp.stack([dp_own(array, 0)] + [dp_send(dp_own(array, k), k) for k in range(1, count)])
    return jnp.stack(
        [lax.dynamic_index_in_dim(got, place ^ a, 0, keepdims=False) for a in range(count)]
    )


def line_send(block, r):
    count = lax.axis_size("fsdp")
    return lax.ppermute(block, "fsdp", [(i, i ^ (2 * r)) for i in range(count)])


def line_gather(block):
    count = lax.axis_size("fsdp") // 2
    place = lax.axis_index("fsdp") // 2
    got = jnp.stack([block] + [line_send(block, r) for r in range(1, count)])
    return jnp.stack(
        [lax.dynamic_index_in_dim(got, place ^ a, 0, keepdims=False) for a in range(count)]
    )


def sum_of_squares(array):
    array = array.astype(jnp.float32)
    return jnp.sum(array * array)


def sum_over_core(term):
    return term + core_swap(term)


def sum_over_line(term):
    return term + sum(line_send(term, r) for r in range(1, lax.axis_size("fsdp") // 2))


def sum_over_dp(term):
    return term + sum(dp_send(term, k) for k in range(1, lax.axis_size("dp")))


def sum_everywhere(term):
    return sum_over_dp(sum_over_line(sum_over_core(term)))


def is_even():
    return lax.rem(lax.axis_index("fsdp"), 2) == 0


def sum_blocks(own, got):
    return [own[k].astype(jnp.float32) + got[k].astype(jnp.float32) for k in range(own.shape[0])]


def reduce_over_dp(summed):
    return [summed[0]] + [dp_send(bf16(summed[k]), k) for k in range(1, len(summed))]


def reduce_over_line(got):
    total = sum(block.astype(jnp.float32) for block in got)
    count = lax.axis_size("fsdp") // 2
    place = lax.axis_index("fsdp") // 2
    parts = total.reshape(count, -1, total.shape[1])
    shard = [lax.dynamic_index_in_dim(parts, place, 0, keepdims=False)]
    for r in range(1, count):
        part = lax.dynamic_index_in_dim(parts, place ^ r, 0, keepdims=False)
        shard.append(line_send(bf16(part), r))
    return shard


def total_shard(shard):
    return sum(block.astype(jnp.float32) for block in shard).T


def unpack_gradients(got, rows, columns):
    ranks, part, width = got.shape
    return got[:, :, :rows], got[:, :, rows:].reshape(ranks, part, -1, columns)


def column_slices(own, other, first, target, width, slices):
    for j in range(slices):
        mine = own(j)
        theirs = other(j)
        target[:, pl.ds(2 * j * width, width)] = jnp.where(first, mine, theirs)
        target[:, pl.ds((2 * j + 1) * width, width)] = jnp.where(first, theirs, mine)


def block_columns(ref, place, k, width):
    return ref[:, pl.ds(pl.multiple_of((place ^ k) * width, 128), width)]


def project_kernel(ranks, slices, *refs):
    info, tokens, gain, bias, cosine, sine = refs[:6]
    own = refs[6 : 6 + ranks]
    other = refs[6 + ranks : 6 + 2 * ranks]
    normed, queries, kv, proj = refs[6 + 2 * ranks :]
    place = info[0]
    first = info[1] == 0
    width = own[0].shape[1]
    step = own[0].shape[0] // slices
    part = QKV // (2 * slices)
    x = tokens[...].astype(jnp.float32)
    scale = lax.rsqrt(jnp.mean(x * x, axis=-1, keepdims=True) + NORM_EPS)
    normed[...] = bf16(x * scale * gain[...])

    def product(mats, j):
        return sum(
            dot_nt(block_columns(normed, place, k, width), mats[k][pl.ds(j * step, part), :])
            for k in range(ranks)
        )

    column_slices(
        lambda j: product(own, j), lambda j: product(other, j), first, proj, part, slices
    )
    for h in range(HEADS + KV_HEADS):
        cols = pl.ds(h * HEAD, HEAD)
        u = proj[:, cols] + bias[:, cols]
        turned = bf16(u * cosine[...] + pltpu.roll(u, HEAD // 2, 1) * sine[...])
        if h < HEADS:
            queries[:, cols] = turned
        else:
            kv[:, pl.ds((h - HEADS) * HEAD, HEAD)] = turned
    cols = pl.ds(D + KV_WIDTH, KV_WIDTH)
    kv[:, pl.ds(KV_WIDTH, KV_WIDTH)] = bf16(proj[:, cols] + bias[:, cols])


def score_bias(info, rows, ranks, target):
    place = info[0]
    length = info[2]
    query = place * rows + lax.broadcasted_iota(jnp.int32, (rows, rows), 1)
    for k in range(ranks):
        key = (place ^ k) * rows + lax.broadcasted_iota(jnp.int32, (rows, rows), 0)
        seen = (key <= query) & (key < length)
        target[pl.ds(k * rows, rows), :] = jnp.where(seen, 0.0, MASKED)


def attend_kernel(ranks, slices, *refs):
    info, tokens, gain, queries = refs[:4]
    kv = refs[4 : 4 + ranks]
    own = refs[4 + ranks : 4 + 2 * ranks]
    other = [refs[4 + 2 * ranks].at[k] for k in range(ranks)]
    attended, totals, middle, normed_again, bias, keys, values, values_t = refs[5 + 2 * ranks :]
    place = info[0]
    first = info[1] == 0
    rows = tokens.shape[0]
    width = own[0].shape[1]
    part = own[0].shape[0] // slices
    score_bias(info, rows, ranks, bias)
    for k in range(ranks):
        keys[pl.ds(k * rows, rows), :] = kv[k][:, pl.ds(0, KV_WIDTH)]
        values[pl.ds(k * rows, rows), :] = kv[k][:, pl.ds(KV_WIDTH, KV_WIDTH)]
    values_t[...] = values[...].T

    @pl.loop(0, HEADS, unroll=2)
    def _(h):
        cols = pl.ds(pl.multiple_of(h * HEAD, HEAD), HEAD)
        kv_cols = pl.ds(pl.multiple_of((h // GROUP) * HEAD, HEAD), HEAD)
        scores = dot_nt(keys[:, kv_cols], queries[:, cols]) * SCALE + bias[...]
        peak = jnp.max(scores, axis=0, keepdims=True)
        exponent = jnp.exp(scores - peak)
        total = jnp.sum(exponent, axis=0, keepdims=True)
        totals[pl.ds(h, 1), :] = peak + jnp.log(total)
        probs = bf16(exponent * (1.0 / total))
        attended[:, cols] = bf16(dot_nn(values_t[kv_cols, :], probs).T)

    def product(mats, j):
        return sum(
            dot_nt(block_columns(attended, place, k, width), mats[k][pl.ds(j * part, part), :])
            for k in range(ranks)
        )

    column_slices(
        lambda j: product(own, j), lambda j: product(other, j), first, middle, part, slices
    )
    total = middle[...] + tokens[...].astype(jnp.float32)
    middle[...] = total
    scale = lax.rsqrt(jnp.mean(total * total, axis=-1, keepdims=True) + NORM_EPS)
    normed_again[...] = bf16(total * scale * gain[...])


def attend_back_kernel(ranks, slices, *refs):
    info, middle, cotangent, gain, queries, totals = refs[:6]
    got = refs[6 : 6 + ranks]
    kv = refs[6 + ranks : 6 + 2 * ranks]
    own = refs[6 + 2 * ranks : 6 + 3 * ranks]
    other = [refs[6 + 3 * ranks].at[k] for k in range(ranks)]
    refs = refs[7 + 3 * ranks :]
    middle_cot, middle_low, gain_grad, query_cot = refs[:4]
    kv_cot = refs[4 : 4 + ranks]
    bias, keys, values, keys_t, attended_cot, key_sum, value_sum, low_own, low_other = refs[
        4 + ranks :
    ]
    place = info[0]
    first = info[1] == 0
    rows = middle.shape[0]
    width = own[0].shape[1]
    part = own[0].shape[0] // slices
    position = place * rows + lax.broadcasted_iota(jnp.int32, (rows, 1), 0)
    valid = jnp.where(position < info[2], 1.0, 0.0)
    cot = got[0][...].astype(jnp.float32)
    for k in range(1, ranks):
        cot = cot + got[k][...].astype(jnp.float32)
    v = middle[...]
    scale = lax.rsqrt(jnp.mean(v * v, axis=-1, keepdims=True) + NORM_EPS)
    n = v * scale
    gain_grad[...] = jnp.sum(cot * n, axis=0, keepdims=True)
    scaled = cot * gain[...]
    back = scale * (scaled - n * jnp.mean(scaled * n, axis=-1, keepdims=True))
    back = back + cotangent[...].astype(jnp.float32) * valid
    middle_cot[...] = back
    middle_low[...] = bf16(back)
    for j in range(slices):
        even = middle_low[:, pl.ds(2 * j * part, part)]
        odd = middle_low[:, pl.ds((2 * j + 1) * part, part)]
        low_own[:, pl.ds(j * part, part)] = jnp.where(first, even, odd)
        low_other[:, pl.ds(j * part, part)] = jnp.where(first, odd, even)
    for k in range(ranks):
        cols = pl.ds(pl.multiple_of((place ^ k) * width, 128), width)
        attended_cot[:, cols] = bf16(
            dot_nn(low_own[...], own[k][...]) + dot_nn(low_other[...], other[k][...])
        )
    score_bias(info, rows, ranks, bias)
    for k in range(ranks):
        keys[pl.ds(k * rows, rows), :] = kv[k][:, pl.ds(0, KV_WIDTH)]
        values[pl.ds(k * rows, rows), :] = kv[k][:, pl.ds(KV_WIDTH, KV_WIDTH)]
    keys_t[...] = keys[...].T
    key_sum[...] = jnp.zeros_like(key_sum)
    value_sum[...] = jnp.zeros_like(value_sum)

    @pl.loop(0, HEADS, unroll=2)
    def _(h):
        cols = pl.ds(pl.multiple_of(h * HEAD, HEAD), HEAD)
        kv_cols = pl.ds(pl.multiple_of((h // GROUP) * HEAD, HEAD), HEAD)
        query = queries[:, cols]
        out_cot = attended_cot[:, cols]
        scores = dot_nt(keys[:, kv_cols], query) * SCALE + bias[...]
        probs = jnp.exp(scores - totals[pl.ds(h, 1), :])
        probs_cot = dot_nt(values[:, kv_cols], out_cot)
        row_dot = jnp.sum(probs * probs_cot, axis=0, keepdims=True)
        scores_cot = bf16(probs * (probs_cot - row_dot))
        value_sum[:, kv_cols] += dot_nn(bf16(probs), out_cot)
        key_sum[:, kv_cols] += dot_nn(scores_cot, query)
        query_cot[:, cols] = dot_nn(keys_t[kv_cols, :], scores_cot).T * SCALE

    for k in range(ranks):
        at = pl.ds(k * rows, rows)
        kv_cot[k][:, pl.ds(0, KV_WIDTH)] = bf16(key_sum[at, :] * SCALE)
        kv_cot[k][:, pl.ds(KV_WIDTH, KV_WIDTH)] = bf16(value_sum[at, :])


def outer_kernel(ranks, slices, *refs):
    info, left, right, own, other, turned = refs
    place = info[0]
    parity = info[1]
    width = own.shape[2]
    part = own.shape[1] // slices
    turned[...] = right[...].T
    for k in range(ranks):
        block = block_columns(left, place, k, width)
        for j in range(slices):
            at = pl.ds(j * part, part)
            mine = pl.ds(pl.multiple_of((2 * j + parity) * part, 16), part)
            theirs = pl.ds(pl.multiple_of((2 * j + 1 - parity) * part, 16), part)
            own[k, at, :] = bf16(dot_nn(turned[mine, :], block))
            other[k, at, :] = bf16(dot_nn(turned[theirs, :], block))


def project_back_kernel(ranks, *refs):
    info, query_cot, cosine, sine = refs[:4]
    got = refs[4 : 4 + ranks]
    projected_low, bias_grad = refs[4 + ranks :]
    kv_cot = got[0][...].astype(jnp.float32)
    for k in range(1, ranks):
        kv_cot = kv_cot + got[k][...].astype(jnp.float32)
    for h in range(HEADS + 2 * KV_HEADS):
        cols = pl.ds(h * HEAD, HEAD)
        if h < HEADS:
            u = query_cot[:, cols]
        else:
            u = kv_cot[:, (h - HEADS) * HEAD : (h - HEADS + 1) * HEAD]
        if h < HEADS + KV_HEADS:
            u = u * cosine[...] + pltpu.roll(u * sine[...], HEAD // 2, 1)
        bias_grad[:, cols] = jnp.sum(u, axis=0, keepdims=True)
        projected_low[:, cols] = bf16(u)


def input_back_kernel(ranks, slices, *refs):
    info, projected_low, tokens, gain, middle_cot = refs[:5]
    own = refs[5 : 5 + ranks]
    other = refs[5 + ranks : 5 + 2 * ranks]
    input_grad, gain_grad, low_own, low_other, normed_cot = refs[5 + 2 * ranks :]
    place = info[0]
    first = info[1] == 0
    width = own[0].shape[1]
    step = own[0].shape[0] // slices
    part = QKV // (2 * slices)
    for j in range(slices):
        even = projected_low[:, pl.ds(2 * j * part, part)]
        odd = projected_low[:, pl.ds((2 * j + 1) * part, part)]
        low_own[:, pl.ds(j * part, part)] = jnp.where(first, even, odd)
        low_other[:, pl.ds(j * part, part)] = jnp.where(first, odd, even)
    for k in range(ranks):
        cols = pl.ds(pl.multiple_of((place ^ k) * width, 128), width)
        normed_cot[:, cols] = sum(
            dot_nn(low[:, pl.ds(j * part, part)], mats[k][pl.ds(j * step, part), :])
            for low, mats in ((low_own, own), (low_other, other))
            for j in range(slices)
        )
    x = tokens[...].astype(jnp.float32)
    scale = lax.rsqrt(jnp.mean(x * x, axis=-1, keepdims=True) + NORM_EPS)
    n = x * scale
    cot = normed_cot[...]
    gain_grad[...] = jnp.sum(cot * n, axis=0, keepdims=True)
    scaled = cot * gain[...]
    back = scale * (scaled - n * jnp.mean(scaled * n, axis=-1, keepdims=True))
    input_grad[...] = bf16(middle_cot[...] + back)


def finish_kernel(info, *refs):
    *terms, grad, small, squares = refs
    total = terms[0][...].astype(jnp.float32)
    for term in terms[1:]:
        total = total + term[...].astype(jnp.float32)
    columns = grad.shape[1]
    grad[...] = total[:columns].T
    small[...] = total[columns : columns + 1]
    squares[...] = jnp.sum(total * total, keepdims=True)


def send_kernel(ranks, info, w_in, w_down, *refs):
    outs = refs[:ranks]
    (turned,) = refs[ranks:]
    place = info[0]
    rows = w_in.shape[1]
    part = w_in.shape[0] // ranks
    columns = w_down.shape[0]
    for p in range(ranks):
        turned[p, :, pl.ds(0, rows)] = bf16(w_in[pl.ds(p * part, part), :])
        for s in range(w_down.shape[1] // (ranks * part)):
            source = w_down[:, pl.ds((s * ranks + p) * part, part)]
            turned[p, :, pl.ds(rows + s * columns, columns)] = bf16(source.T)
    for k in range(ranks):
        outs[k][...] = turned[place ^ k]


def place_kernel(chunks, ranks, info, *refs):
    got = refs[:ranks]
    outs = refs[ranks : ranks + len(chunks)]
    stacked, *lows = refs[ranks + len(chunks) :]
    place = info[0]
    rows = D // ranks
    for k in range(ranks):
        stacked[k] = got[k][...]
    for chunk, out, low in zip(chunks, outs, lows):
        low[...] = jnp.zeros_like(low)
        if chunk.deep > chunk.real:
            out[...] = jnp.zeros_like(out)
    for a in range(ranks):
        start = 0
        for chunk, out, low in zip(chunks, outs, lows):
            each = chunk.slices // ranks
            piece = stacked[place ^ a, pl.ds(start, chunk.real), :]
            out[pl.ds(0, chunk.real), pl.ds(a * rows, rows)] = piece[:, :rows]
            for s in range(each):
                at = rows + s * chunk.columns
                turned = piece[:, at : at + chunk.columns].astype(jnp.float32).T
                for i in range(chunk.folds):
                    lane = i * chunk.wide + (a * each + s) * chunk.deep
                    low[:, pl.ds(lane, chunk.real)] = turned[i * chunk.low : (i + 1) * chunk.low]
            start += chunk.real
    for chunk, out, low in zip(chunks, outs, lows):
        out[pl.ds(chunk.deep, chunk.low), :] = bf16(low[...])


def pack_kernel(chunk, ranks, info, shard, *refs):
    outs = refs[:ranks]
    squares, turned = refs[ranks:]
    place = info[0]
    block = D // ranks
    each = chunk.slices // ranks
    rows = shard[pl.ds(0, chunk.real), :].astype(jnp.float32)
    total = jnp.sum(rows * rows, keepdims=True)
    low = shard[pl.ds(chunk.deep, chunk.low), :].astype(jnp.float32)
    for s in range(chunk.slices):
        for i in range(chunk.folds):
            start = i * chunk.wide + s * chunk.deep
            part = low[:, start : start + chunk.real]
            total = total + jnp.sum(part * part, keepdims=True)
            at = (s % each) * chunk.columns + i * chunk.low
            turned[s // each, :, pl.ds(at, chunk.low)] = part.T
    squares[...] = total
    for k in range(ranks):
        cols = pl.ds(pl.multiple_of((place ^ k) * block, 128), block)
        outs[k][:, pl.ds(0, block)] = shard[pl.ds(0, chunk.real), cols]
        outs[k][:, pl.ds(block, each * chunk.columns)] = bf16(turned[place ^ k])


def call(kernel, args, outs, scratch, micros):
    vmem = pl.BlockSpec(memory_space=pltpu.VMEM)
    moved = sum(math.prod(a.shape) * a.dtype.itemsize for a in args)
    moved += sum(math.prod(a.shape) * a.dtype.itemsize for a in outs)
    moved *= min(micros, 1)
    return pl.pallas_call(
        kernel,
        out_shape=tuple(outs),
        in_specs=[pl.BlockSpec(memory_space=pltpu.SMEM)] + [vmem] * (len(args) - 1),
        out_specs=(vmem,) * len(outs),
        scratch_shapes=scratch,
        compiler_params=pltpu.CompilerParams(vmem_limit_bytes=VMEM_LIMIT),
        cost_estimate=pl.CostEstimate(
            flops=micros * FLOPS_PER_MICRO, bytes_accessed=moved, transcendentals=0
        ),
    )(*args)


def f32_like(*shape):
    return jax.ShapeDtypeStruct(shape, jnp.float32)


def bf16_like(*shape):
    return jax.ShapeDtypeStruct(shape, jnp.bfloat16)


class Chunk:
    def __init__(self, size, lines):
        self.lines = lines
        self.slices = lines // 2
        self.real = size // self.slices
        self.deep = -(-self.real // 16) * 16
        self.units = self.slices * self.deep
        self.wide = -(-self.units // 128) * 128
        self.columns = D // lines
        self.folds = D // self.wide if self.columns * self.wide % (16 * D) == 0 else 1
        self.low = self.columns // self.folds
        self.step = self.deep + self.low
        self.rows = lines * self.step
        self.blocks = [
            (s, min(UNIT_TILE, self.units - s)) for s in range(0, self.units, UNIT_TILE)
        ]

    def in_parts(self, s, n, half):
        parts = []
        at = s
        while at < s + n:
            k = at // self.deep
            count = min(s + n, (k + 1) * self.deep) - at
            line = half * self.slices + k
            parts.append((at - s, count, line * self.step + at - k * self.deep))
            at += count
        return parts

    def down_parts(self, s, n):
        width = min(self.wide, s + UNIT_TILE) - s
        return [
            (
                line * self.columns + i * self.low,
                line * self.step + self.deep,
                i * self.wide + s,
                width,
            )
            for line in range(self.lines)
            for i in range(self.folds)
        ]


class Copies:
    def __init__(self, sems):
        self.sems = sems
        self.used = 0

    def start(self, source, target):
        copy = pltpu.make_async_copy(source, target, self.sems.at[self.used])
        self.used += 1
        copy.start()
        return copy


def wait_all(copies):
    for copy in copies:
        copy.wait()


def transpose_tokens(source, target, tokens):
    @pl.loop(0, tokens // TURN_TILE)
    def _(t):
        at = pl.multiple_of(t * TURN_TILE, TURN_TILE)
        target[:, pl.ds(at, TURN_TILE)] = source[pl.ds(at, TURN_TILE), :].T


def load_tokens(blocks, target, copies):
    rows = blocks[0].shape[0]
    return [
        copies.start(block, target.at[pl.ds(k * rows, rows)]) for k, block in enumerate(blocks)
    ]


def load_chunk(chunk, ranks, na_in, oc_in, weights, na, oc, w, d, copies):
    first = load_tokens(na_in, na, copies)
    block_copies = []
    for b, (s, n) in enumerate(chunk.blocks):
        mine = []
        for half in range(2):
            for offset, count, row in chunk.in_parts(s, n, half):
                target = w.at[pl.ds(half * chunk.units + s + offset, count)]
                mine.append(copies.start(weights.at[pl.ds(row, count)], target))
        if b == 0:
            first += load_tokens(oc_in, oc, copies)
        for column, row, at, width in chunk.down_parts(s, n):
            source = weights.at[pl.ds(row, chunk.low), pl.ds(at, width)]
            target = d.at[pl.ds(column, chunk.low), pl.ds(s, width)]
            mine.append(copies.start(source, target))
        block_copies.append(mine)
    return first, block_copies


def store_in(chunk, s, n, half, dw, at, weights_out, copies):
    return [
        copies.start(dw.at[pl.ds(at + offset, count)], weights_out.at[pl.ds(row, count)])
        for offset, count, row in chunk.in_parts(s, n, half)
    ]


def store_down(chunk, s, n, dd, at, weights_out, copies):
    return [
        copies.start(
            dd.at[pl.ds(column, chunk.low), pl.ds(at, width)],
            weights_out.at[pl.ds(row, chunk.low), pl.ds(place, width)],
        )
        for column, row, place, width in chunk.down_parts(s, n)
    ]


def copy_count(chunk):
    parts = sum(len(chunk.in_parts(s, n, 0)) for s, n in chunk.blocks)
    return 2 * parts + len(chunk.blocks) * chunk.lines * chunk.folds


def unit_block(units, s, n, tokens, na, oc, w, d, back, mixed, gt, ut, ht, at_row, add, final):
    wg = w.at[pl.ds(s, n)]
    wu = w.at[pl.ds(units + s, n)]
    db = d.at[:, pl.ds(s, n)]

    @pl.loop(0, tokens // TOKEN_TILE)
    def _(t):
        at = pl.ds(pl.multiple_of(t * TOKEN_TILE, TOKEN_TILE), TOKEN_TILE)
        gate = dot_nt(na[at, :], wg[...])
        up = dot_nt(na[at, :], wu[...])
        hidden_cot = dot_nn(oc[at, :], db[...])
        sigmoid = 1.0 / (1.0 + jnp.exp(-gate))
        activated = gate * sigmoid
        hidden = bf16(activated * up)
        gate_cot = bf16(hidden_cot * up * sigmoid * (1.0 + gate * (1.0 - sigmoid)))
        up_cot = bf16(hidden_cot * activated)
        ht[pl.ds(at_row, n), at] = hidden.T
        gt[pl.ds(at_row, n), at] = gate_cot.T
        ut[pl.ds(at_row, n), at] = up_cot.T
        back_term = dot_nn(gate_cot, wg[...]) + dot_nn(up_cot, wu[...])
        mixed_term = dot_nt(hidden, db[...])
        if add:
            back_term = back_term + back[at, :]
            mixed_term = mixed_term + mixed[at, :]
        if final:
            na[at, :] = bf16(back_term)
            oc[at, :] = bf16(mixed_term)
        else:
            back[at, :] = back_term
            mixed[at, :] = mixed_term


def gradient_block(n, na, oc_t, gt, ut, ht, at_row, dw, dw_gate, dw_up, dd, dd_at):
    at = pl.ds(at_row, n)

    @pl.loop(0, D // GRAD_TILE)
    def _(j):
        cols = pl.ds(pl.multiple_of(j * GRAD_TILE, GRAD_TILE), GRAD_TILE)
        dw[pl.ds(dw_gate, n), cols] = bf16(dot_nn(gt[at, :], na[:, cols]))
        dw[pl.ds(dw_up, n), cols] = bf16(dot_nn(ut[at, :], na[:, cols]))
        dd[cols, pl.ds(dd_at, n)] = bf16(dot_nt(oc_t[cols, :], ht[at, :]))


def first_chunk_kernel(chunk, ranks, carried, *refs):
    na_in = refs[:ranks]
    oc_in = refs[ranks : 2 * ranks]
    weights = refs[2 * ranks]
    refs = refs[2 * ranks + 1 :]
    if carried:
        back_in, mixed_in = refs[:2]
        refs = refs[2:]
    back_out, mixed_out, weights_out = refs[:3]
    na, oc, oc_t, w, d, dw, dd, back, mixed, gt, ut, ht, in_sem, out_sem = refs[3:]
    tokens = na.shape[0]
    copies = Copies(in_sem)
    first, block_copies = load_chunk(chunk, ranks, na_in, oc_in, weights, na, oc, w, d, copies)
    if carried:
        first.append(copies.start(back_in, back))
        first.append(copies.start(mixed_in, mixed))
    wait_all(first)
    transpose_tokens(oc, oc_t, tokens)
    copies = Copies(out_sem)
    outs = []
    stored = []
    for b, (s, n) in enumerate(chunk.blocks):
        wait_all(block_copies[b])
        add = carried or bool(b)
        unit_block(
            chunk.units, s, n, tokens, na, oc, w, d, back, mixed, gt, ut, ht, 0, add, False
        )
        if b == len(chunk.blocks) - 1:
            outs.append(copies.start(back, back_out))
            outs.append(copies.start(mixed, mixed_out))
        wait_all(stored)
        gradient_block(n, na, oc_t, gt, ut, ht, 0, dw, 0, UNIT_TILE, dd, 0)
        stored = store_in(chunk, s, n, 0, dw, 0, weights_out, copies)
        stored += store_in(chunk, s, n, 1, dw, UNIT_TILE, weights_out, copies)
        stored += store_down(chunk, s, n, dd, 0, weights_out, copies)
    wait_all(outs + stored)


def last_chunk_kernel(chunk, ranks, carried, start, *refs):
    na_in = refs[:ranks]
    oc_in = refs[ranks : 2 * ranks]
    weights = refs[2 * ranks]
    refs = refs[2 * ranks + 1 :]
    if carried:
        back_in, mixed_in = refs[:2]
        refs = refs[2:]
    back_out = refs[:ranks]
    mixed_out = refs[ranks : 2 * ranks]
    kept_out = refs[2 * ranks : 2 * ranks + 3]
    na, oc, w, d, back, mixed, gt, ut, ht, in_sem, out_sem = refs[2 * ranks + 3 :]
    tokens = na.shape[0]
    rows = tokens // ranks
    copies = Copies(in_sem)
    first, block_copies = load_chunk(chunk, ranks, na_in, oc_in, weights, na, oc, w, d, copies)
    if carried:
        at = pl.ds(start * rows, tokens)
        first.append(copies.start(back_in.at[at], back))
        first.append(copies.start(mixed_in.at[at], mixed))
    wait_all(first)
    copies = Copies(out_sem)
    outs = []
    for b, (s, n) in enumerate(chunk.blocks):
        wait_all(block_copies[b])
        unit_block(
            chunk.units,
            s,
            n,
            tokens,
            na,
            oc,
            w,
            d,
            back,
            mixed,
            gt,
            ut,
            ht,
            s,
            carried or bool(b),
            b == len(chunk.blocks) - 1,
        )
        for kept, target in zip((gt, ut, ht), kept_out):
            at = pl.ds(s, n)
            outs.append(copies.start(kept.at[at], target.at[at]))
    for k in range(ranks):
        at = pl.ds(k * rows, rows)
        outs.append(copies.start(na.at[at], back_out[k]))
        outs.append(copies.start(oc.at[at], mixed_out[k]))
    wait_all(outs)


def gradient_kernel(chunk, ranks, *refs):
    na_in = refs[:ranks]
    oc_in = refs[ranks : 2 * ranks]
    kept_in = refs[2 * ranks : 2 * ranks + 6]
    weights_out, na, oc, oc_t, gt, ut, ht, dw, dd, in_sem, out_sem = refs[2 * ranks + 6 :]
    tokens = na.shape[0]
    copies = Copies(in_sem)
    first = load_tokens(oc_in, oc, copies)
    later = load_tokens(na_in, na, copies)
    half = tokens // 2
    for i, source in enumerate(kept_in):
        kept = (gt, ut, ht)[i % 3].at[:, pl.ds(i // 3 * half, half)]
        later.append(copies.start(source, kept))
    wait_all(first)
    transpose_tokens(oc, oc_t, tokens)
    if chunk.wide > chunk.units:
        spare = chunk.wide - chunk.units
        dd[:, pl.ds(chunk.units, spare)] = jnp.zeros((D, spare), jnp.bfloat16)
    wait_all(later)
    copies = Copies(out_sem)
    outs = []
    for s, n in chunk.blocks:
        gradient_block(n, na, oc_t, gt, ut, ht, s, dw, s, chunk.units + s, dd, s)
        outs += store_in(chunk, s, n, 0, dw, s, weights_out, copies)
        outs += store_in(chunk, s, n, 1, dw, chunk.units + s, weights_out, copies)
        outs += store_down(chunk, s, n, dd, s, weights_out, copies)
    wait_all(outs)


def hbm_call(kernel, args, outs, scratch, micros):
    moved = sum(math.prod(a.shape) * a.dtype.itemsize for a in args)
    moved += sum(math.prod(a.shape) * a.dtype.itemsize for a in outs)
    anywhere = pl.BlockSpec(memory_space=pl.ANY)
    return pl.pallas_call(
        kernel,
        out_shape=tuple(outs),
        in_specs=[anywhere] * len(args),
        out_specs=(anywhere,) * len(outs),
        scratch_shapes=scratch,
        compiler_params=pltpu.CompilerParams(vmem_limit_bytes=VMEM_LIMIT),
        cost_estimate=pl.CostEstimate(
            flops=micros * FLOPS_PER_MICRO, bytes_accessed=moved, transcendentals=0
        ),
    )(*args)


def vmem_bf16(*shape):
    return pltpu.VMEM(shape, jnp.bfloat16)


def vmem_f32(*shape):
    return pltpu.VMEM(shape, jnp.float32)


def first_chunk(chunk, na, oc, weights, carry):
    ranks = len(na)
    tokens = ranks * na[0].shape[0]
    scratch = [
        vmem_bf16(tokens, D),
        vmem_bf16(tokens, D),
        vmem_bf16(D, tokens),
        vmem_bf16(2 * chunk.units, D),
        vmem_bf16(D, chunk.wide),
        vmem_bf16(2 * UNIT_TILE, D),
        vmem_bf16(D, UNIT_TILE),
        vmem_f32(tokens, D),
        vmem_f32(tokens, D),
        vmem_bf16(UNIT_TILE, tokens),
        vmem_bf16(UNIT_TILE, tokens),
        vmem_bf16(UNIT_TILE, tokens),
        pltpu.SemaphoreType.DMA((2 * ranks + 2 + copy_count(chunk),)),
        pltpu.SemaphoreType.DMA((2 + copy_count(chunk),)),
    ]
    outs = [f32_like(tokens, D), f32_like(tokens, D), bf16_like(chunk.rows, D)]
    kernel = functools.partial(first_chunk_kernel, chunk, ranks, bool(carry))
    return hbm_call(kernel, [*na, *oc, weights, *carry], outs, scratch, 68)


def last_chunk(chunk, na, oc, weights, carry, start):
    ranks = len(na)
    rows = na[0].shape[0]
    tokens = ranks * rows
    scratch = [
        vmem_bf16(tokens, D),
        vmem_bf16(tokens, D),
        vmem_bf16(2 * chunk.units, D),
        vmem_bf16(D, chunk.wide),
        vmem_f32(tokens, D),
        vmem_f32(tokens, D),
        vmem_bf16(chunk.units, tokens),
        vmem_bf16(chunk.units, tokens),
        vmem_bf16(chunk.units, tokens),
        pltpu.SemaphoreType.DMA((2 * ranks + 2 + copy_count(chunk),)),
        pltpu.SemaphoreType.DMA((2 * ranks + 3 * len(chunk.blocks),)),
    ]
    outs = [bf16_like(rows, D)] * (2 * ranks) + [bf16_like(chunk.units, tokens)] * 3
    kernel = functools.partial(last_chunk_kernel, chunk, ranks, bool(carry), start)
    got = hbm_call(
        kernel, [*na, *oc, weights, *carry], outs, scratch, 20
    )
    return got[:ranks], got[ranks : 2 * ranks], got[2 * ranks :]


def chunk_gradients(chunk, na, oc, kept):
    ranks = len(na)
    tokens = ranks * na[0].shape[0]
    scratch = [
        vmem_bf16(tokens, D),
        vmem_bf16(tokens, D),
        vmem_bf16(D, tokens),
        vmem_bf16(chunk.units, tokens),
        vmem_bf16(chunk.units, tokens),
        vmem_bf16(chunk.units, tokens),
        vmem_bf16(2 * chunk.units, D),
        vmem_bf16(D, chunk.wide),
        pltpu.SemaphoreType.DMA((2 * ranks + 6,)),
        pltpu.SemaphoreType.DMA((copy_count(chunk),)),
    ]
    kernel = functools.partial(gradient_kernel, chunk, ranks)
    (terms,) = hbm_call(
        kernel,
        [*na, *oc, *kept],
        [bf16_like(chunk.rows, D)],
        scratch,
        16,
    )
    return terms


def sharded_pass(tokens, cotangent, lengths, half_qkv, half_out, half_in, half_down, half_small):
    ranks = lax.axis_size("dp")
    lines = lax.axis_size("fsdp")
    place = lax.axis_index("dp")
    rows = tokens.shape[1]
    slices = lines // 2
    block = D // ranks
    inputs = tokens[0]
    info = jnp.stack([place, lax.rem(lax.axis_index("fsdp"), 2), lengths[0]])

    small_rows, small_columns = half_small.shape
    columns = half_qkv.shape[1]
    line = jnp.concatenate([half_qkv.T, half_out.T])
    line = scoped("matrix_line", line_gather, line)
    qkv_along = line[:, :columns].reshape(-1, block)
    out_along = line[:, columns:].reshape(-1, block)
    half_small, qkv_along = lax.optimization_barrier((half_small, qkv_along))
    small_line = scoped("small_gather", line_gather, half_small)
    small_other = scoped("small_gather", core_swap, small_line)
    small_line = jnp.stack(
        [
            jnp.where(is_even(), small_line, small_other),
            jnp.where(is_even(), small_other, small_line),
        ],
        axis=1,
    )
    small_line = small_line.reshape(lines, small_rows, small_columns)
    small_stack = jnp.stack(
        [small_line]
        + [scoped("small_gather", dp_send, small_line, k) for k in range(1, ranks)]
    )
    small_vec = jnp.stack(
        [
            lax.dynamic_index_in_dim(small_stack, place ^ a, 0, keepdims=False)
            for a in range(ranks)
        ]
    )
    small_vec = small_vec.transpose(0, 2, 1, 3).reshape(-1).astype(jnp.float32)
    gain_attn, gain_mlp, biases = unpack_small(small_vec)
    gain_attn = gain_attn[None]
    gain_mlp = gain_mlp[None]

    part = half_in.shape[1] // ranks
    width = block + D // ranks // 2
    sent = call(
        functools.partial(send_kernel, ranks),
        [info, half_in.T, half_down.T],
        [bf16_like(part, width)] * ranks,
        [vmem_bf16(ranks, part, width)],
        1,
    )
    got = [sent[0]] + [
        scoped("weights_exchange", dp_send, sent[k], k) for k in range(1, ranks)
    ]
    got, out_along, qkv_along = lax.optimization_barrier((got, out_along, qkv_along))
    qkv_own = scoped("qkv_gather", dp_gather, qkv_along)
    qkv_other = [scoped("qkv_swap", core_swap, block) for block in qkv_own]
    out_along, qkv_other = lax.optimization_barrier((out_along, qkv_other))
    out_near = scoped("out_gather", gather_near, out_along)

    chunks = [Chunk(size, lines) for size in CHUNKS]
    packed = call(
        functools.partial(place_kernel, chunks, ranks),
        [info, *got],
        [bf16_like(chunk.step, D) for chunk in chunks],
        [vmem_bf16(ranks, part, width)] + [vmem_f32(chunk.low, D) for chunk in chunks],
        1,
    )
    gathered = [lax.all_gather(array, "fsdp", axis=0, tiled=True) for array in packed]

    query_places = place * rows + jnp.arange(rows, dtype=jnp.int32)
    cosine, sine = rope_tables(query_places.astype(jnp.float32))
    sine = jnp.where(jnp.arange(HEAD) < HEAD // 2, -sine, sine)
    normed, queries, kv = call(
        functools.partial(project_kernel, ranks, slices),
        [info, inputs, gain_attn, biases[None], cosine, sine, *qkv_own, *qkv_other],
        [bf16_like(rows, D), bf16_like(rows, D), bf16_like(rows, 2 * KV_WIDTH)],
        [vmem_f32(rows, QKV)],
        7,
    )
    kv_near = scoped("kv_gather", gather_near, kv)
    kv, out_near = lax.optimization_barrier((kv, out_near))
    kv_near, out_near = lax.optimization_barrier((kv_near, out_near))
    out_own = scoped("out_gather", gather_far, out_near)
    kv_blocks = scoped("kv_gather", gather_far, kv_near)
    out_other = scoped("out_swap", core_swap, jnp.stack(out_own))

    valid = query_places < lengths[0]
    out_cot = jnp.where(valid[:, None], cotangent[0], jnp.zeros_like(cotangent[0]))
    out_cot, *kv_blocks = lax.optimization_barrier((out_cot, *kv_blocks))
    cot_blocks = scoped("cot_gather", dp_gather, out_cot)

    attended, totals, middle, normed_again = call(
        functools.partial(attend_kernel, ranks, slices),
        [info, inputs, gain_mlp, queries, *kv_blocks, *out_own, out_other],
        [bf16_like(rows, D), f32_like(16, rows), f32_like(rows, D), bf16_like(rows, D)],
        [
            vmem_f32(ranks * rows, rows),
            vmem_bf16(ranks * rows, KV_WIDTH),
            vmem_bf16(ranks * rows, KV_WIDTH),
            vmem_bf16(KV_WIDTH, ranks * rows),
        ],
        24,
    )
    normed_blocks = scoped("normed_gather", dp_gather, normed_again)

    *before, end = zip(chunks, gathered)
    carry = ()
    terms = []
    for chunk, weights in before:
        back, mixed, term = first_chunk(chunk, normed_blocks, cot_blocks, weights, carry)
        carry = (back, mixed)
        terms.append(term)
    chunk, weights = end
    half = ranks // 2
    far_back, far_mixed, far_kept = last_chunk(
        chunk, normed_blocks[half:], cot_blocks[half:], weights, carry, half
    )
    far_got = [scoped("back_reduce", dp_send, far_back[k - half], k) for k in range(half, ranks)]
    near_cot, far_back = lax.optimization_barrier((cot_blocks[:half], far_back))
    near_back, near_mixed, near_kept = last_chunk(
        chunk, normed_blocks[:half], near_cot, weights, carry, 0
    )
    back_got = [scoped("back_reduce", dp_send, near_back[k], k) for k in range(1, half)] + far_got
    back_blocks = near_back
    mixed_blocks = [*near_mixed, *far_mixed]
    kept = [*near_kept, *far_kept]
    term = chunk_gradients(chunk, normed_blocks, cot_blocks, kept)
    term, back_blocks, back_got, mixed_blocks = lax.optimization_barrier(
        (term, back_blocks, back_got, mixed_blocks)
    )
    terms.append(term)
    first_shard = lax.psum_scatter(terms[0], "fsdp", scatter_dimension=0, tiled=True)

    def pack_chunk(chunk, shard):
        width = block + D // ranks // 2
        *sent, squares = call(
            functools.partial(pack_kernel, chunk, ranks),
            [info, shard],
            [bf16_like(chunk.real, width)] * ranks + [f32_like(1, 1)],
            [vmem_f32(ranks, chunk.real, width - block)],
            0,
        )
        return sent, squares[0, 0]

    def exchange_chunk(sent):
        got = sent[:1] + [scoped("gradient_exchange", dp_send, sent[k], k) for k in range(1, ranks)]
        return got

    def place_chunk(got):
        stacked = jnp.stack(got)
        ordered = jnp.stack(
            [
                lax.dynamic_index_in_dim(stacked, place ^ a, 0, keepdims=False)
                for a in range(ranks)
            ]
        )
        return unpack_gradients(ordered, half_in.shape[0], half_down.shape[1])

    mixed_got = [scoped("mixed_reduce", dp_send, mixed_blocks[k], k) for k in range(1, ranks - 1)]
    middle_cot, middle_low, gain_mlp_grad, query_cot, *kv_cot = call(
        functools.partial(attend_back_kernel, ranks, slices),
        [
            info,
            middle,
            out_cot,
            gain_mlp,
            queries,
            totals,
            back_blocks[0],
            *back_got,
            *kv_blocks,
            *out_own,
            out_other,
        ],
        [f32_like(rows, D), bf16_like(rows, D), f32_like(1, D), f32_like(rows, D)]
        + [bf16_like(rows, 2 * KV_WIDTH)] * ranks,
        [
            vmem_f32(ranks * rows, rows),
            vmem_bf16(ranks * rows, KV_WIDTH),
            vmem_bf16(ranks * rows, KV_WIDTH),
            vmem_bf16(KV_WIDTH, ranks * rows),
            vmem_bf16(rows, D),
            vmem_f32(ranks * rows, KV_WIDTH),
            vmem_f32(ranks * rows, KV_WIDTH),
            vmem_bf16(rows, D // 2),
            vmem_bf16(rows, D // 2),
        ],
        31,
    )

    def outer(left, right):
        columns = right.shape[1]
        return call(
            functools.partial(outer_kernel, ranks, slices),
            [info, left, right],
            [bf16_like(ranks, columns // 2, block)] * 2,
            [vmem_bf16(columns, rows)],
            0,
        )

    kv_cot, middle_low, mixed_got = lax.optimization_barrier((kv_cot, middle_low, mixed_got))
    kv_got = [scoped("kv_reduce", dp_send, kv_cot[k], k) for k in range(1, ranks)]
    out_own_term, out_other_term = outer(attended, middle_low)


    kv_got, out_own_term, out_other_term = lax.optimization_barrier(
        (kv_got, out_own_term, out_other_term)
    )
    out_swapped = scoped("out_core", core_swap, out_other_term)
    projected_low, bias_grad = call(
        functools.partial(project_back_kernel, ranks),
        [info, query_cot, cosine, sine, kv_cot[0], *kv_got],
        [bf16_like(rows, QKV), f32_like(1, QKV)],
        [],
        0,
    )
    out_sums = sum_blocks(out_own_term, out_swapped)
    out_sums = [out_sums[0]] + [bf16(total) for total in out_sums[1:]]
    projected_low, out_sums = lax.optimization_barrier((projected_low, out_sums))
    out_got = scoped("out_dp", reduce_over_dp, out_sums)
    qkv_own_term, qkv_other_term = outer(normed, projected_low)

    qkv_own_term, qkv_other_term, projected_low = lax.optimization_barrier(
        (qkv_own_term, qkv_other_term, projected_low)
    )
    qkv_swapped = scoped("qkv_core", core_swap, qkv_other_term)
    input_grad, gain_attn_grad = call(
        functools.partial(input_back_kernel, ranks, slices),
        [info, projected_low, inputs, gain_attn, middle_cot, *qkv_own, *qkv_other],
        [bf16_like(rows, D), f32_like(1, D)],
        [vmem_bf16(rows, QKV // 2), vmem_bf16(rows, QKV // 2), vmem_f32(rows, D)],
        0,
    )

    gain_attn_grad, first_shard, last_term, out_got[1:3] = lax.optimization_barrier(
        (gain_attn_grad, first_shard, terms[1], out_got[1:3])
    )
    last_shard = lax.psum_scatter(last_term, "fsdp", scatter_dimension=0, tiled=True)
    small_term = group_small(gain_attn_grad[0], gain_mlp_grad[0], bias_grad[0])
    small_term = small_term.reshape(ranks, small_rows, slices, 2, small_columns)
    small_term = small_term.transpose(3, 0, 2, 1, 4).reshape(2, ranks, slices, -1)
    small_parity = lax.rem(lax.axis_index("fsdp"), 2)
    small_own = lax.dynamic_index_in_dim(small_term, small_parity, 0, keepdims=False)
    small_other = lax.dynamic_index_in_dim(small_term, 1 - small_parity, 0, keepdims=False)
    small_sums = small_own + scoped("small_core", core_swap, small_other)

    qkv_swapped, out_got, small_sums, first_shard = lax.optimization_barrier(
        (qkv_swapped, out_got, small_sums, first_shard)
    )
    small_rest = ((0, 0), (0, 15), (0, block - small_sums.shape[2]))
    qkv_sums = []
    for k, total in enumerate(sum_blocks(qkv_own_term, qkv_swapped)):
        extra = jnp.pad(dp_own(small_sums, k)[:, None], small_rest)
        total = jnp.concatenate([total.reshape(slices, -1, block), extra], axis=1)
        qkv_sums.append(total.reshape(-1, block))
    qkv_got = scoped("qkv_dp", reduce_over_dp, qkv_sums)
    out_shard = scoped("out_line", reduce_over_line, out_got)
    first_sent, squares = pack_chunk(chunks[0], first_shard)

    qkv_got, out_shard, squares, first_sent = lax.optimization_barrier(
        (qkv_got, out_shard, squares, first_sent)
    )
    qkv_shard = scoped("qkv_line", reduce_over_line, qkv_got)
    out_grad = total_shard(out_shard)
    squares = squares + sum_of_squares(out_grad)
    first_got = exchange_chunk(first_sent)
    mixed_last, first_got = lax.optimization_barrier((mixed_blocks[-1], first_got))
    mixed_got.append(scoped("mixed_reduce", dp_send, mixed_last, ranks - 1))

    qkv_shard, squares, last_shard, first_got = lax.optimization_barrier(
        (qkv_shard, squares, last_shard, first_got)
    )
    last_sent, last_squares = pack_chunk(chunks[1], last_shard)
    last_got = exchange_chunk(last_sent)
    qkv_grad, small_row, qkv_squares = call(
        finish_kernel,
        [info, *qkv_shard],
        [f32_like(block, columns), f32_like(1, block), f32_like(1, 1)],
        [],
        0,
    )
    squares = squares + last_squares + qkv_squares[0, 0]
    squares, last_got[1], mixed_got = lax.optimization_barrier((squares, last_got[1], mixed_got))
    total_squares = scoped("norm_sum", sum_everywhere, squares)
    small_grad = small_row[0, : small_rows * small_columns]
    small_grad = small_grad.reshape(small_rows, small_columns)
    in_first, down_first = place_chunk(first_got)
    in_last, down_last = place_chunk(last_got)
    in_grad = jnp.concatenate([in_first, in_last], axis=1)
    in_grad = in_grad.transpose(2, 0, 1).reshape(half_in.shape)
    down_grad = jnp.concatenate([down_first, down_last], axis=1)
    down_grad = down_grad.transpose(2, 0, 1, 3).reshape(half_down.shape)
    in_grad, down_grad = lax.optimization_barrier((in_grad, down_grad))
    in_grad = in_grad.astype(jnp.float32)
    down_grad = down_grad.astype(jnp.float32)
    mixed = middle + mixed_blocks[0].astype(jnp.float32)
    for got in mixed_got:
        mixed = mixed + got.astype(jnp.float32)
    mixed = bf16(mixed)
    return (mixed, input_grad, total_squares, qkv_grad, out_grad, in_grad, down_grad, small_grad)


def per_device(
    tokens,
    cotangent,
    lengths,
    qkv_weight,
    qkv_first,
    qkv_second,
    out_weight,
    out_first,
    out_second,
    mlp_in_weight,
    mlp_in_first,
    mlp_in_second,
    down_weight,
    down_first,
    down_second,
    small_params,
    small_first,
    small_second,
):
    results = sharded_pass(
        tokens,
        cotangent,
        lengths,
        bf16(qkv_weight),
        bf16(out_weight),
        mlp_in_weight,
        down_weight,
        bf16(small_params),
    )
    mixed, input_cot, total_squares, qkv_grad, out_grad, in_grad, down_grad, small_grad = results
    grad_norm = jnp.sqrt(total_squares)
    clip_factor = CLIP_NORM / jnp.maximum(grad_norm, CLIP_NORM)
    outs = [mixed[None], input_cot[None], grad_norm]
    for weight, first, second, gradient, rate, decay in (
        (qkv_weight, qkv_first, qkv_second, qkv_grad, MATRIX_RATE, MATRIX_DECAY),
        (out_weight, out_first, out_second, out_grad, MATRIX_RATE, MATRIX_DECAY),
        (mlp_in_weight, mlp_in_first, mlp_in_second, in_grad, MATRIX_RATE, MATRIX_DECAY),
        (down_weight, down_first, down_second, down_grad, MATRIX_RATE, MATRIX_DECAY),
        (small_params, small_first, small_second, small_grad, SMALL_RATE, 0.0),
    ):
        outs.extend(update(weight, first, second, gradient, clip_factor, rate, decay))
    return tuple(outs)


def solution(mesh):
    rows = P("fsdp", "dp", None)
    shard = P("dp", "fsdp")
    return jax.shard_map(
        per_device,
        mesh=mesh,
        in_specs=(rows, rows, P("fsdp")) + (shard,) * 15,
        out_specs=(rows, rows, P()) + (shard,) * 20,
        check_vma=False,
    )
```
